32 devices in a mesh: rows: 8 (over z, x), cols: 4 (over y, core).
Axes of the slice: x: 2, y: 2, z: 4, core: 2. Of those that a mesh axis runs over, the one named last changes fastest.
Arguments:
- tokens: bfloat16 [2048, 4096], P('rows', 'cols'), may hold values from -6 to 6
- cotangent: bfloat16 [2048, 4096], P('rows', 'cols'), may hold values from -6 to 6
- gate_weight: bfloat16 [4096, 7168], P('rows', 'cols'), may hold values from -0.09375 to 0.09375
- down_weight: bfloat16 [4096, 7168], P('rows', 'cols'), may hold values from -0.0625 to 0.0625
- proj_in: bfloat16 [4096, 128], replicated, may hold values from -0.09375 to 0.09375
- proj_out: bfloat16 [7168, 64], P('cols'), may hold values from -0.0625 to 0.0625
- lengths: int32 [32], P('rows'), may hold values from 16 to 64
- loss_mask: int32 [32, 64], P('rows'), may hold values 0 or 1
- gram_in: float32 [8, 1024, 8, 1024], P(None, 'rows', None, 'cols'), as said below
- queries: float32 [256, 8, 1024], P('cols', None, 'rows'), may hold values from -6 to 6
Outputs:
- gram_next: float32 [8, 1024, 8, 1024], P(None, 'rows', None, 'cols')
- query_next: float32 [256, 8, 1024], P('cols', None, 'rows')
- scores: float32 [256, 32], P('cols', 'rows')
The draws below stay inside these ranges and needn't reach their ends.
Inputs may be any that keep to these rules, and one draw needn't show every extreme that they name: gram_in, read as a 8192 x 8192 matrix, is symmetric positive definite.
All inputs are finite; a program needn't handle non-finite values. No bound on the sum of `loss_mask` on one device may be relied on, other than what follows from the above.
Results may differ from the reference program's by a relative error of at most 0.004.
Values may be sent and summed in bfloat16 or wider, within the bound.
No kernel may reach another device: no remote copies, remote signals or barrier semaphores. Data moves between devices by JAX's collectives and lax.ppermute only.
A program may use at most 128 MiB of HBM per device.

```python
import math
import jax
import jax.numpy as jnp
from jax import lax

D = 4096
FF_WIN = 7168
K_IN = 128
K_OUT = 64
WIN = 64
PW = 1024
QN = 256
SEQS = 32
TOKENS = 2048
FEAT = 8192
CYC = 8


def draw_gram_in(key, part):
    key_noise, key_diag = jax.random.split(key, 2)
    noise_raw = jax.random.normal(key_noise, (FEAT, FEAT), jnp.float32)
    matrix = (noise_raw + noise_raw.T) * (0.6 / math.sqrt(FEAT))
    diagonal = jnp.exp(jax.random.uniform(key_diag, (FEAT,), jnp.float32, math.log(2.5), math.log(10.0)))
    matrix = matrix + jnp.diag(diagonal)
    return matrix.reshape(CYC, PW, CYC, PW)


def set_ends(values, stream_key, least, largest):
    longest = values.shape.index(max(values.shape))
    spots = []
    for shift in (0, 1):
        where = [jax.random.randint(jax.random.fold_in(stream_key, axis), (), 0, length) for axis, length in enumerate(values.shape)]
        where[longest] = (where[longest] + shift) % values.shape[longest]
        spots.append(tuple(where))
    return values.at[spots[0]].set(least).at[spots[1]].set(largest)


def levels(own_key, dims, cuts, least, largest):
    def one(axis_at, blocks):
        steps = jax.random.uniform(jax.random.fold_in(jax.random.fold_in(own_key, 6), axis_at), (blocks,), jnp.float32, least / len(cuts), largest / len(cuts))
        return jnp.repeat(jnp.exp(steps), dims[axis_at] // blocks).reshape((-1,) + (1,) * (len(dims) - axis_at - 1))

    factor_of = one(*cuts[0])
    for cut in cuts[1:]:
        factor_of = factor_of * one(*cut)
    return factor_of


def noise(rng, dims, scale, limit, cuts=(), kind=jnp.bfloat16):
    values = jax.random.normal(rng, dims, jnp.float32) * scale
    if len(cuts) > 0:
        values = levels(rng, dims, cuts, -0.22, 0.18) * values
    return jnp.clip(values, min=-limit, max=limit).astype(kind)


def setup_inputs(seed: int = 0) -> dict:
    keys = jax.random.split(jax.random.key(seed), 11)
    return {
        "tokens": noise(keys[0], (TOKENS, D), 1.0, 6.0, ((0, 8), (1, 4))),
        "cotangent": noise(keys[1], (TOKENS, D), 1.0, 6.0, ((0, 8), (1, 4))),
        "gate_weight": noise(keys[2], (D, FF_WIN), D ** -0.5, 0.09375, ((0, 8), (1, 4))),
        "down_weight": noise(keys[3], (D, FF_WIN), FF_WIN ** -0.5, 0.0625, ((0, 8), (1, 4))),
        "proj_in": noise(keys[4], (D, K_IN), D ** -0.5, 0.09375),
        "proj_out": noise(keys[5], (FF_WIN, K_OUT), FF_WIN ** -0.5, 0.0625, ((0, 4),)),
        "lengths": set_ends(jax.random.randint(keys[6], (SEQS,), WIN // 4, WIN + 1), jax.random.fold_in(keys[6], 1), WIN // 4, WIN).astype(jnp.int32),
        "loss_mask": set_ends((jax.random.randint(keys[7], (SEQS, WIN), 0, 4) < 3).astype(jnp.int32), jax.random.fold_in(keys[7], 1), 0, 1),
        "gram_in": draw_gram_in(jax.random.fold_in(keys[10], 71), 0),
        "queries": noise(keys[9], (QN, CYC, PW), 1.0, 6.0, ((0, 4), (2, 8)), jnp.float32),
    }


highest = lax.Precision.HIGHEST

def reference(tokens, cotangent, gate_weight, down_weight, proj_in, proj_out, lengths, loss_mask, gram_in, queries):
    gate_pre = jnp.dot(tokens.astype(jnp.float32), gate_weight.astype(jnp.float32), preferred_element_type=jnp.float32)
    grad_hidden = jnp.dot(cotangent.astype(jnp.float32), down_weight.astype(jnp.float32), preferred_element_type=jnp.float32)
    grad_up = (grad_hidden * jax.nn.silu(gate_pre)).astype(jnp.bfloat16)
    proj_inner = jnp.dot(tokens.astype(jnp.float32), proj_in.astype(jnp.float32), preferred_element_type=jnp.float32)
    proj_outer = jnp.dot(grad_up.astype(jnp.float32), proj_out.astype(jnp.float32), preferred_element_type=jnp.float32)
    positions = jnp.arange(WIN, dtype=jnp.int32)
    token_live = (positions[None, :] >= (WIN - lengths)[:, None]).astype(jnp.float32) * loss_mask.astype(jnp.float32)
    weighted = proj_inner.reshape(SEQS, WIN, K_IN) * token_live[:, :, None]
    features = jnp.einsum('stk,stl->skl', weighted, proj_outer.reshape(SEQS, WIN, K_OUT), precision=highest)
    features = features.reshape(SEQS, FEAT)
    updated = gram_in.reshape(FEAT, FEAT) + jnp.dot(features.T.astype(jnp.float32), features.astype(jnp.float32), precision=highest, preferred_element_type=jnp.float32) / SEQS
    factor = jnp.linalg.cholesky(updated[:PW, :PW])
    lower_part = jax.scipy.linalg.solve_triangular(factor, updated[PW:, :PW].T, lower=True).T
    panel_cols = jnp.concatenate([factor, lower_part], axis=0)
    gram_next = updated.at[:, :PW].set(panel_cols).reshape(CYC, PW, CYC, PW)
    query_flat = queries.reshape(QN, FEAT)
    solved = jax.scipy.linalg.solve_triangular(factor, query_flat[:, :PW].T, lower=True)
    query_tail = query_flat[:, PW:] - jnp.dot(solved.T.astype(jnp.float32), lower_part.T.astype(jnp.float32), precision=highest, preferred_element_type=jnp.float32)
    query_next = jnp.concatenate([solved.T, query_tail], axis=1).reshape(QN, CYC, PW)
    whitened = jax.scipy.linalg.solve_triangular(factor, features[:, :PW].T, lower=True)
    scores = jnp.dot(solved.T.astype(jnp.float32), whitened.astype(jnp.float32), precision=highest, preferred_element_type=jnp.float32)
    return (gram_next, query_next, scores)
```

```python
import functools
import jax
import jax.numpy as jnp
from jax import lax
from jax.experimental import pallas as pl
from jax.experimental.pallas import tpu as pltpu
from jax.sharding import PartitionSpec as P

highest = lax.Precision.HIGHEST


def eliminate(rows, size):
    shape = (8, size)
    sub = lax.broadcasted_iota(jnp.int32, shape, 0)
    lane = lax.broadcasted_iota(jnp.int32, shape, 1)
    count = size // 8

    def row_of(x, k):
        return jnp.broadcast_to(x[k : k + 1, :], shape)

    for p in range(count):
        base = 8 * p
        inside = (lane >= base) & (lane < base + 8)

        def columns(q):
            return [jnp.broadcast_to(rows[q][:, base + k : base + k + 1], shape) for k in range(8)]

        cols = columns(p)
        own = jnp.where(inside, jnp.where(lane - base == sub, 1.0, 0.0), rows[p])
        scaled_cols, scaled_rows, scale = [], [], jnp.zeros(shape, jnp.float32)
        for k in range(8):
            pivot = row_of(cols[k], k)
            inverse = 1.0 / pivot
            scale = jnp.where(sub == k, lax.rsqrt(pivot), scale)
            heads = [row_of(cols[j], k) * inverse for j in range(k + 1, 8)]
            head_row = row_of(own, k) * inverse
            scaled_cols.append(heads)
            scaled_rows.append(head_row)
            below = jnp.where(sub > k, cols[k], 0.0)
            for j in range(k + 1, 8):
                cols[j] = cols[j] - below * heads[j - k - 1]
            own = own - below * head_row
        for q in range(p + 1, count):
            other = columns(q)
            value = jnp.where(inside, 0.0, rows[q])
            for k in range(8):
                for j in range(k + 1, 8):
                    other[j] = other[j] - other[k] * scaled_cols[k][j - k - 1]
                value = value - other[k] * scaled_rows[k]
            rows[q] = value
        rows[p] = jnp.where(lane < base + 8, own * scale, 0.0)
    return rows


def mm(a, b):
    return jnp.dot(a, b, precision=highest, preferred_element_type=jnp.float32)


def mm_t(a, b):
    return lax.dot_general(
        a, b, (((1,), (1,)), ((), ())), precision=highest, preferred_element_type=jnp.float32
    )


def panel_kernel(block, share, diag_ref, below_ref, head_ref, left_ref, right_ref, out_ref, inv_ref, upper_ref):
    width = diag_ref.shape[0]
    low = below_ref.shape[0]
    total = out_ref.shape[0]
    for start in range(0, width, block):
        rows = slice(start, start + block)
        out_ref[rows, :] = (
            diag_ref[rows, :]
            + jnp.dot(left_ref[rows, :], right_ref[...], preferred_element_type=jnp.float32) * share
        )
    step = block if low % block == 0 else low
    for start in range(0, low, step):
        rows = slice(start, start + step)
        left = slice(width + start, width + start + step)
        out_ref[left, :] = (
            below_ref[rows, :]
            + jnp.dot(left_ref[left, :], right_ref[...], preferred_element_type=jnp.float32) * share
        )
    out_ref[width + low :, :] = head_ref[...]
    blocks = width // block

    def one(b, carry):
        off = pl.multiple_of(b * block, block)
        rows = [
            out_ref[pl.ds(pl.multiple_of(off + 8 * q, 8), 8), pl.ds(off, block)]
            for q in range(block // 8)
        ]
        rows = eliminate(rows, block)
        for q in range(block // 8):
            inv_ref[8 * q : 8 * q + 8, :] = rows[q]
        for s in range(blocks):

            @pl.when(b == s)
            def _():
                here = slice(s * block, (s + 1) * block)
                inv = inv_ref[...]
                if s + 1 < blocks:
                    upper_ref[:, (s + 1) * block :] = mm(inv, out_ref[here, (s + 1) * block :])
                chunk = 2 * block
                for start in range(s * block, total, chunk):
                    these = slice(start, min(start + chunk, total))
                    out_ref[these, here] = mm_t(out_ref[these, here], inv)
                for start in range((s + 1) * block, total, chunk):
                    if s + 1 < blocks:
                        these = slice(start, min(start + chunk, total))
                        out_ref[these, (s + 1) * block :] = out_ref[these, (s + 1) * block :] - mm(
                            out_ref[these, here], upper_ref[:, (s + 1) * block :]
                        )

        return carry

    lax.fori_loop(0, blocks, one, 0)


def panel(diag, below, heads, left, right, share):
    block = 128
    width, low, extra = diag.shape[0], below.shape[0], heads.shape[0]
    return pl.pallas_call(
        functools.partial(panel_kernel, block, share),
        out_shape=jax.ShapeDtypeStruct((width + low + extra, width), jnp.float32),
        in_specs=[pl.BlockSpec(memory_space=pltpu.VMEM)] * 5,
        out_specs=pl.BlockSpec(memory_space=pltpu.VMEM),
        scratch_shapes=[pltpu.VMEM((block, block), jnp.float32), pltpu.VMEM((block, width), jnp.float32)],
        compiler_params=pltpu.CompilerParams(vmem_limit_bytes=48 * 1024 * 1024),
        name="panel_factor",
    )(diag, below, heads, left, right)


def pack(x, left):
    high = lax.reduce_precision(x, 8, 7)
    rest = x - high
    mid = lax.reduce_precision(rest, 8, 7)
    low = rest - mid
    high, mid, low = (v.astype(jnp.bfloat16) for v in (high, mid, low))
    parts = (high, high, mid, high, low, mid) if left else (high, mid, high, low, high, mid)
    return jnp.concatenate(parts, axis=-1 if left else -2)


def gram_kernel(cycles, share, gram_ref, left_ref, right_ref, panel_ref, out_ref):
    count = left_ref.shape[1]
    out_ref[pl.ds(0, count, stride=cycles), :] = panel_ref[0]
    for b in range(1, cycles):
        update = jnp.dot(left_ref[0], right_ref[b], preferred_element_type=jnp.float32)
        here = pl.ds(b, count, stride=cycles)
        out_ref[here, :] = gram_ref[here, :] + update * share


def gram_update(gram, left, right, panel_part, share):
    cycles, count, depth = left.shape
    width = gram.shape[1]
    lanes = 128
    if width % lanes:
        update = jnp.einsum("auk,bkv->aubv", left, right, preferred_element_type=jnp.float32)
        full = gram.reshape(cycles, count, cycles, width) + update * share
        return full.at[:, :, 0, :].set(panel_part).reshape(gram.shape)
    return pl.pallas_call(
        functools.partial(gram_kernel, cycles, share),
        out_shape=jax.ShapeDtypeStruct(gram.shape, jnp.float32),
        grid=(cycles, width // lanes),
        in_specs=[
            pl.BlockSpec((count * cycles, lanes), lambda a, v: (a, v)),
            pl.BlockSpec((1, count, depth), lambda a, v: (a, 0, 0)),
            pl.BlockSpec((cycles, depth, lanes), lambda a, v: (0, 0, v)),
            pl.BlockSpec((1, count, lanes), lambda a, v: (a, 0, v)),
        ],
        out_specs=pl.BlockSpec((count * cycles, lanes), lambda a, v: (a, v)),
        compiler_params=pltpu.CompilerParams(vmem_limit_bytes=48 * 1024 * 1024),
        name="gram_update",
    )(gram, left, right, panel_part)


def finish(features, gram_in, queries, panel_rows, diag_block, heads):
    row_count = lax.axis_size("rows")
    row_index = lax.axis_index("rows")
    col_index = lax.axis_index("cols")
    cycles, band_rows, _, band_cols = gram_in.shape
    panel_width = band_rows * row_count
    query_count = queries.shape[0]
    every_seq = lax.all_gather(features, "rows", axis=0, tiled=True)
    seq_count, seq_total = features.shape[0], every_seq.shape[0]
    share = 1.0 / seq_total
    flat = jnp.transpose(every_seq, (1, 2, 0))
    first_left = pack(flat[0], True)
    first_right = pack(every_seq[:, 0, :], False)
    own_left = pack(lax.dynamic_slice_in_dim(flat, row_index * band_rows, band_rows, 1), True)
    col_part = lax.dynamic_slice_in_dim(every_seq, col_index * band_cols, band_cols, 2)
    own_right = pack(jnp.transpose(col_part, (1, 0, 2)), False)
    low = (cycles - 1) * band_rows
    left = jnp.concatenate([first_left, own_left[1:].reshape(low, -1)], axis=0)
    below = panel_rows[1:].reshape(low, panel_width)
    used = low + query_count + seq_count
    spare = -used % 128
    head_rows = jnp.concatenate(
        [heads, features[:, 0, :], jnp.zeros((spare, panel_width), jnp.float32)], axis=0
    )
    solved_all = panel(diag_block, below, head_rows, left, first_right, share)
    own_factor = lax.dynamic_slice_in_dim(solved_all, row_index * band_rows, band_rows, 0)
    place = row_index * band_rows + lax.broadcasted_iota(jnp.int32, own_factor.shape, 0)
    own_factor = jnp.where(
        lax.broadcasted_iota(jnp.int32, own_factor.shape, 1) <= place, own_factor, 0.0
    )
    lower_part = solved_all[panel_width : panel_width + low]
    solved = solved_all[panel_width + low : panel_width + low + query_count]
    whitened = solved_all[panel_width + low + query_count : panel_width + used]
    column_block = jnp.concatenate([own_factor, lower_part], axis=0)
    panel_part = lax.dynamic_slice_in_dim(column_block, col_index * band_cols, band_cols, 1)
    gram_next = gram_update(
        gram_in.reshape(cycles * band_rows * cycles, band_cols),
        own_left,
        own_right,
        panel_part.reshape(cycles, band_rows, band_cols),
        share,
    ).reshape(gram_in.shape)
    query_tail = queries[:, 1:, :] - mm_t(solved, lower_part).reshape(
        query_count, cycles - 1, band_rows
    )
    own_head = lax.dynamic_slice_in_dim(solved, row_index * band_rows, band_rows, 1)
    query_next = jnp.concatenate([own_head[:, None, :], query_tail], axis=1)
    scores = mm_t(solved, whitened)
    return gram_next, query_next, scores


def early(gram_in, queries):
    panel_rows = lax.all_gather(gram_in[:, :, 0, :], "cols", axis=2, tiled=True)
    diag_block = lax.all_gather(panel_rows[0], "rows", axis=0, tiled=True)
    heads = lax.all_gather(queries[:, 0, :], "rows", axis=1, tiled=True)
    return panel_rows, diag_block, heads


def local(
    tokens,
    cotangent,
    gate_weight,
    down_weight,
    proj_in,
    proj_out,
    lengths,
    loss_mask,
    gram_in,
    queries,
):
    col_index = lax.axis_index("cols")
    full_tokens, full_cotangent = (
        lax.all_gather(tokens, "cols", axis=1, tiled=True),
        lax.all_gather(cotangent, "cols", axis=1, tiled=True),
    )
    gate_pre = jnp.dot(
        full_tokens,
        lax.all_gather(gate_weight, "rows", axis=0, tiled=True),
        preferred_element_type=jnp.float32,
    )
    grad_hidden = jnp.dot(
        full_cotangent,
        lax.all_gather(down_weight, "rows", axis=0, tiled=True),
        preferred_element_type=jnp.float32,
    )
    grad_up = (grad_hidden * jax.nn.silu(gate_pre)).astype(jnp.bfloat16)
    outer_part = jnp.dot(grad_up, proj_out, preferred_element_type=jnp.float32)
    band_width = tokens.shape[1]
    proj_slice = lax.dynamic_slice_in_dim(proj_in, col_index * band_width, band_width, 0)
    inner_part = jnp.dot(tokens, proj_slice, preferred_element_type=jnp.float32)
    proj_inner, proj_outer = lax.psum((inner_part, outer_part), "cols")
    seq_count, window = loss_mask.shape
    inner_width = proj_in.shape[1]
    outer_width = proj_out.shape[1]
    positions = jnp.arange(window, dtype=jnp.int32)
    token_live = (positions[None, :] >= (window - lengths)[:, None]).astype(
        jnp.float32
    ) * loss_mask.astype(jnp.float32)
    weighted = proj_inner.reshape(seq_count, window, inner_width) * token_live[:, :, None]
    features = jnp.einsum(
        "stk,stl->skl",
        weighted,
        proj_outer.reshape(seq_count, window, outer_width),
        precision=highest,
    )
    cycles, band_rows, _, band_cols = gram_in.shape
    features = features.reshape(seq_count, cycles, band_rows * lax.axis_size("rows"))
    panel_rows, diag_block, heads = early(gram_in, queries)
    return finish(features, gram_in, queries, panel_rows, diag_block, heads)


def solution(mesh):
    return jax.shard_map(
        local,
        mesh=mesh,
        in_specs=(
            P("rows", "cols"),
            P("rows", "cols"),
            P("rows", "cols"),
            P("rows", "cols"),
            P(),
            P("cols", None),
            P("rows"),
            P("rows", None),
            P(None, "rows", None, "cols"),
            P("cols", None, "rows"),
        ),
        out_specs=(P(None, "rows", None, "cols"), P("cols", None, "rows"), P("cols", "rows")),
        check_vma=False,
    )
```

```python
import functools
import itertools
import jax
import jax.numpy as jnp
from jax import lax
from jax.experimental import pallas as pl
from jax.experimental.pallas import tpu as pltpu
from jax.sharding import PartitionSpec as P

highest = lax.Precision.HIGHEST


def eliminate(rows, size):
    shape = (8, size)
    sub = lax.broadcasted_iota(jnp.int32, shape, 0)
    lane = lax.broadcasted_iota(jnp.int32, shape, 1)
    count = size // 8

    def row_of(x, k):
        return jnp.broadcast_to(x[k : k + 1, :], shape)

    for p in range(count):
        base = 8 * p
        inside = (lane >= base) & (lane < base + 8)

        def columns(q):
            return [jnp.broadcast_to(rows[q][:, base + k : base + k + 1], shape) for k in range(8)]

        cols = columns(p)
        own = jnp.where(inside, jnp.where(lane - base == sub, 1.0, 0.0), rows[p])
        scaled_cols, scaled_rows, scale = [], [], jnp.zeros(shape, jnp.float32)
        for k in range(8):
            pivot = row_of(cols[k], k)
            inverse = 1.0 / pivot
            scale = jnp.where(sub == k, lax.rsqrt(pivot), scale)
            heads = [row_of(cols[j], k) * inverse for j in range(k + 1, 8)]
            head_row = row_of(own, k) * inverse
            scaled_cols.append(heads)
            scaled_rows.append(head_row)
            below = jnp.where(sub > k, cols[k], 0.0)
            for j in range(k + 1, 8):
                cols[j] = cols[j] - below * heads[j - k - 1]
            own = own - below * head_row
        for q in range(p + 1, count):
            other = columns(q)
            value = jnp.where(inside, 0.0, rows[q])
            for k in range(8):
                for j in range(k + 1, 8):
                    other[j] = other[j] - other[k] * scaled_cols[k][j - k - 1]
                value = value - other[k] * scaled_rows[k]
            rows[q] = value
        rows[p] = jnp.where(lane < base + 8, own * scale, 0.0)
    return rows


def mm(a, b):
    return jnp.dot(a, b, precision=highest, preferred_element_type=jnp.float32)


def mm_t(a, b):
    return lax.dot_general(
        a, b, (((1,), (1,)), ((), ())), precision=highest, preferred_element_type=jnp.float32
    )


def panel_kernel(block, share, diag_ref, below_ref, head_ref, left_ref, right_ref, out_ref, inv_ref, upper_ref):
    width = diag_ref.shape[0]
    low = below_ref.shape[0]
    total = out_ref.shape[0]
    for start in range(0, width, block):
        rows = slice(start, start + block)
        out_ref[rows, :] = (
            diag_ref[rows, :]
            + jnp.dot(left_ref[rows, :], right_ref[...], preferred_element_type=jnp.float32) * share
        )
    step = block if low % block == 0 else low
    for start in range(0, low, step):
        rows = slice(start, start + step)
        left = slice(width + start, width + start + step)
        out_ref[left, :] = (
            below_ref[rows, :]
            + jnp.dot(left_ref[left, :], right_ref[...], preferred_element_type=jnp.float32) * share
        )
    out_ref[width + low :, :] = head_ref[...]
    blocks = width // block

    def one(b, carry):
        off = pl.multiple_of(b * block, block)
        rows = [
            out_ref[pl.ds(pl.multiple_of(off + 8 * q, 8), 8), pl.ds(off, block)]
            for q in range(block // 8)
        ]
        rows = eliminate(rows, block)
        for q in range(block // 8):
            inv_ref[8 * q : 8 * q + 8, :] = rows[q]
        for s in range(blocks):

            @pl.when(b == s)
            def _():
                here = slice(s * block, (s + 1) * block)
                inv = inv_ref[...]
                if s + 1 < blocks:
                    upper_ref[:, (s + 1) * block :] = mm(inv, out_ref[here, (s + 1) * block :])
                chunk = 2 * block
                for start in range(s * block, total, chunk):
                    these = slice(start, min(start + chunk, total))
                    out_ref[these, here] = mm_t(out_ref[these, here], inv)
                for start in range((s + 1) * block, total, chunk):
                    if s + 1 < blocks:
                        these = slice(start, min(start + chunk, total))
                        out_ref[these, (s + 1) * block :] = out_ref[these, (s + 1) * block :] - mm(
                            out_ref[these, here], upper_ref[:, (s + 1) * block :]
                        )

        return carry

    lax.fori_loop(0, blocks, one, 0)


def panel(diag, below, heads, left, right, share):
    block = 128
    width, low, extra = diag.shape[0], below.shape[0], heads.shape[0]
    return pl.pallas_call(
        functools.partial(panel_kernel, block, share),
        out_shape=jax.ShapeDtypeStruct((width + low + extra, width), jnp.float32),
        in_specs=[pl.BlockSpec(memory_space=pltpu.VMEM)] * 5,
        out_specs=pl.BlockSpec(memory_space=pltpu.VMEM),
        scratch_shapes=[pltpu.VMEM((block, block), jnp.float32), pltpu.VMEM((block, width), jnp.float32)],
        compiler_params=pltpu.CompilerParams(vmem_limit_bytes=48 * 1024 * 1024),
        name="panel_factor",
    )(diag, below, heads, left, right)


def pack(x, left):
    high = lax.reduce_precision(x, 8, 7)
    rest = x - high
    mid = lax.reduce_precision(rest, 8, 7)
    low = rest - mid
    high, mid, low = (v.astype(jnp.bfloat16) for v in (high, mid, low))
    parts = (high, high, mid, high, low, mid) if left else (high, mid, high, low, high, mid)
    return jnp.concatenate(parts, axis=-1 if left else -2)


def gram_kernel(cycles, share, gram_ref, left_ref, right_ref, panel_ref, out_ref):
    count = left_ref.shape[1]
    out_ref[pl.ds(0, count, stride=cycles), :] = panel_ref[0]
    for b in range(1, cycles):
        update = jnp.dot(left_ref[0], right_ref[b], preferred_element_type=jnp.float32)
        here = pl.ds(b, count, stride=cycles)
        out_ref[here, :] = gram_ref[here, :] + update * share


def gram_update(gram, left, right, panel_part, share):
    cycles, count, depth = left.shape
    width = gram.shape[1]
    lanes = 128
    if width % lanes:
        update = jnp.einsum("auk,bkv->aubv", left, right, preferred_element_type=jnp.float32)
        full = gram.reshape(cycles, count, cycles, width) + update * share
        return full.at[:, :, 0, :].set(panel_part).reshape(gram.shape)
    return pl.pallas_call(
        functools.partial(gram_kernel, cycles, share),
        out_shape=jax.ShapeDtypeStruct(gram.shape, jnp.float32),
        grid=(cycles, width // lanes),
        in_specs=[
            pl.BlockSpec((count * cycles, lanes), lambda a, v: (a, v)),
            pl.BlockSpec((1, count, depth), lambda a, v: (a, 0, 0)),
            pl.BlockSpec((cycles, depth, lanes), lambda a, v: (0, 0, v)),
            pl.BlockSpec((1, count, lanes), lambda a, v: (a, 0, v)),
        ],
        out_specs=pl.BlockSpec((count * cycles, lanes), lambda a, v: (a, v)),
        compiler_params=pltpu.CompilerParams(vmem_limit_bytes=48 * 1024 * 1024),
        name="gram_update",
    )(gram, left, right, panel_part)


def sizes():
    rows, cols = lax.axis_size("rows"), lax.axis_size("cols")
    pair_x = 2 if rows % 2 == 0 else 1
    pair_core = 2 if cols % 2 == 0 else 1
    return {"z": rows // pair_x, "x": pair_x, "y": cols // pair_core, "core": pair_core}


def place_of(size):
    row, col = lax.axis_index("rows"), lax.axis_index("cols")
    return {
        "z": row // size["x"],
        "x": row % size["x"],
        "y": col // size["core"],
        "core": col % size["core"],
    }


def moves(size, axis, step, wrap=True):
    names = ("z", "x", "y", "core")
    pairs = []
    for at in itertools.product(*(range(size[name]) for name in names)):
        to = list(at)
        which = names.index(axis)
        to[which] = at[which] + step
        if wrap:
            to[which] %= size[axis]
        elif not 0 <= to[which] < size[axis]:
            continue
        linear = lambda spot: ((spot[0] * size["x"] + spot[1]) * size["y"] + spot[2]) * size["core"] + spot[3]
        pairs.append((linear(at), linear(to)))
    return pairs


def shift(value, size, axis, step, wrap=True):
    return lax.ppermute(value, ("rows", "cols"), moves(size, axis, step, wrap))


def gather(value, size, me, axis):
    count = size[axis]
    if count == 1:
        return value[None]
    parts = jnp.zeros((count,) + value.shape, value.dtype)
    parts = lax.dynamic_update_index_in_dim(parts, value, me[axis], 0)
    for step in range(1, count):
        came = shift(value, size, axis, step)
        parts = lax.dynamic_update_index_in_dim(parts, came, (me[axis] - step) % count, 0)
    return parts


def total(value, size, axis):
    result = value
    for step in range(1, size[axis]):
        result = result + shift(value, size, axis, step)
    return result


def chain(value, size, me):
    count = size["z"]
    if count > 4:
        parts = gather(value, size, me, "z")
        return [lax.dynamic_index_in_dim(parts, (me["z"] - s) % count, 0, False) for s in range(count)]
    up, down = [value], [value]
    for _ in range(1, count):
        up.append(shift(up[-1], size, "z", 1, False))
        down.append(shift(down[-1], size, "z", -1, False))
    slots = [value]
    for s in range(1, count):
        slots.append(jnp.where(me["z"] >= s, up[s], down[count - s]))
    return slots


def gathered_tokens(both, size, me):
    kinds, height, width = both.shape
    slots = chain(both, size, me)
    full = jnp.zeros((kinds, size["z"] * height, size["y"] * size["core"] * width), both.dtype)
    for s, slot in enumerate(slots):
        for dy in range(size["y"]):
            own = slot if dy == 0 else shift(slot, size, "y", dy)
            for dc in range(size["core"]):
                piece = own if dc == 0 else shift(own, size, "core", dc)
                col = ((me["y"] - dy) % size["y"]) * size["core"] + (me["core"] - dc) % size["core"]
                full = lax.dynamic_update_slice(full, piece, (0, s * height, col * width))
    return full


def weight_parts(gate_weight, down_weight, size, me):
    depth, width = gate_weight.shape
    count = size["z"]
    share = width // count
    both = jnp.stack([gate_weight, down_weight]).reshape(2, depth, count, share)
    both = jnp.transpose(both, (2, 0, 1, 3))
    parts = []
    for s in range(count):
        piece = lax.dynamic_index_in_dim(both, (me["z"] + s) % count, 0, False)
        if s > 0:
            piece = shift(piece, size, "z", s)
        across = gather(piece, size, me, "x")
        parts.append(jnp.transpose(across, (1, 0, 2, 3)).reshape(2, size["x"] * depth, share))
    return parts


def summed_outer(outer_part, size, me):
    count = size["z"]
    height = outer_part.shape[0] // count
    result = outer_part[:height]
    for s in range(1, count):
        result = result + shift(outer_part[s * height : (s + 1) * height], size, "z", -s)
    return total(total(result, size, "y"), size, "core")


def early(gram_in, queries, size, me):
    cycles, band_rows, _, band_cols = gram_in.shape
    diag = gram_in[0, :, 0, :]
    diag = gather(gather(diag, size, me, "z"), size, me, "x")
    diag = gather(gather(diag, size, me, "y"), size, me, "core")
    diag = jnp.transpose(diag, (3, 2, 4, 1, 0, 5)).reshape(
        size["z"] * size["x"] * band_rows, size["y"] * size["core"] * band_cols
    )
    below = gram_in[1:, :, 0, :]
    below = gather(gather(below, size, me, "y"), size, me, "core")
    below = jnp.transpose(below, (2, 3, 1, 0, 4)).reshape((cycles - 1) * band_rows, diag.shape[1])
    heads = gather(gather(queries[:, 0, :], size, me, "x"), size, me, "z")
    heads = jnp.transpose(heads, (2, 0, 1, 3)).reshape(queries.shape[0], diag.shape[0])
    return diag, below, heads


def spread_features(features, size, me, band_cols):
    seqs, cycles, panel_width = features.shape
    col = me["y"] * size["core"] + me["core"]
    part = lax.dynamic_slice_in_dim(features, col * band_cols, band_cols, 2)
    part = gather(gather(part, size, me, "x"), size, me, "z")
    part = part.reshape(-1, cycles, band_cols)
    full = gather(gather(part, size, me, "y"), size, me, "core")
    return part, jnp.transpose(full, (2, 3, 1, 0, 4)).reshape(part.shape[0], cycles, panel_width)


def finish(features, every_seq, col_part, gram_in, queries, diag_block, below, heads):
    row_count = lax.axis_size("rows")
    row_index = lax.axis_index("rows")
    col_index = lax.axis_index("cols")
    cycles, band_rows, _, band_cols = gram_in.shape
    panel_width = band_rows * row_count
    query_count = queries.shape[0]
    seq_count, seq_total = features.shape[0], every_seq.shape[0]
    share = 1.0 / seq_total
    flat = jnp.transpose(every_seq, (1, 2, 0))
    first_left = pack(flat[0], True)
    first_right = pack(every_seq[:, 0, :], False)
    own_left = pack(lax.dynamic_slice_in_dim(flat, row_index * band_rows, band_rows, 1), True)
    own_right = pack(jnp.transpose(col_part, (1, 0, 2)), False)
    low = (cycles - 1) * band_rows
    left = jnp.concatenate([first_left, own_left[1:].reshape(low, -1)], axis=0)
    used = low + query_count + seq_count
    spare = -used % 128
    head_rows = jnp.concatenate(
        [heads, features[:, 0, :], jnp.zeros((spare, panel_width), jnp.float32)], axis=0
    )
    solved_all = panel(diag_block, below, head_rows, left, first_right, share)
    own_factor = lax.dynamic_slice_in_dim(solved_all, row_index * band_rows, band_rows, 0)
    place = row_index * band_rows + lax.broadcasted_iota(jnp.int32, own_factor.shape, 0)
    own_factor = jnp.where(
        lax.broadcasted_iota(jnp.int32, own_factor.shape, 1) <= place, own_factor, 0.0
    )
    lower_part = solved_all[panel_width : panel_width + low]
    solved = solved_all[panel_width + low : panel_width + low + query_count]
    whitened = solved_all[panel_width + low + query_count : panel_width + used]
    column_block = jnp.concatenate([own_factor, lower_part], axis=0)
    panel_part = lax.dynamic_slice_in_dim(column_block, col_index * band_cols, band_cols, 1)
    gram_next = gram_update(
        gram_in.reshape(cycles * band_rows * cycles, band_cols),
        own_left,
        own_right,
        panel_part.reshape(cycles, band_rows, band_cols),
        share,
    ).reshape(gram_in.shape)
    query_tail = queries[:, 1:, :] - mm_t(solved, lower_part).reshape(
        query_count, cycles - 1, band_rows
    )
    own_head = lax.dynamic_slice_in_dim(solved, row_index * band_rows, band_rows, 1)
    query_next = jnp.concatenate([own_head[:, None, :], query_tail], axis=1)
    scores = mm_t(solved, whitened)
    return gram_next, query_next, scores


def local(
    tokens,
    cotangent,
    gate_weight,
    down_weight,
    proj_in,
    proj_out,
    lengths,
    loss_mask,
    gram_in,
    queries,
):
    size = sizes()
    me = place_of(size)
    height = tokens.shape[0]
    both = gathered_tokens(jnp.stack([tokens, cotangent]), size, me)
    gate_pre, grad_hidden = 0.0, 0.0
    for s, part in enumerate(weight_parts(gate_weight, down_weight, size, me)):
        depth = part.shape[1]
        start = ((me["z"] - s) % size["z"]) * depth
        piece = lax.dynamic_slice_in_dim(both, start, depth, 2)
        gate_pre = gate_pre + jnp.dot(piece[0], part[0], preferred_element_type=jnp.float32)
        grad_hidden = grad_hidden + jnp.dot(piece[1], part[1], preferred_element_type=jnp.float32)
    grad_up = (grad_hidden * jax.nn.silu(gate_pre)).astype(jnp.bfloat16)
    share = grad_up.shape[1]
    proj_slice = lax.dynamic_slice_in_dim(proj_out, me["z"] * share, share, 0)
    outer_part = jnp.dot(grad_up, proj_slice, preferred_element_type=jnp.float32)
    proj_inner = jnp.dot(both[0, :height], proj_in, preferred_element_type=jnp.float32)
    proj_outer = summed_outer(outer_part, size, me)
    seq_count, window = loss_mask.shape
    inner_width = proj_in.shape[1]
    outer_width = proj_out.shape[1]
    positions = jnp.arange(window, dtype=jnp.int32)
    token_live = (positions[None, :] >= (window - lengths)[:, None]).astype(
        jnp.float32
    ) * loss_mask.astype(jnp.float32)
    weighted = proj_inner.reshape(seq_count, window, inner_width) * token_live[:, :, None]
    features = jnp.einsum(
        "stk,stl->skl",
        weighted,
        proj_outer.reshape(seq_count, window, outer_width),
        precision=highest,
    )
    cycles, band_rows, _, band_cols = gram_in.shape
    features = features.reshape(seq_count, cycles, band_rows * lax.axis_size("rows"))
    diag_block, below, heads = early(gram_in, queries, size, me)
    col_part, every_seq = spread_features(features, size, me, band_cols)
    return finish(features, every_seq, col_part, gram_in, queries, diag_block, below, heads)


def solution(mesh):
    return jax.shard_map(
        local,
        mesh=mesh,
        in_specs=(
            P("rows", "cols"),
            P("rows", "cols"),
            P("rows", "cols"),
            P("rows", "cols"),
            P(),
            P("cols", None),
            P("rows"),
            P("rows", None),
            P(None, "rows", None, "cols"),
            P("cols", None, "rows"),
        ),
        out_specs=(P(None, "rows", None, "cols"), P("cols", None, "rows"), P("cols", "rows")),
        check_vma=False,
    )
```

```python
import functools
import jax
import jax.numpy as jnp
from jax import lax
from jax.experimental import pallas as pl
from jax.experimental.pallas import tpu as pltpu
from jax.sharding import PartitionSpec as P

highest = lax.Precision.HIGHEST
vmem_limit = 56 * 1024 * 1024


def eliminate(rows, size):
    shape = (8, size)
    sub = lax.broadcasted_iota(jnp.int32, shape, 0)
    lane = lax.broadcasted_iota(jnp.int32, shape, 1)
    count = size // 8

    def row_of(x, k):
        return jnp.broadcast_to(x[k : k + 1, :], shape)

    for p in range(count):
        base = 8 * p
        inside = (lane >= base) & (lane < base + 8)

        def columns(q):
            return [jnp.broadcast_to(rows[q][:, base + k : base + k + 1], shape) for k in range(8)]

        cols = columns(p)
        own = jnp.where(inside, jnp.where(lane - base == sub, 1.0, 0.0), rows[p])
        scaled_cols, scaled_rows, scale = [], [], jnp.zeros(shape, jnp.float32)
        for k in range(8):
            pivot = row_of(cols[k], k)
            inverse = 1.0 / pivot
            scale = jnp.where(sub == k, lax.rsqrt(pivot), scale)
            heads = [row_of(cols[j], k) * inverse for j in range(k + 1, 8)]
            head_row = row_of(own, k) * inverse
            scaled_cols.append(heads)
            scaled_rows.append(head_row)
            below = jnp.where(sub > k, cols[k], 0.0)
            for j in range(k + 1, 8):
                cols[j] = cols[j] - below * heads[j - k - 1]
            own = own - below * head_row
        for q in range(p + 1, count):
            other = columns(q)
            value = jnp.where(inside, 0.0, rows[q])
            for k in range(8):
                for j in range(k + 1, 8):
                    other[j] = other[j] - other[k] * scaled_cols[k][j - k - 1]
                value = value - other[k] * scaled_rows[k]
            rows[q] = value
        rows[p] = jnp.where(lane < base + 8, own * scale, 0.0)
    return rows


def mm(a, b):
    return jnp.dot(a, b, precision=highest, preferred_element_type=jnp.float32)


def mm_t(a, b):
    return lax.dot_general(
        a, b, (((1,), (1,)), ((), ())), precision=highest, preferred_element_type=jnp.float32
    )


def three_way(x):
    high = x.astype(jnp.bfloat16)
    rest = x - high.astype(jnp.float32)
    mid = rest.astype(jnp.bfloat16)
    return high, mid, (rest - mid.astype(jnp.float32)).astype(jnp.bfloat16)


def pack_left(x):
    high, mid, low = three_way(x)
    return jnp.concatenate([high, high, mid, high, low, mid], axis=0)


def pack_right(x):
    high, mid, low = three_way(x)
    return jnp.concatenate([high, mid, high, low, high, mid], axis=0)


def outer_sum(left, right):
    return lax.dot_general(
        left, right, (((0,), (0,)), ((), ())), preferred_element_type=jnp.float32
    )


def panel_kernel(
    block,
    share,
    band,
    spot_ref,
    diag_ref,
    below_ref,
    head_ref,
    first_ref,
    own_ref,
    part_ref,
    solved_ref,
    product_ref,
    work_ref,
    inv_ref,
    upper_ref,
):
    width = diag_ref.shape[0]
    low = below_ref.shape[0]
    total = work_ref.shape[0]
    blocks = width // block
    right = pack_right(first_ref[...])
    for start in range(0, width, block):
        rows = slice(start, start + block)
        left = pack_left(first_ref[:, rows])
        work_ref[rows, :] = diag_ref[rows, :] + outer_sum(left, right) * share
    cycles, _, band_rows = own_ref.shape
    for a in range(1, cycles):
        rows = slice((a - 1) * band_rows, a * band_rows)
        here = slice(width + (a - 1) * band_rows, width + a * band_rows)
        work_ref[here, :] = below_ref[rows, :] + outer_sum(pack_left(own_ref[a]), right) * share
    work_ref[width + low :, :] = head_ref[...]

    def one(b, carry):
        off = pl.multiple_of(b * block, block)
        rows = [
            work_ref[pl.ds(pl.multiple_of(off + 8 * q, 8), 8), pl.ds(off, block)]
            for q in range(block // 8)
        ]
        rows = eliminate(rows, block)
        for q in range(block // 8):
            inv_ref[8 * q : 8 * q + 8, :] = rows[q]
        for s in range(blocks):

            @pl.when(b == s)
            def _():
                here = slice(s * block, (s + 1) * block)
                after = slice((s + 1) * block, width)
                inv = inv_ref[...]
                if s + 1 < blocks:
                    upper_ref[:, after] = mm(inv, work_ref[here, after])
                chunk = 2 * block
                for start in range(s * block, total, chunk):
                    these = slice(start, min(start + chunk, total))
                    work_ref[these, here] = mm_t(work_ref[these, here], inv)
                for start in range((s + 1) * block, total, chunk):
                    if s + 1 < blocks:
                        these = slice(start, min(start + chunk, total))
                        work_ref[these, after] = work_ref[these, after] - mm(
                            work_ref[these, here], upper_ref[:, after]
                        )

        return carry

    lax.fori_loop(0, blocks, one, 0)
    solved_ref[...] = work_ref[width + low :, :]
    product_ref[...] = mm_t(work_ref[width + low :, :], work_ref[width:, :])
    if band == 0:
        part_ref[...] = work_ref[: width + low, :]
    else:
        row_start = spot_ref[0] * band_rows
        lanes = pl.ds(pl.multiple_of(spot_ref[1] * band, 128), band)
        mine = work_ref[pl.ds(pl.multiple_of(row_start, 8), band_rows), lanes]
        row = row_start + lax.broadcasted_iota(jnp.int32, mine.shape, 0)
        col = spot_ref[1] * band + lax.broadcasted_iota(jnp.int32, mine.shape, 1)
        part_ref[:band_rows, :] = jnp.where(col <= row, mine, 0.0)
        part_ref[band_rows:, :] = work_ref[width : width + low, lanes]


def panel(spot, diag, below, heads, first, own, band, share):
    block = 128
    width, low, extra = diag.shape[0], below.shape[0], heads.shape[0]
    cycles, _, band_rows = own.shape
    part = (cycles * band_rows, band) if band else (width + low, width)
    whole = pl.BlockSpec(memory_space=pltpu.VMEM)
    return pl.pallas_call(
        functools.partial(panel_kernel, block, share, band),
        out_shape=[
            jax.ShapeDtypeStruct(part, jnp.float32),
            jax.ShapeDtypeStruct((extra, width), jnp.float32),
            jax.ShapeDtypeStruct((extra, low + extra), jnp.float32),
        ],
        in_specs=[pl.BlockSpec(memory_space=pltpu.SMEM)] + [whole] * 5,
        out_specs=[whole] * 3,
        scratch_shapes=[
            pltpu.VMEM((width + low + extra, width), jnp.float32),
            pltpu.VMEM((block, block), jnp.float32),
            pltpu.VMEM((block, width), jnp.float32),
        ],
        compiler_params=pltpu.CompilerParams(vmem_limit_bytes=vmem_limit),
        name="panel_factor",
    )(spot, diag, below, heads, first, own)


def gram_kernel(share, gram_ref, own_ref, col_ref, panel_ref, out_ref):
    steps, _, count = own_ref.shape
    cycles, _, lanes = col_ref.shape
    right = jnp.concatenate([pack_right(col_ref[b]) for b in range(cycles)], axis=1)
    for a in range(steps):
        base = a * count * cycles
        out_ref[pl.ds(base, count, stride=cycles), :] = panel_ref[a]
        update = outer_sum(pack_left(own_ref[a]), right) * share
        for b in range(1, cycles):
            here = pl.ds(base + b, count, stride=cycles)
            out_ref[here, :] = gram_ref[here, :] + update[:, b * lanes : (b + 1) * lanes]


def gram_update(gram_in, own, col, panel_part, share):
    cycles, seqs, count = own.shape
    width = col.shape[2]
    lanes = 128
    if width % lanes:
        update = jnp.einsum("asu,bsv->aubv", own, col, precision=highest)
        return (gram_in + update * share).at[:, :, 0, :].set(panel_part)
    steps = 2 if cycles % 2 == 0 else 1
    gram = gram_in.reshape(cycles * count * cycles, width)
    tall = pl.BlockSpec((steps * count * cycles, lanes), lambda v, a: (a, v))
    return pl.pallas_call(
        functools.partial(gram_kernel, share),
        out_shape=jax.ShapeDtypeStruct(gram.shape, jnp.float32),
        grid=(width // lanes, cycles // steps),
        in_specs=[
            tall,
            pl.BlockSpec((steps, seqs, count), lambda v, a: (a, 0, 0)),
            pl.BlockSpec((cycles, seqs, lanes), lambda v, a: (0, 0, v)),
            pl.BlockSpec((steps, count, lanes), lambda v, a: (a, 0, v)),
        ],
        out_specs=tall,
        compiler_params=pltpu.CompilerParams(vmem_limit_bytes=vmem_limit),
        name="gram_update",
    )(gram, own, col, panel_part).reshape(gram_in.shape)


def finish(features, first, own, col, gram_in, queries, diag, below, heads):
    row_index, col_index = lax.axis_index("rows"), lax.axis_index("cols")
    cycles, band_rows, _, band_cols = gram_in.shape
    width, low = diag.shape[0], below.shape[0]
    query_count, seq_count = queries.shape[0], features.shape[0]
    share = 1.0 / first.shape[0]
    used = query_count + seq_count
    spare = -(low + used) % 128
    head_rows = jnp.concatenate(
        [heads, features, jnp.zeros((spare, width), jnp.float32)], axis=0
    )
    band = band_cols if band_cols % 128 == 0 else 0
    spot = jnp.stack([row_index, col_index]).astype(jnp.int32)
    part, solved, product = panel(spot, diag, below, head_rows, first, own, band, share)
    if band == 0:
        mine = lax.dynamic_slice_in_dim(part, row_index * band_rows, band_rows, 0)
        row = row_index * band_rows + lax.broadcasted_iota(jnp.int32, mine.shape, 0)
        mine = jnp.where(lax.broadcasted_iota(jnp.int32, mine.shape, 1) <= row, mine, 0.0)
        part = jnp.concatenate([mine, part[width:]], axis=0)
        part = lax.dynamic_slice_in_dim(part, col_index * band_cols, band_cols, 1)
    gram_next = gram_update(
        gram_in, own, col, part.reshape(cycles, band_rows, band_cols), share
    )
    tail = queries[:, 1:, :] - product[:query_count, :low].reshape(
        query_count, cycles - 1, band_rows
    )
    own_head = lax.dynamic_slice_in_dim(
        solved[:query_count], row_index * band_rows, band_rows, 1
    )
    query_next = jnp.concatenate([own_head[:, None, :], tail], axis=1)
    scores = product[:query_count, low + query_count : low + used]
    return gram_next, query_next, scores


def sequence_features(proj_inner, proj_outer, lengths, loss_mask):
    seq_count, window = loss_mask.shape
    positions = jnp.arange(window, dtype=jnp.int32)
    token_live = (positions[None, :] >= (window - lengths)[:, None]).astype(
        jnp.float32
    ) * loss_mask.astype(jnp.float32)
    weighted = proj_inner.reshape(seq_count, window, -1) * token_live[:, :, None]
    features = jnp.einsum(
        "stk,stl->skl",
        weighted,
        proj_outer.reshape(seq_count, window, -1),
        precision=highest,
    )
    return features.reshape(seq_count, -1)


def general(
    tokens,
    cotangent,
    gate_weight,
    down_weight,
    proj_in,
    proj_out,
    lengths,
    loss_mask,
    gram_in,
    queries,
):
    row_index, col_index = lax.axis_index("rows"), lax.axis_index("cols")
    full_tokens = lax.all_gather(tokens, "cols", axis=1, tiled=True)
    full_cotangent = lax.all_gather(cotangent, "cols", axis=1, tiled=True)
    gate_pre = jnp.dot(
        full_tokens,
        lax.all_gather(gate_weight, "rows", axis=0, tiled=True),
        preferred_element_type=jnp.float32,
    )
    grad_hidden = jnp.dot(
        full_cotangent,
        lax.all_gather(down_weight, "rows", axis=0, tiled=True),
        preferred_element_type=jnp.float32,
    )
    grad_up = (grad_hidden * jax.nn.silu(gate_pre)).astype(jnp.bfloat16)
    outer_part = jnp.dot(grad_up, proj_out, preferred_element_type=jnp.float32)
    proj_inner = jnp.dot(full_tokens, proj_in, preferred_element_type=jnp.float32)
    proj_outer = lax.psum(outer_part, "cols")
    features = sequence_features(proj_inner, proj_outer, lengths, loss_mask)
    cycles, band_rows, _, band_cols = gram_in.shape
    every = lax.all_gather(features, "rows", axis=0, tiled=True)
    every = jnp.transpose(every.reshape(every.shape[0], cycles, -1), (1, 0, 2))
    own = lax.dynamic_slice_in_dim(every, row_index * band_rows, band_rows, 2)
    col = lax.dynamic_slice_in_dim(every, col_index * band_cols, band_cols, 2)
    panel_rows = lax.all_gather(gram_in[:, :, 0, :], "cols", axis=2, tiled=True)
    width = panel_rows.shape[2]
    diag = lax.all_gather(panel_rows[0], "rows", axis=0, tiled=True)
    heads = lax.all_gather(queries[:, 0, :], "rows", axis=1, tiled=True)
    below = panel_rows[1:].reshape((cycles - 1) * band_rows, width)
    return finish(features[:, :width], every[0], own, col, gram_in, queries, diag, below, heads)


sizes = {"z": 4, "x": 2, "y": 2, "core": 2}


def shift(value, axis, step, wrap=True):
    names = ("z", "x", "y", "core")
    pairs = []
    for source in range(sizes["z"] * sizes["x"] * sizes["y"] * sizes["core"]):
        rest, at = source, []
        for name in reversed(names):
            at.append(rest % sizes[name])
            rest //= sizes[name]
        at = at[::-1]
        which = names.index(axis)
        there = at[which] + step
        if wrap:
            there %= sizes[axis]
        elif not 0 <= there < sizes[axis]:
            continue
        at[which] = there
        target = 0
        for name, spot in zip(names, at):
            target = target * sizes[name] + spot
        pairs.append((source, target))
    return lax.ppermute(value, ("rows", "cols"), pairs)


def in_order(place, own, other):
    first = jnp.where(place == 0, own, other)
    second = jnp.where(place == 0, other, own)
    return first, second


def gather_columns(value, me):
    width = value.shape[1]
    near = jnp.concatenate(in_order(me["y"], value, shift(value, "y", 1)), axis=1)
    left, right = in_order(me["core"], near, shift(near, "core", 1))
    return jnp.concatenate(
        [left[:, :width], right[:, :width], left[:, width:], right[:, width:]], axis=1
    )


slot_of = (((0, 3, 2, 1), (0, 2, 3, 1), (0, 1, 3, 2), (0, 1, 2, 3)))


def gradient_kernel(spot_ref, *refs):
    token_refs, refs = refs[:16], refs[16:]
    weight_refs, refs = refs[:8], refs[8:]
    out_proj_ref, in_proj_ref, outer_ref, inner_ref, token_buf, weight_buf, token_sem, weight_sem = refs
    z, x, y, core = (spot_ref[i] for i in range(4))
    height, band = token_refs[0].shape[1:]
    depth = weight_refs[0].shape[2]
    weight_copies = []
    for i, ref in enumerate(weight_refs):
        row = ((z - i // 2) % 4) * 2 + (x + i % 2) % 2
        there = weight_buf.at[:, :, pl.ds(pl.multiple_of(row * depth, 128), depth)]
        weight_copies.append(pltpu.make_async_copy(ref, there, weight_sem.at[i]))
    token_copies = []
    for i, ref in enumerate(token_refs):
        col = ((y + i % 4 // 2) % 2) * 2 + (core + i % 2) % 2
        there = token_buf.at[i // 4, :, :, pl.ds(pl.multiple_of(col * band, 128), band)]
        token_copies.append(pltpu.make_async_copy(ref, there, token_sem.at[i]))
    for copy in weight_copies + token_copies:
        copy.start()
    for copy in weight_copies:
        copy.wait()
    for s in range(4):
        for copy in token_copies[4 * s : 4 * s + 4]:
            copy.wait()
        if s == 0:
            inner_ref[...] = jnp.dot(
                token_buf[0, 0], in_proj_ref[...], preferred_element_type=jnp.float32
            )
        over = (((1,), (1,)), ((), ()))
        gate = lax.dot_general(
            token_buf[s, 0], weight_buf[0], over, preferred_element_type=jnp.float32
        )
        hidden = lax.dot_general(
            token_buf[s, 1], weight_buf[1], over, preferred_element_type=jnp.float32
        )
        grad = (hidden * (gate / (1.0 + jnp.exp(-gate)))).astype(jnp.bfloat16)
        outer_ref[s] = jnp.dot(grad, out_proj_ref[...], preferred_element_type=jnp.float32)


def gradient(spot, tokens, weights, out_proj, in_proj):
    kinds, height, band = tokens[0].shape
    share, depth = weights[0].shape[1:]
    full = depth * 8
    hbm = pl.BlockSpec(memory_space=pl.ANY)
    whole = pl.BlockSpec(memory_space=pltpu.VMEM)
    return pl.pallas_call(
        gradient_kernel,
        out_shape=[
            jax.ShapeDtypeStruct((4, height, out_proj.shape[1]), jnp.float32),
            jax.ShapeDtypeStruct((height, in_proj.shape[1]), jnp.float32),
        ],
        in_specs=[pl.BlockSpec(memory_space=pltpu.SMEM)] + [hbm] * 24 + [whole] * 2,
        out_specs=[whole] * 2,
        scratch_shapes=[
            pltpu.VMEM((4, kinds, height, full), jnp.bfloat16),
            pltpu.VMEM((kinds, share, full), jnp.bfloat16),
            pltpu.SemaphoreType.DMA((16,)),
            pltpu.SemaphoreType.DMA((8,)),
        ],
        compiler_params=pltpu.CompilerParams(vmem_limit_bytes=vmem_limit),
        name="gradient",
    )(spot, *tokens, *weights, out_proj, in_proj)


def rounds(tokens, cotangent, gate_weight, down_weight, gram_in, queries, me):
    z = me["z"]
    both = jnp.stack([tokens, cotangent])
    depth, width = gate_weight.shape
    share = width // 4
    cut = jnp.stack(
        [gate_weight.T.reshape(4, share, depth), down_weight.T.reshape(4, share, depth)], axis=1
    )
    piece = [lax.dynamic_index_in_dim(cut, (z + s) % 4, 0, False) for s in range(4)]
    cycles, band_rows, _, band_cols = gram_in.shape
    corner = gram_in[0, :, 0, :]
    below = gram_in[1:, :, 0, :].reshape((cycles - 1) * band_rows, band_cols)
    head = queries[:, 0, :]

    up1, down1 = shift(both, "z", 1, False), shift(both, "z", -1, False)
    wz1 = shift(piece[1], "z", 1)
    y_own = shift(both, "y", 1)
    wx0 = shift(piece[0], "x", 1)
    c_own = shift(both, "core", 1)
    up1, down1, wz1, y_own, wx0, p3, below = lax.optimization_barrier(
        (up1, down1, wz1, y_own, wx0, piece[3], below)
    )

    slot_a = jnp.where(z < 2, down1, up1)
    up2, down2 = shift(up1, "z", 1, False), shift(down1, "z", -1, False)
    wz3 = shift(p3, "z", 3)
    y_a = shift(slot_a, "y", 1)
    wx1 = shift(wz1, "x", 1)
    c_a = shift(slot_a, "core", 1)
    cy_own = shift(y_own, "core", 1)
    up2, down2, wz3, y_a, wx1, p2, corner, head = lax.optimization_barrier(
        (up2, down2, wz3, y_a, wx1, piece[2], corner, head)
    )

    slot_b = jnp.where(z == 0, down2, jnp.where(z == 1, up1, jnp.where(z == 2, down1, up2)))
    up3, down3 = shift(up2, "z", 1, False), shift(down2, "z", -1, False)
    wz2 = shift(p2, "z", 2)
    y_b = shift(slot_b, "y", 1)
    wx3 = shift(wz3, "x", 1)
    c_b = shift(slot_b, "core", 1)
    cy_a = shift(y_a, "core", 1)
    up3, down3, wz2, y_b, wx3 = lax.optimization_barrier((up3, down3, wz2, y_b, wx3))

    slot_c = jnp.where(z == 0, down3, jnp.where(z == 1, down2, jnp.where(z == 2, up2, up3)))
    y_c = shift(slot_c, "y", 1)
    wx2 = shift(wz2, "x", 1)
    c_c = shift(slot_c, "core", 1)
    cy_b = shift(y_b, "core", 1)
    cy_c = shift(y_c, "core", 1)
    pieces = [
        both, c_own, y_own, cy_own,
        slot_a, c_a, y_a, cy_a,
        slot_b, c_b, y_b, cy_b,
        slot_c, c_c, y_c, cy_c,
    ]
    weights = [piece[0], wx0, wz1, wx1, wz2, wx2, wz3, wx3]

    near = [corner] + [shift(corner, "z", s) for s in range(1, 4)]
    across = shift(jnp.concatenate(near, axis=0), "x", 1)
    diag = jnp.zeros((8 * band_rows, band_cols), jnp.float32)
    for s in range(4):
        row = ((z - s) % 4) * 2
        diag = lax.dynamic_update_slice(diag, near[s], ((row + me["x"]) * band_rows, 0))
        other = across[s * band_rows : (s + 1) * band_rows]
        diag = lax.dynamic_update_slice(diag, other, ((row + 1 - me["x"]) * band_rows, 0))
    diag = gather_columns(diag, me)
    below = gather_columns(below, me)
    pair = jnp.concatenate(in_order(me["x"], head, shift(head, "x", 1)), axis=1)
    span = pair.shape[1]
    heads = jnp.zeros((head.shape[0], 4 * span), jnp.float32)
    for s in range(4):
        came = pair if s == 0 else shift(pair, "z", s)
        heads = lax.dynamic_update_slice(heads, came, (0, ((z - s) % 4) * span))
    return pieces, weights, diag, below, heads


def local(
    tokens,
    cotangent,
    gate_weight,
    down_weight,
    proj_in,
    proj_out,
    lengths,
    loss_mask,
    gram_in,
    queries,
):
    row_index, col_index = lax.axis_index("rows"), lax.axis_index("cols")
    me = {"z": row_index // 2, "x": row_index % 2, "y": col_index // 2, "core": col_index % 2}
    pieces, weights, diag, below, heads = rounds(
        tokens, cotangent, gate_weight, down_weight, gram_in, queries, me
    )
    share = weights[0].shape[1]
    out_proj = lax.dynamic_slice_in_dim(proj_out, me["z"] * share, share, 0)
    spot = jnp.stack([me["z"], me["x"], me["y"], me["core"]]).astype(jnp.int32)
    outer, proj_inner = gradient(spot, pieces, weights, out_proj, proj_in)
    proj_outer = outer[0]
    table = jnp.array(slot_of, jnp.int32)
    for s in range(1, 4):
        part = lax.dynamic_index_in_dim(outer, table[me["z"], s], 0, False)
        proj_outer = proj_outer + shift(part, "z", -s)
    proj_outer = proj_outer + shift(proj_outer, "y", 1)
    proj_outer = proj_outer + shift(proj_outer, "core", 1)
    features = sequence_features(proj_inner, proj_outer, lengths, loss_mask)
    cycles, band_rows, _, band_cols = gram_in.shape
    seqs = features.shape[0]
    width = diag.shape[0]
    mine = lax.dynamic_slice_in_dim(
        features.reshape(seqs * cycles, width), col_index * band_cols, band_cols, 1
    )
    pair = jnp.concatenate([mine, shift(mine, "x", 1)], axis=0)
    column = jnp.concatenate([pair] + [shift(pair, "z", s) for s in range(1, 4)], axis=0)
    every = gather_columns(column, me)
    every = jnp.transpose(every.reshape(-1, cycles, width), (1, 0, 2))
    own = lax.dynamic_slice_in_dim(every, row_index * band_rows, band_rows, 2)
    col = lax.dynamic_slice_in_dim(every, col_index * band_cols, band_cols, 2)
    return finish(features[:, :width], every[0], own, col, gram_in, queries, diag, below, heads)


def solution(mesh):
    fits = mesh.shape["rows"] == 8 and mesh.shape["cols"] == 4
    return jax.shard_map(
        local if fits else general,
        mesh=mesh,
        in_specs=(
            P("rows", "cols"),
            P("rows", "cols"),
            P("rows", "cols"),
            P("rows", "cols"),
            P(),
            P("cols", None),
            P("rows"),
            P("rows", None),
            P(None, "rows", None, "cols"),
            P("cols", None, "rows"),
        ),
        out_specs=(P(None, "rows", None, "cols"), P("cols", None, "rows"), P("cols", "rows")),
        check_vma=False,
    )
```

```python
import functools
import jax
import jax.numpy as jnp
from jax import lax
from jax.experimental import pallas as pl
from jax.experimental.pallas import tpu as pltpu
from jax.sharding import PartitionSpec as P

highest = lax.Precision.HIGHEST
vmem_limit = 56 * 1024 * 1024
block = 128


def eliminate(rows):
    shape = (8, block)
    sub = lax.broadcasted_iota(jnp.int32, shape, 0)
    lane = lax.broadcasted_iota(jnp.int32, shape, 1)
    count = block // 8

    def row_of(x, k):
        return jnp.broadcast_to(x[k : k + 1, :], shape)

    for p in range(count):
        base = 8 * p
        inside = (lane >= base) & (lane < base + 8)

        def columns(q):
            return [jnp.broadcast_to(rows[q][:, base + k : base + k + 1], shape) for k in range(8)]

        cols = columns(p)
        own = jnp.where(inside, jnp.where(lane - base == sub, 1.0, 0.0), rows[p])
        heads, tops, scale = [], [], jnp.zeros(shape, jnp.float32)
        for k in range(0, 8, 2):
            a, b, d = row_of(cols[k], k), row_of(cols[k + 1], k), row_of(cols[k + 1], k + 1)
            det = a * d - b * b
            inverse = 1.0 / det
            single = 1.0 / a

            def solve(u, v):
                return (d * u - b * v) * inverse, (a * v - b * u) * inverse

            pairs = [solve(row_of(cols[j], k), row_of(cols[j], k + 1)) for j in range(k + 2, 8)]
            upper = row_of(own, k)
            top = solve(upper, row_of(own, k + 1))
            heads.append(pairs)
            tops.append(top)
            c0 = jnp.where(sub > k + 1, cols[k], 0.0)
            c1 = jnp.where(sub > k + 1, cols[k + 1], 0.0)
            for j in range(k + 2, 8):
                h0, h1 = pairs[j - k - 2]
                cols[j] = cols[j] - (c0 * h0 + c1 * h1)
            own = own - (c0 * top[0] + c1 * top[1])
            own = own - jnp.where(sub == k + 1, b * single, 0.0) * upper
            scale = jnp.where(sub == k, lax.rsqrt(a), scale)
            scale = jnp.where(sub == k + 1, lax.rsqrt(det * single), scale)
        for q in range(p + 1, count):
            other = columns(q)
            value = jnp.where(inside, 0.0, rows[q])
            for k in range(0, 8, 2):
                for j in range(k + 2, 8):
                    h0, h1 = heads[k // 2][j - k - 2]
                    other[j] = other[j] - (other[k] * h0 + other[k + 1] * h1)
                top = tops[k // 2]
                value = value - (other[k] * top[0] + other[k + 1] * top[1])
            rows[q] = value
        rows[p] = jnp.where(lane < base + 8, own * scale, 0.0)
    return rows


def mm(a, b):
    return jnp.dot(a, b, precision=highest, preferred_element_type=jnp.float32)


def mm_t(a, b):
    return lax.dot_general(
        a, b, (((1,), (1,)), ((), ())), precision=highest, preferred_element_type=jnp.float32
    )


def three_way(x):
    high = x.astype(jnp.bfloat16)
    rest = x - high.astype(jnp.float32)
    mid = rest.astype(jnp.bfloat16)
    return high, mid, (rest - mid.astype(jnp.float32)).astype(jnp.bfloat16)


def pack_left(x):
    high, mid, low = three_way(x)
    return jnp.concatenate([high, high, mid, high, low, mid], axis=0)


def pack_right(x):
    high, mid, low = three_way(x)
    return jnp.concatenate([high, mid, high, low, high, mid], axis=0)


def outer_sum(left, right):
    return lax.dot_general(
        left, right, (((0,), (0,)), ((), ())), preferred_element_type=jnp.float32
    )


def spans(start, stop, step):
    return [slice(at, min(at + step, stop)) for at in range(start, stop, step)]


def factor(work_ref, inv_ref, upper_ref, root_ref):
    total, width = work_ref.shape
    blocks = width // block
    chunk = 4 * block
    eye = lax.broadcasted_iota(jnp.int32, (block, block), 0) == lax.broadcasted_iota(
        jnp.int32, (block, block), 1
    )
    across, along = [], []
    for here in spans(0, width, block):
        diagonal = jnp.where(eye, work_ref[here, here], 0.0)
        across.append(lax.rsqrt(jnp.sum(diagonal, axis=0, keepdims=True)))
        down = jnp.sum(diagonal, axis=1, keepdims=True)
        along.append(lax.rsqrt(down))
        root_ref[here, :] = jnp.broadcast_to(down * along[-1], (block, block))
    across = jnp.concatenate(across, axis=1)
    for i, here in enumerate(spans(0, width, block)):
        work_ref[here, :] = work_ref[here, :] * along[i] * across
    for here in spans(width, total, block):
        work_ref[here, :] = work_ref[here, :] * across

    def one(b, carry):
        off = pl.multiple_of(b * block, block)
        rows = [
            work_ref[pl.ds(pl.multiple_of(off + 8 * q, 8), 8), pl.ds(off, block)]
            for q in range(block // 8)
        ]
        rows = eliminate(rows)
        for q in range(block // 8):
            inv_ref[8 * q : 8 * q + 8, :] = rows[q]
        for s in range(blocks):

            @pl.when(b == s)
            def _():
                here = slice(s * block, (s + 1) * block)
                after = slice((s + 1) * block, width)
                half = s % 2
                kept = slice(half * block, (half + 1) * block)
                inv = inv_ref[...]
                if s + 1 < blocks:
                    upper_ref[kept, after] = mm(inv, work_ref[here, after])
                for these in spans(s * block, total, chunk):
                    work_ref[these, here] = mm_t(work_ref[these, here], inv)
                if half == 0 and s + 1 < blocks:
                    near = slice((s + 1) * block, (s + 2) * block)
                    far = slice((s + 2) * block, width)
                    for these in spans((s + 1) * block, total, chunk):
                        work_ref[these, near] = work_ref[these, near] - mm(
                            work_ref[these, here], upper_ref[kept, near]
                        )
                    if s + 2 < blocks:
                        work_ref[near, far] = work_ref[near, far] - mm(
                            work_ref[near, here], upper_ref[kept, far]
                        )
                elif s + 1 < blocks:
                    both = slice((s - 1) * block, (s + 1) * block)
                    for these in spans((s + 1) * block, total, chunk):
                        work_ref[these, after] = work_ref[these, after] - mm(
                            work_ref[these, both], upper_ref[:, after]
                        )

        return carry

    lax.fori_loop(0, blocks, one, 0)


def factor_scratch(total, width):
    return [
        pltpu.VMEM((total, width), jnp.float32),
        pltpu.VMEM((block, block), jnp.float32),
        pltpu.VMEM((2 * block, width), jnp.float32),
        pltpu.VMEM((width, block), jnp.float32),
    ]


def plain_kernel(rows_ref, out_ref, work_ref, inv_ref, upper_ref, root_ref):
    work_ref[...] = rows_ref[...]
    factor(work_ref, inv_ref, upper_ref, root_ref)
    width = work_ref.shape[1]
    out_ref[width:, :] = work_ref[width:, :]
    for here in spans(0, width, block):
        for there in spans(0, width, block):
            out_ref[here, there] = work_ref[here, there] * root_ref[here, :]


def plain_panel(rows):
    whole = pl.BlockSpec(memory_space=pltpu.VMEM)
    return pl.pallas_call(
        plain_kernel,
        out_shape=jax.ShapeDtypeStruct(rows.shape, jnp.float32),
        in_specs=[whole],
        out_specs=whole,
        scratch_shapes=factor_scratch(*rows.shape),
        compiler_params=pltpu.CompilerParams(vmem_limit_bytes=vmem_limit),
        name="plain_panel",
    )(rows)


def panel_kernel(
    share,
    seqs,
    spot_ref,
    d0_ref,
    d1_ref,
    b0_ref,
    b1_ref,
    near_ref,
    far_ref,
    head_ref,
    query_ref,
    part_ref,
    next_ref,
    score_ref,
    own_ref,
    work_ref,
    inv_ref,
    upper_ref,
    root_ref,
    feat_ref,
):
    total, width = work_ref.shape
    _, low, band = b0_ref.shape
    cycles = low // block + 1
    row, col = spot_ref[0], spot_ref[1]
    core = col % 2
    for far, (diag_ref, below_ref) in enumerate(((d0_ref, b0_ref), (d1_ref, b1_ref))):
        for half in range(2):
            there = 2 * half + (core + far) % 2
            lanes = pl.ds(pl.multiple_of(there * band, 128), band)
            work_ref[:width, lanes] = diag_ref[half]
            work_ref[width : width + low, lanes] = below_ref[half]
    for far, ref in enumerate((near_ref, far_ref)):
        side = (core + far) % 2
        for i in range(4):
            feat_ref[(i // 2) * 4 + 2 * side + i % 2] = ref[:, i * 128 : (i + 1) * 128]
    every = feat_ref.shape[1] // cycles
    first = [feat_ref[i, pl.ds(0, every, stride=cycles), :] for i in range(width // 128)]
    right = pack_right(jnp.concatenate(first, axis=1))
    for i, here in enumerate(spans(0, width, block)):
        work_ref[here, :] = work_ref[here, :] + outer_sum(pack_left(first[i]), right) * share
    for a in range(cycles):
        mine = feat_ref[row, pl.ds(a, every, stride=cycles), :]
        own_ref[a] = mine
        if a > 0:
            here = slice(width + (a - 1) * block, width + a * block)
            work_ref[here, :] = work_ref[here, :] + outer_sum(pack_left(mine), right) * share
    queries = head_ref.shape[0]
    top = width + low
    work_ref[top : top + queries, :] = head_ref[...]
    work_ref[top + queries :, :] = jnp.zeros((total - top - queries, width), jnp.float32)
    for i in range(width // 128):
        work_ref[top + queries : top + queries + seqs, i * 128 : (i + 1) * 128] = feat_ref[
            i, pl.ds(0, seqs, stride=cycles), :
        ]
    factor(work_ref, inv_ref, upper_ref, root_ref)
    lanes = pl.ds(pl.multiple_of(col * band, 128), band)
    rows = pl.ds(pl.multiple_of(row * block, block), block)
    mine = work_ref[rows, lanes] * jnp.concatenate([root_ref[rows, :]] * (band // block), axis=1)
    row_at = row * block + lax.broadcasted_iota(jnp.int32, mine.shape, 0)
    col_at = col * band + lax.broadcasted_iota(jnp.int32, mine.shape, 1)
    part_ref[:block, :] = jnp.where(col_at <= row_at, mine, 0.0)
    part_ref[block:, :] = work_ref[width:top, lanes]
    solved = work_ref[top : top + queries, :]
    product = mm_t(solved, work_ref[width:top, :])
    next_ref[pl.ds(0, queries, stride=cycles), :] = work_ref[
        top : top + queries, pl.ds(pl.multiple_of(row * block, block), block)
    ]
    for a in range(1, cycles):
        here = pl.ds(a, queries, stride=cycles)
        next_ref[here, :] = query_ref[here, :] - product[:, (a - 1) * block : a * block]
    score_ref[...] = mm_t(solved, work_ref[top + queries : top + queries + 8, :])[:, :seqs]


def panel(spot, diags, belows, near, far, heads, queries, seqs, share):
    _, low, band = belows[0].shape
    width = heads.shape[1]
    cycles = low // block + 1
    total = -(-(width + low + heads.shape[0] + 8) // block) * block
    whole = pl.BlockSpec(memory_space=pltpu.VMEM)
    return pl.pallas_call(
        functools.partial(panel_kernel, share, seqs),
        out_shape=[
            jax.ShapeDtypeStruct((cycles * block, band), jnp.float32),
            jax.ShapeDtypeStruct(queries.shape, jnp.float32),
            jax.ShapeDtypeStruct((heads.shape[0], seqs), jnp.float32),
            jax.ShapeDtypeStruct((cycles, near.shape[0] // cycles, block), jnp.float32),
        ],
        in_specs=[pl.BlockSpec(memory_space=pltpu.SMEM)] + [whole] * 8,
        out_specs=[whole] * 4,
        scratch_shapes=factor_scratch(total, width)
        + [pltpu.VMEM((width // 128, near.shape[0], 128), jnp.float32)],
        compiler_params=pltpu.CompilerParams(vmem_limit_bytes=vmem_limit),
        name="panel_factor",
    )(spot, *diags, *belows, near, far, heads, queries)


def gram_kernel(share, gram_ref, own_ref, col_ref, panel_ref, out_ref):
    steps, seqs, count = own_ref.shape
    cycles, lanes = col_ref.shape[0] // seqs, col_ref.shape[1]
    right = jnp.concatenate(
        [pack_right(col_ref[pl.ds(b, seqs, stride=cycles), :]) for b in range(cycles)], axis=1
    )
    for a in range(steps):
        base = a * count * cycles
        out_ref[pl.ds(base, count, stride=cycles), :] = panel_ref[a]
        update = outer_sum(pack_left(own_ref[a]), right) * share
        for b in range(1, cycles):
            here = pl.ds(base + b, count, stride=cycles)
            out_ref[here, :] = gram_ref[here, :] + update[:, b * lanes : (b + 1) * lanes]


def gram_update(gram_in, own, col, part, share):
    cycles, seqs, count = own.shape
    rows, width = col.shape
    lanes = 128
    steps = 2 if cycles % 2 == 0 else 1
    gram = gram_in.reshape(cycles * count * cycles, width)
    tall = pl.BlockSpec((steps * count * cycles, lanes), lambda v, a: (a, v))
    return pl.pallas_call(
        functools.partial(gram_kernel, share),
        out_shape=jax.ShapeDtypeStruct(gram.shape, jnp.float32),
        grid=(width // lanes, cycles // steps),
        in_specs=[
            tall,
            pl.BlockSpec((steps, seqs, count), lambda v, a: (a, 0, 0)),
            pl.BlockSpec((rows, lanes), lambda v, a: (0, v)),
            pl.BlockSpec((steps, count, lanes), lambda v, a: (a, 0, v)),
        ],
        out_specs=tall,
        compiler_params=pltpu.CompilerParams(vmem_limit_bytes=vmem_limit),
        name="gram_update",
    )(gram, own, col, part.reshape(cycles, count, width)).reshape(gram_in.shape)


def sequence_features(proj_inner, proj_outer, lengths, loss_mask):
    seq_count, window = loss_mask.shape
    positions = jnp.arange(window, dtype=jnp.int32)
    token_live = (positions[None, :] >= (window - lengths)[:, None]).astype(
        jnp.float32
    ) * loss_mask.astype(jnp.float32)
    weighted = proj_inner.reshape(seq_count, window, -1) * token_live[:, :, None]
    features = jnp.einsum(
        "stk,stl->skl",
        weighted,
        proj_outer.reshape(seq_count, window, -1),
        precision=highest,
    )
    return features.reshape(seq_count, -1)


def general(
    tokens,
    cotangent,
    gate_weight,
    down_weight,
    proj_in,
    proj_out,
    lengths,
    loss_mask,
    gram_in,
    queries,
):
    row_index, col_index = lax.axis_index("rows"), lax.axis_index("cols")
    full_tokens = lax.all_gather(tokens, "cols", axis=1, tiled=True)
    full_cotangent = lax.all_gather(cotangent, "cols", axis=1, tiled=True)
    gate_pre = jnp.dot(
        full_tokens,
        lax.all_gather(gate_weight, "rows", axis=0, tiled=True),
        preferred_element_type=jnp.float32,
    )
    grad_hidden = jnp.dot(
        full_cotangent,
        lax.all_gather(down_weight, "rows", axis=0, tiled=True),
        preferred_element_type=jnp.float32,
    )
    grad_up = (grad_hidden * jax.nn.silu(gate_pre)).astype(jnp.bfloat16)
    outer_part = jnp.dot(grad_up, proj_out, preferred_element_type=jnp.float32)
    proj_inner = jnp.dot(full_tokens, proj_in, preferred_element_type=jnp.float32)
    proj_outer = lax.psum(outer_part, "cols")
    features = sequence_features(proj_inner, proj_outer, lengths, loss_mask)
    cycles, band_rows, _, band_cols = gram_in.shape
    every = lax.all_gather(features, "rows", axis=0, tiled=True)
    every = jnp.transpose(every.reshape(every.shape[0], cycles, -1), (1, 0, 2))
    own = lax.dynamic_slice_in_dim(every, row_index * band_rows, band_rows, 2)
    col = lax.dynamic_slice_in_dim(every, col_index * band_cols, band_cols, 2)
    panel_rows = lax.all_gather(gram_in[:, :, 0, :], "cols", axis=2, tiled=True)
    width = panel_rows.shape[2]
    diag = lax.all_gather(panel_rows[0], "rows", axis=0, tiled=True)
    heads = lax.all_gather(queries[:, 0, :], "rows", axis=1, tiled=True)
    below = panel_rows[1:].reshape((cycles - 1) * band_rows, width)
    share = 1.0 / every.shape[1]
    seqs, low, query_count = features.shape[0], below.shape[0], queries.shape[0]
    first = every[0]
    update = jnp.einsum("sr,sc->rc", first, first, precision=highest) * share
    more = jnp.einsum("asr,sc->arc", own[1:], first, precision=highest) * share
    used = width + low + query_count + seqs
    rows = [diag + update, below + more.reshape(low, width), heads, features[:, :width]]
    rows.append(jnp.zeros((-used % block, width), jnp.float32))
    done = plain_panel(jnp.concatenate(rows, axis=0))
    mine = lax.dynamic_slice_in_dim(done, row_index * band_rows, band_rows, 0)
    row_at = row_index * band_rows + lax.broadcasted_iota(jnp.int32, mine.shape, 0)
    mine = jnp.where(lax.broadcasted_iota(jnp.int32, mine.shape, 1) <= row_at, mine, 0.0)
    lower_part = done[width : width + low]
    solved = done[width + low : width + low + query_count]
    whitened = done[width + low + query_count : used]
    part = jnp.concatenate([mine, lower_part], axis=0)
    part = lax.dynamic_slice_in_dim(part, col_index * band_cols, band_cols, 1)
    updated = gram_in + jnp.einsum("asu,bsv->aubv", own, col, precision=highest) * share
    gram_next = updated.at[:, :, 0, :].set(part.reshape(cycles, band_rows, band_cols))
    tail = queries[:, 1:, :] - mm_t(solved, lower_part).reshape(query_count, cycles - 1, band_rows)
    own_head = lax.dynamic_slice_in_dim(solved, row_index * band_rows, band_rows, 1)
    query_next = jnp.concatenate([own_head[:, None, :], tail], axis=1)
    return gram_next, query_next, mm_t(solved, whitened)


sizes = {"z": 4, "x": 2, "y": 2, "core": 2}


def shift(value, axis, step, wrap=True, steps=None):
    names = ("z", "x", "y", "core")
    pairs = []
    for source in range(sizes["z"] * sizes["x"] * sizes["y"] * sizes["core"]):
        rest, at = source, []
        for name in reversed(names):
            at.append(rest % sizes[name])
            rest //= sizes[name]
        at = at[::-1]
        which = names.index(axis)
        there = at[which] + step
        if steps is not None:
            there = steps[at[which]]
        if wrap:
            there %= sizes[axis]
        elif not 0 <= there < sizes[axis]:
            continue
        at[which] = there
        target = 0
        for name, spot in zip(names, at):
            target = target * sizes[name] + spot
        pairs.append((source, target))
    return lax.ppermute(value, ("rows", "cols"), pairs)


slot_of = (((0, 3, 2, 1), (0, 2, 3, 1), (0, 1, 3, 2), (0, 1, 2, 3)))


def gradient_kernel(spot_ref, *refs):
    token_refs, refs = refs[:11], refs[11:]
    weight_refs, refs = refs[:8], refs[8:]
    out_proj_ref, in_proj_ref, outer_ref, inner_ref, token_buf, weight_buf, token_sem, weight_sem = refs
    z, x, y, core = (spot_ref[i] for i in range(4))
    height, band = token_refs[0].shape[1:]
    near, (far_1, far_2, far_3) = token_refs[:8], token_refs[8:]
    far = [far_1.at[i] for i in range(4)] + [far_2.at[i] for i in range(3)] + [far_3]
    depth = weight_refs[0].shape[2]
    weight_copies = []
    for i, ref in enumerate(weight_refs):
        row = ((z - i // 2) % 4) * 2 + (x + i % 2) % 2
        there = weight_buf.at[:, :, pl.ds(pl.multiple_of(row * depth, 128), depth)]
        weight_copies.append(pltpu.make_async_copy(ref, there, weight_sem.at[i]))
    token_copies = []
    for i in range(16):
        ref = (far if i % 2 else near)[i // 2]
        col = ((y + i % 4 // 2) % 2) * 2 + (core + i % 2) % 2
        there = token_buf.at[i // 4, :, :, pl.ds(pl.multiple_of(col * band, 128), band)]
        token_copies.append(pltpu.make_async_copy(ref, there, token_sem.at[i]))
    for copy in weight_copies + token_copies:
        copy.start()
    for copy in weight_copies:
        copy.wait()
    for s in range(4):
        for copy in token_copies[4 * s : 4 * s + 4]:
            copy.wait()
        if s == 0:
            inner_ref[...] = jnp.dot(
                token_buf[0, 0], in_proj_ref[...], preferred_element_type=jnp.float32
            )
        over = (((1,), (1,)), ((), ()))
        gate = lax.dot_general(
            token_buf[s, 0], weight_buf[0], over, preferred_element_type=jnp.float32
        )
        hidden = lax.dot_general(
            token_buf[s, 1], weight_buf[1], over, preferred_element_type=jnp.float32
        )
        grad = (hidden * (gate / (1.0 + jnp.exp(-gate)))).astype(jnp.bfloat16)
        outer_ref[s] = jnp.dot(grad, out_proj_ref[...], preferred_element_type=jnp.float32)


def gradient(spot, tokens, weights, out_proj, in_proj):
    kinds, height, band = tokens[0].shape
    share, depth = weights[0].shape[1:]
    full = depth * 8
    hbm = pl.BlockSpec(memory_space=pl.ANY)
    whole = pl.BlockSpec(memory_space=pltpu.VMEM)
    return pl.pallas_call(
        gradient_kernel,
        out_shape=[
            jax.ShapeDtypeStruct((4, height, out_proj.shape[1]), jnp.float32),
            jax.ShapeDtypeStruct((height, in_proj.shape[1]), jnp.float32),
        ],
        in_specs=[pl.BlockSpec(memory_space=pltpu.SMEM)] + [hbm] * 19 + [whole] * 2,
        out_specs=[whole] * 2,
        scratch_shapes=[
            pltpu.VMEM((4, kinds, height, full), jnp.bfloat16),
            pltpu.VMEM((kinds, share, full), jnp.bfloat16),
            pltpu.SemaphoreType.DMA((16,)),
            pltpu.SemaphoreType.DMA((8,)),
        ],
        compiler_params=pltpu.CompilerParams(vmem_limit_bytes=vmem_limit),
        cost_estimate=pl.CostEstimate(
            flops=16 * kinds * height * full * share,
            bytes_accessed=2 * kinds * full * (4 * height + share),
            transcendentals=4 * height * share,
        ),
        name="gradient",
    )(spot, *tokens, *weights, out_proj, in_proj)


def tie(values, *after):
    count = len(values)
    return lax.optimization_barrier((*values, *after))[:count]


def rounds(tokens, cotangent, gate_weight, down_weight, gram_in, queries, me):
    z = me["z"]
    both = jnp.stack([tokens, cotangent])
    depth, width = gate_weight.shape
    share = width // 4
    cut = jnp.stack(
        [gate_weight.T.reshape(4, share, depth), down_weight.T.reshape(4, share, depth)], axis=1
    )
    piece = [lax.dynamic_index_in_dim(cut, (z + s) % 4, 0, False) for s in range(4)]
    cycles, band_rows, _, band_cols = gram_in.shape
    count = queries.shape[0]
    below = gram_in[1:, :, 0, :].reshape((cycles - 1) * band_rows, band_cols)
    small = jnp.concatenate([gram_in[0, :, 0, :], queries[:, 0, :].reshape(-1, band_cols)], axis=0)
    small = lax.all_gather(small, "rows", axis=0)
    over_y = [[0, 2], [1, 3]]
    belows = lax.all_gather(below, "cols", axis=0, axis_index_groups=over_y)
    diag = small[:, :band_rows].reshape(-1, band_cols)
    diags = lax.all_gather(diag, "cols", axis=0, axis_index_groups=over_y)
    heads = jnp.transpose(small[:, band_rows:].reshape(8, count, band_rows), (1, 0, 2))
    heads = heads.reshape(count, 8 * band_rows)

    up1, down1 = shift(both, "z", 1, False), shift(both, "z", -1, False)
    y_own = shift(both, "y", 1)
    wx0 = shift(piece[0], "x", 1)
    wz1 = shift(piece[1], "z", 1)
    up1, down1, wz1, y_own, wx0, p3 = tie((up1, down1, wz1, y_own, wx0, piece[3]))

    slot_a = jnp.where(z < 2, down1, up1)
    up2, down2 = shift(up1, "z", 1, False), shift(down1, "z", -1, False)
    y_a = shift(slot_a, "y", 1)
    wx1 = shift(wz1, "x", 1)
    wz3 = shift(p3, "z", 3)
    up2, down2, wz3, y_a, wx1, p2 = tie((up2, down2, wz3, y_a, wx1, piece[2]))

    slot_b = jnp.where(z == 0, down2, jnp.where(z == 1, up1, jnp.where(z == 2, down1, up2)))
    last = shift(jnp.where(z == 2, up2, down2), "z", 1, False, (-1, 0, 3, -1))
    y_b = shift(slot_b, "y", 1)
    wx3 = shift(wz3, "x", 1)
    wz2 = shift(p2, "z", 2)
    core_1 = shift(jnp.stack([both, y_own, slot_a, y_a]), "core", 1)
    last, wz2, y_b, wx3, core_1 = tie((last, wz2, y_b, wx3, core_1))

    slot_c = jnp.where(z == 0, last, jnp.where(z == 1, down2, jnp.where(z == 2, up2, last)))
    y_c = shift(slot_c, "y", 1)
    wx2 = shift(wz2, "x", 1)
    core_2 = shift(jnp.stack([slot_b, y_b, slot_c]), "core", 1)
    y_c, wx2, core_2, diags, belows = tie((y_c, wx2, core_2, diags, belows))
    core_3 = shift(y_c, "core", 1)
    diag_c = shift(diags, "core", 1)
    below_c = shift(belows, "core", 1)
    pieces = [both, y_own, slot_a, y_a, slot_b, y_b, slot_c, y_c, core_1, core_2, core_3]
    weights = [piece[0], wx0, wz1, wx1, wz2, wx2, wz3, wx3]
    diags, belows = [diags, diag_c], [belows, below_c]
    return pieces, weights, diags, belows, heads


def local(
    tokens,
    cotangent,
    gate_weight,
    down_weight,
    proj_in,
    proj_out,
    lengths,
    loss_mask,
    gram_in,
    queries,
):
    row_index, col_index = lax.axis_index("rows"), lax.axis_index("cols")
    me = {"z": row_index // 2, "x": row_index % 2, "y": col_index // 2, "core": col_index % 2}
    pieces, weights, diags, belows, heads = rounds(
        tokens, cotangent, gate_weight, down_weight, gram_in, queries, me
    )
    share = weights[0].shape[1]
    out_proj = lax.dynamic_slice_in_dim(proj_out, me["z"] * share, share, 0)
    spot = jnp.stack([me["z"], me["x"], me["y"], me["core"]]).astype(jnp.int32)
    outer, proj_inner = gradient(spot, pieces, weights, out_proj, proj_in)
    tied = tie((outer, *diags, *belows))
    outer, diags, belows = tied[0], tied[1:3], tied[3:5]
    proj_outer = outer[0]
    table = jnp.array(slot_of, jnp.int32)
    for s in range(1, 4):
        part = lax.dynamic_index_in_dim(outer, table[me["z"], s], 0, False)
        proj_outer = proj_outer + shift(part, "z", -s)
    proj_outer = proj_outer + shift(proj_outer, "y", 1)
    proj_outer = proj_outer + shift(proj_outer, "core", 1)
    features = sequence_features(proj_inner, proj_outer, lengths, loss_mask)
    cycles, band_rows, _, band_cols = gram_in.shape
    seqs = features.shape[0]
    features = features.reshape(seqs * cycles, -1)
    mine = [
        lax.dynamic_slice_in_dim(features, (2 * i + me["core"]) * band_cols, band_cols, 1)
        for i in range(2)
    ]
    mine = jnp.concatenate(mine, axis=1)
    pair = jnp.concatenate([mine, shift(mine, "x", 1)], axis=0)
    near = jnp.concatenate([pair] + [shift(pair, "z", s) for s in range(1, 4)], axis=0)
    far = shift(near, "core", 1)
    share = cycles / near.shape[0]
    where = jnp.stack([row_index, col_index]).astype(jnp.int32)
    part, query_next, scores, own = panel(
        where, diags, belows, near, far, heads, queries.reshape(-1, band_rows), seqs, share
    )
    col = lax.dynamic_slice_in_dim(near, me["y"] * band_cols, band_cols, 1)
    gram_next = gram_update(gram_in, own, col, part, share)
    return gram_next, query_next.reshape(queries.shape), scores


def solution(mesh):
    fits = mesh.shape["rows"] == 8 and mesh.shape["cols"] == 4
    return jax.shard_map(
        local if fits else general,
        mesh=mesh,
        in_specs=(
            P("rows", "cols"),
            P("rows", "cols"),
            P("rows", "cols"),
            P("rows", "cols"),
            P(),
            P("cols", None),
            P("rows"),
            P("rows", None),
            P(None, "rows", None, "cols"),
            P("cols", None, "rows"),
        ),
        out_specs=(P(None, "rows", None, "cols"), P("cols", None, "rows"), P("cols", "rows")),
        check_vma=False,
    )
```

```python
import functools
import jax
import jax.numpy as jnp
from jax import lax
from jax.experimental import pallas as pl
from jax.experimental.pallas import tpu as pltpu
from jax.sharding import PartitionSpec as P

highest = lax.Precision.HIGHEST
vmem_limit = 56 * 1024 * 1024
block = 128


def eliminate(rows):
    shape = (8, block)
    sub = lax.broadcasted_iota(jnp.int32, shape, 0)
    lane = lax.broadcasted_iota(jnp.int32, shape, 1)
    count = block // 8

    def row_of(x, k):
        return jnp.broadcast_to(x[k : k + 1, :], shape)

    for p in range(count):
        base = 8 * p
        inside = (lane >= base) & (lane < base + 8)

        def columns(q):
            return [jnp.broadcast_to(rows[q][:, base + k : base + k + 1], shape) for k in range(8)]

        cols = columns(p)
        own = jnp.where(inside, jnp.where(lane - base == sub, 1.0, 0.0), rows[p])
        heads, tops, scale = [], [], jnp.zeros(shape, jnp.float32)
        for k in range(0, 8, 2):
            a, b, d = row_of(cols[k], k), row_of(cols[k + 1], k), row_of(cols[k + 1], k + 1)
            det = a * d - b * b
            inverse = 1.0 / det
            single = 1.0 / a

            def solve(u, v):
                return (d * u - b * v) * inverse, (a * v - b * u) * inverse

            pairs = [solve(row_of(cols[j], k), row_of(cols[j], k + 1)) for j in range(k + 2, 8)]
            upper = row_of(own, k)
            top = solve(upper, row_of(own, k + 1))
            heads.append(pairs)
            tops.append(top)
            c0 = jnp.where(sub > k + 1, cols[k], 0.0)
            c1 = jnp.where(sub > k + 1, cols[k + 1], 0.0)
            for j in range(k + 2, 8):
                h0, h1 = pairs[j - k - 2]
                cols[j] = cols[j] - (c0 * h0 + c1 * h1)
            own = own - (c0 * top[0] + c1 * top[1])
            own = own - jnp.where(sub == k + 1, b * single, 0.0) * upper
            scale = jnp.where(sub == k, lax.rsqrt(a), scale)
            scale = jnp.where(sub == k + 1, lax.rsqrt(det * single), scale)
        for q in range(p + 1, count):
            other = columns(q)
            value = jnp.where(inside, 0.0, rows[q])
            for k in range(0, 8, 2):
                for j in range(k + 2, 8):
                    h0, h1 = heads[k // 2][j - k - 2]
                    other[j] = other[j] - (other[k] * h0 + other[k + 1] * h1)
                top = tops[k // 2]
                value = value - (other[k] * top[0] + other[k + 1] * top[1])
            rows[q] = value
        rows[p] = jnp.where(lane < base + 8, own * scale, 0.0)
    return rows


def mm(a, b):
    return jnp.dot(a, b, precision=highest, preferred_element_type=jnp.float32)


def mm_t(a, b):
    return lax.dot_general(
        a, b, (((1,), (1,)), ((), ())), precision=highest, preferred_element_type=jnp.float32
    )


def three_way(x):
    high = x.astype(jnp.bfloat16)
    rest = x - high.astype(jnp.float32)
    mid = rest.astype(jnp.bfloat16)
    return high, mid, (rest - mid.astype(jnp.float32)).astype(jnp.bfloat16)


def pack_left(x):
    high, mid, low = three_way(x)
    return jnp.concatenate([high, high, mid, high, low, mid], axis=0)


def pack_right(x):
    high, mid, low = three_way(x)
    return jnp.concatenate([high, mid, high, low, high, mid], axis=0)


def outer_sum(left, right):
    return lax.dot_general(
        left, right, (((0,), (0,)), ((), ())), preferred_element_type=jnp.float32
    )


def spans(start, stop, step):
    return [slice(at, min(at + step, stop)) for at in range(start, stop, step)]


def factor(work_ref, inv_ref, upper_ref, root_ref):
    total, width = work_ref.shape
    blocks = width // block
    chunk = 4 * block
    eye = lax.broadcasted_iota(jnp.int32, (block, block), 0) == lax.broadcasted_iota(
        jnp.int32, (block, block), 1
    )
    across, along = [], []
    for here in spans(0, width, block):
        diagonal = jnp.where(eye, work_ref[here, here], 0.0)
        across.append(lax.rsqrt(jnp.sum(diagonal, axis=0, keepdims=True)))
        down = jnp.sum(diagonal, axis=1, keepdims=True)
        along.append(lax.rsqrt(down))
        root_ref[here, :] = jnp.broadcast_to(down * along[-1], (block, block))
    across = jnp.concatenate(across, axis=1)
    for i, here in enumerate(spans(0, width, block)):
        work_ref[here, :] = work_ref[here, :] * along[i] * across
    for here in spans(width, total, block):
        work_ref[here, :] = work_ref[here, :] * across

    def one(b, carry):
        off = pl.multiple_of(b * block, block)
        rows = [
            work_ref[pl.ds(pl.multiple_of(off + 8 * q, 8), 8), pl.ds(off, block)]
            for q in range(block // 8)
        ]
        rows = eliminate(rows)
        for half in range(2):

            @pl.when(b % 2 == half)
            def _():
                kept = slice(half * block, (half + 1) * block)
                for q in range(block // 8):
                    at = half * block + 8 * q
                    inv_ref[at : at + 8, kept] = rows[q]

        for s in range(blocks):

            @pl.when(b == s)
            def _():
                half = s % 2
                here = slice(s * block, (s + 1) * block)
                kept = slice(half * block, (half + 1) * block)
                inv = inv_ref[kept, kept]
                work_ref[here, here] = mm_t(work_ref[here, here], inv)
                if half == 0:
                    near = slice((s + 1) * block, (s + 2) * block)
                    across = mm_t(work_ref[near, here], inv)
                    work_ref[near, here] = across
                    work_ref[near, near] = work_ref[near, near] - mm_t(across, across)
                    return
                both = slice((s - 1) * block, (s + 1) * block)
                after = slice((s + 1) * block, width)
                old = slice(0, block)
                across = work_ref[here, (s - 1) * block : s * block]
                inv_ref[kept, old] = -mm(inv, mm(across, inv_ref[old, old]))
                inv = inv_ref[...]
                if s + 1 < blocks:
                    upper_ref[:, after] = mm(inv, work_ref[both, after])
                for these in spans((s + 1) * block, total, chunk):
                    solved = mm_t(work_ref[these, both], inv)
                    work_ref[these, both] = solved
                    if s + 1 < blocks:
                        work_ref[these, after] = work_ref[these, after] - mm(
                            solved, upper_ref[:, after]
                        )

        return carry

    inv_ref[:block, block:] = jnp.zeros((block, block), jnp.float32)
    lax.fori_loop(0, blocks, one, 0)


def factor_scratch(total, width):
    return [
        pltpu.VMEM((total, width), jnp.float32),
        pltpu.VMEM((2 * block, 2 * block), jnp.float32),
        pltpu.VMEM((2 * block, width), jnp.float32),
        pltpu.VMEM((width, block), jnp.float32),
    ]


def plain_kernel(rows_ref, out_ref, work_ref, inv_ref, upper_ref, root_ref):
    work_ref[...] = rows_ref[...]
    factor(work_ref, inv_ref, upper_ref, root_ref)
    width = work_ref.shape[1]
    out_ref[width:, :] = work_ref[width:, :]
    for here in spans(0, width, block):
        for there in spans(0, width, block):
            out_ref[here, there] = work_ref[here, there] * root_ref[here, :]


def plain_panel(rows):
    whole = pl.BlockSpec(memory_space=pltpu.VMEM)
    return pl.pallas_call(
        plain_kernel,
        out_shape=jax.ShapeDtypeStruct(rows.shape, jnp.float32),
        in_specs=[whole],
        out_specs=whole,
        scratch_shapes=factor_scratch(*rows.shape),
        compiler_params=pltpu.CompilerParams(vmem_limit_bytes=vmem_limit),
        name="plain_panel",
    )(rows)


def band_of(row, k):
    z, x = row // 2, row % 2
    step = k // 2
    near = (z // 2) * 2 + (z + step % 2) % 2
    return ((near + 2 * (step // 2)) % 4) * 2 + (x + k % 2) % 2


def panel_kernel(
    share,
    seqs,
    spot_ref,
    d0_ref,
    d1_ref,
    d2_ref,
    d3_ref,
    b0_ref,
    b1_ref,
    b2_ref,
    b3_ref,
    near_ref,
    far_ref,
    head_ref,
    query_ref,
    part_ref,
    next_ref,
    score_ref,
    own_ref,
    work_ref,
    inv_ref,
    upper_ref,
    root_ref,
    feat_ref,
):
    total, width = work_ref.shape
    low, band = b0_ref.shape
    cycles = low // block + 1
    row, col = spot_ref[0], spot_ref[1]
    y, core = col // 2, col % 2
    queries = query_ref.shape[0] // cycles
    top = width + low
    diag_refs, below_refs = (d0_ref, d1_ref, d2_ref, d3_ref), (b0_ref, b1_ref, b2_ref, b3_ref)
    for i, (diag_ref, below_ref) in enumerate(zip(diag_refs, below_refs)):
        there = ((y + i // 2) % 2) * 2 + (core + i % 2) % 2
        lanes = pl.ds(pl.multiple_of(there * band, 128), band)
        work_ref[width:top, lanes] = below_ref[...]
        for k in range(8):
            at = band_of(row, k) * block
            work_ref[pl.ds(pl.multiple_of(at, block), block), lanes] = diag_ref[
                k * block : (k + 1) * block, :
            ]
    half = queries // 2
    for k in range(8):
        lanes = pl.ds(pl.multiple_of(band_of(row, k) * block, block), block)
        rows = slice(k * half, (k + 1) * half)
        work_ref[top : top + half, lanes] = head_ref[rows, :block]
        work_ref[top + half : top + queries, lanes] = head_ref[rows, block:]
    for far, ref in enumerate((near_ref, far_ref)):
        side = (core + far) % 2
        for i in range(4):
            feat_ref[(i // 2) * 4 + 2 * side + i % 2] = ref[:, i * 128 : (i + 1) * 128]
    every = feat_ref.shape[1] // cycles
    first = [feat_ref[i, pl.ds(0, every, stride=cycles), :] for i in range(width // 128)]
    right = pack_right(jnp.concatenate(first, axis=1))
    for i, here in enumerate(spans(0, width, block)):
        work_ref[here, :] = work_ref[here, :] + outer_sum(pack_left(first[i]), right) * share
    for a in range(cycles):
        mine = feat_ref[row, pl.ds(a, every, stride=cycles), :]
        own_ref[a] = mine
        if a > 0:
            here = slice(width + (a - 1) * block, width + a * block)
            work_ref[here, :] = work_ref[here, :] + outer_sum(pack_left(mine), right) * share
    work_ref[top + queries :, :] = jnp.zeros((total - top - queries, width), jnp.float32)
    for i in range(width // 128):
        work_ref[top + queries : top + queries + seqs, i * 128 : (i + 1) * 128] = feat_ref[
            i, pl.ds(0, seqs, stride=cycles), :
        ]
    factor(work_ref, inv_ref, upper_ref, root_ref)
    lanes = pl.ds(pl.multiple_of(col * band, 128), band)
    rows = pl.ds(pl.multiple_of(row * block, block), block)
    mine = work_ref[rows, lanes] * jnp.concatenate([root_ref[rows, :]] * (band // block), axis=1)
    row_at = row * block + lax.broadcasted_iota(jnp.int32, mine.shape, 0)
    col_at = col * band + lax.broadcasted_iota(jnp.int32, mine.shape, 1)
    part_ref[:block, :] = jnp.where(col_at <= row_at, mine, 0.0)
    part_ref[block:, :] = work_ref[width:top, lanes]
    solved = work_ref[top : top + queries, :]
    product = mm_t(solved, work_ref[width:top, :])
    next_ref[pl.ds(0, queries, stride=cycles), :] = work_ref[
        top : top + queries, pl.ds(pl.multiple_of(row * block, block), block)
    ]
    for a in range(1, cycles):
        here = pl.ds(a, queries, stride=cycles)
        next_ref[here, :] = query_ref[here, :] - product[:, (a - 1) * block : a * block]
    score_ref[...] = mm_t(solved, work_ref[top + queries : top + queries + 8, :])[:, :seqs]


def panel(spot, diags, belows, near, far, heads, queries, seqs, share):
    low, band = belows[0].shape
    width = diags[0].shape[0]
    cycles = low // block + 1
    count = queries.shape[0] // cycles
    total = -(-(width + low + count + 8) // block) * block
    whole = pl.BlockSpec(memory_space=pltpu.VMEM)
    return pl.pallas_call(
        functools.partial(panel_kernel, share, seqs),
        out_shape=[
            jax.ShapeDtypeStruct((cycles * block, band), jnp.float32),
            jax.ShapeDtypeStruct(queries.shape, jnp.float32),
            jax.ShapeDtypeStruct((count, seqs), jnp.float32),
            jax.ShapeDtypeStruct((cycles, near.shape[0] // cycles, block), jnp.float32),
        ],
        in_specs=[pl.BlockSpec(memory_space=pltpu.SMEM)] + [whole] * 12,
        out_specs=[whole] * 4,
        scratch_shapes=factor_scratch(total, width)
        + [pltpu.VMEM((width // 128, near.shape[0], 128), jnp.float32)],
        compiler_params=pltpu.CompilerParams(vmem_limit_bytes=vmem_limit),
        name="panel_factor",
    )(spot, *diags, *belows, near, far, heads, queries)


def gram_kernel(share, gram_ref, own_ref, col_ref, panel_ref, out_ref):
    steps, seqs, count = own_ref.shape
    cycles, lanes = col_ref.shape[0] // seqs, col_ref.shape[1]
    right = jnp.concatenate(
        [pack_right(col_ref[pl.ds(b, seqs, stride=cycles), :]) for b in range(cycles)], axis=1
    )
    for a in range(steps):
        base = a * count * cycles
        out_ref[pl.ds(base, count, stride=cycles), :] = panel_ref[a]
        update = outer_sum(pack_left(own_ref[a]), right) * share
        for b in range(1, cycles):
            here = pl.ds(base + b, count, stride=cycles)
            out_ref[here, :] = gram_ref[here, :] + update[:, b * lanes : (b + 1) * lanes]


def gram_update(gram_in, own, col, part, share):
    cycles, seqs, count = own.shape
    rows, width = col.shape
    lanes = 128
    steps = 2 if cycles % 2 == 0 else 1
    gram = gram_in.reshape(cycles * count * cycles, width)
    tall = pl.BlockSpec((steps * count * cycles, lanes), lambda v, a: (a, v))
    return pl.pallas_call(
        functools.partial(gram_kernel, share),
        out_shape=jax.ShapeDtypeStruct(gram.shape, jnp.float32),
        grid=(width // lanes, cycles // steps),
        in_specs=[
            tall,
            pl.BlockSpec((steps, seqs, count), lambda v, a: (a, 0, 0)),
            pl.BlockSpec((rows, lanes), lambda v, a: (0, v)),
            pl.BlockSpec((steps, count, lanes), lambda v, a: (a, 0, v)),
        ],
        out_specs=tall,
        compiler_params=pltpu.CompilerParams(vmem_limit_bytes=vmem_limit),
        name="gram_update",
    )(gram, own, col, part.reshape(cycles, count, width)).reshape(gram_in.shape)


def sequence_features(proj_inner, proj_outer, lengths, loss_mask):
    seq_count, window = loss_mask.shape
    positions = jnp.arange(window, dtype=jnp.int32)
    token_live = (positions[None, :] >= (window - lengths)[:, None]).astype(
        jnp.float32
    ) * loss_mask.astype(jnp.float32)
    weighted = proj_inner.reshape(seq_count, window, -1) * token_live[:, :, None]
    features = jnp.einsum(
        "stk,stl->skl",
        weighted,
        proj_outer.reshape(seq_count, window, -1),
        precision=highest,
    )
    return features.reshape(seq_count, -1)


def general(
    tokens,
    cotangent,
    gate_weight,
    down_weight,
    proj_in,
    proj_out,
    lengths,
    loss_mask,
    gram_in,
    queries,
):
    row_index, col_index = lax.axis_index("rows"), lax.axis_index("cols")
    full_tokens = lax.all_gather(tokens, "cols", axis=1, tiled=True)
    full_cotangent = lax.all_gather(cotangent, "cols", axis=1, tiled=True)
    gate_pre = jnp.dot(
        full_tokens,
        lax.all_gather(gate_weight, "rows", axis=0, tiled=True),
        preferred_element_type=jnp.float32,
    )
    grad_hidden = jnp.dot(
        full_cotangent,
        lax.all_gather(down_weight, "rows", axis=0, tiled=True),
        preferred_element_type=jnp.float32,
    )
    grad_up = (grad_hidden * jax.nn.silu(gate_pre)).astype(jnp.bfloat16)
    outer_part = jnp.dot(grad_up, proj_out, preferred_element_type=jnp.float32)
    proj_inner = jnp.dot(full_tokens, proj_in, preferred_element_type=jnp.float32)
    proj_outer = lax.psum(outer_part, "cols")
    features = sequence_features(proj_inner, proj_outer, lengths, loss_mask)
    cycles, band_rows, _, band_cols = gram_in.shape
    every = lax.all_gather(features, "rows", axis=0, tiled=True)
    every = jnp.transpose(every.reshape(every.shape[0], cycles, -1), (1, 0, 2))
    own = lax.dynamic_slice_in_dim(every, row_index * band_rows, band_rows, 2)
    col = lax.dynamic_slice_in_dim(every, col_index * band_cols, band_cols, 2)
    panel_rows = lax.all_gather(gram_in[:, :, 0, :], "cols", axis=2, tiled=True)
    width = panel_rows.shape[2]
    diag = lax.all_gather(panel_rows[0], "rows", axis=0, tiled=True)
    heads = lax.all_gather(queries[:, 0, :], "rows", axis=1, tiled=True)
    below = panel_rows[1:].reshape((cycles - 1) * band_rows, width)
    share = 1.0 / every.shape[1]
    seqs, low, query_count = features.shape[0], below.shape[0], queries.shape[0]
    first = every[0]
    update = jnp.einsum("sr,sc->rc", first, first, precision=highest) * share
    more = jnp.einsum("asr,sc->arc", own[1:], first, precision=highest) * share
    used = width + low + query_count + seqs
    rows = [diag + update, below + more.reshape(low, width), heads, features[:, :width]]
    rows.append(jnp.zeros((-used % block, width), jnp.float32))
    done = plain_panel(jnp.concatenate(rows, axis=0))
    mine = lax.dynamic_slice_in_dim(done, row_index * band_rows, band_rows, 0)
    row_at = row_index * band_rows + lax.broadcasted_iota(jnp.int32, mine.shape, 0)
    mine = jnp.where(lax.broadcasted_iota(jnp.int32, mine.shape, 1) <= row_at, mine, 0.0)
    lower_part = done[width : width + low]
    solved = done[width + low : width + low + query_count]
    whitened = done[width + low + query_count : used]
    part = jnp.concatenate([mine, lower_part], axis=0)
    part = lax.dynamic_slice_in_dim(part, col_index * band_cols, band_cols, 1)
    updated = gram_in + jnp.einsum("asu,bsv->aubv", own, col, precision=highest) * share
    gram_next = updated.at[:, :, 0, :].set(part.reshape(cycles, band_rows, band_cols))
    tail = queries[:, 1:, :] - mm_t(solved, lower_part).reshape(query_count, cycles - 1, band_rows)
    own_head = lax.dynamic_slice_in_dim(solved, row_index * band_rows, band_rows, 1)
    query_next = jnp.concatenate([own_head[:, None, :], tail], axis=1)
    return gram_next, query_next, mm_t(solved, whitened)


sizes = {"z": 4, "x": 2, "y": 2, "core": 2}


def shift(value, axis, step, wrap=True, steps=None):
    names = ("z", "x", "y", "core")
    pairs = []
    for source in range(sizes["z"] * sizes["x"] * sizes["y"] * sizes["core"]):
        rest, at = source, []
        for name in reversed(names):
            at.append(rest % sizes[name])
            rest //= sizes[name]
        at = at[::-1]
        if axis == "both":
            pairs.append((source, source ^ 3))
            continue
        which = names.index(axis)
        there = at[which] + step
        if steps is not None:
            there = steps[at[which]]
        if wrap:
            there %= sizes[axis]
        elif not 0 <= there < sizes[axis]:
            continue
        at[which] = there
        target = 0
        for name, spot in zip(names, at):
            target = target * sizes[name] + spot
        pairs.append((source, target))
    return lax.ppermute(value, ("rows", "cols"), pairs)


slot_of = (((0, 3, 2, 1), (0, 2, 3, 1), (0, 1, 3, 2), (0, 1, 2, 3)))


def gradient_kernel(spot_ref, *refs):
    token_refs, refs = refs[:13], refs[13:]
    weight_refs, refs = refs[:8], refs[8:]
    out_proj_ref, in_proj_ref, outer_ref, inner_ref, token_buf, weight_buf, token_sem, weight_sem = refs
    z, x, y, core = (spot_ref[i] for i in range(4))
    height, band = token_refs[0].shape[1:]
    near, group = token_refs[:8], token_refs[8]
    far = [group.at[i] for i in range(4)] + list(token_refs[9:])
    depth = weight_refs[0].shape[2]
    weight_copies = []
    for i, ref in enumerate(weight_refs):
        row = ((z - i // 2) % 4) * 2 + (x + i % 2) % 2
        there = weight_buf.at[:, :, pl.ds(pl.multiple_of(row * depth, 128), depth)]
        weight_copies.append(pltpu.make_async_copy(ref, there, weight_sem.at[i]))
    token_copies = []
    for i in range(16):
        ref = (far if i % 2 else near)[i // 2]
        col = ((y + i % 4 // 2) % 2) * 2 + (core + i % 2) % 2
        there = token_buf.at[i // 4, :, :, pl.ds(pl.multiple_of(col * band, 128), band)]
        token_copies.append(pltpu.make_async_copy(ref, there, token_sem.at[i]))
    for copy in weight_copies + token_copies:
        copy.start()
    for copy in weight_copies:
        copy.wait()
    for s in range(4):
        for copy in token_copies[4 * s : 4 * s + 4]:
            copy.wait()
        if s == 0:
            inner_ref[...] = jnp.dot(
                token_buf[0, 0], in_proj_ref[...], preferred_element_type=jnp.float32
            )
        over = (((1,), (1,)), ((), ()))
        gate = lax.dot_general(
            token_buf[s, 0], weight_buf[0], over, preferred_element_type=jnp.float32
        )
        hidden = lax.dot_general(
            token_buf[s, 1], weight_buf[1], over, preferred_element_type=jnp.float32
        )
        grad = (hidden * (gate / (1.0 + jnp.exp(-gate)))).astype(jnp.bfloat16)
        outer_ref[s] = jnp.dot(grad, out_proj_ref[...], preferred_element_type=jnp.float32)


def gradient(spot, tokens, weights, out_proj, in_proj):
    kinds, height, band = tokens[0].shape
    share, depth = weights[0].shape[1:]
    full = depth * 8
    hbm = pl.BlockSpec(memory_space=pl.ANY)
    whole = pl.BlockSpec(memory_space=pltpu.VMEM)
    return pl.pallas_call(
        gradient_kernel,
        out_shape=[
            jax.ShapeDtypeStruct((4, height, out_proj.shape[1]), jnp.float32),
            jax.ShapeDtypeStruct((height, in_proj.shape[1]), jnp.float32),
        ],
        in_specs=[pl.BlockSpec(memory_space=pltpu.SMEM)] + [hbm] * 21 + [whole] * 2,
        out_specs=[whole] * 2,
        scratch_shapes=[
            pltpu.VMEM((4, kinds, height, full), jnp.bfloat16),
            pltpu.VMEM((kinds, share, full), jnp.bfloat16),
            pltpu.SemaphoreType.DMA((16,)),
            pltpu.SemaphoreType.DMA((8,)),
        ],
        compiler_params=pltpu.CompilerParams(vmem_limit_bytes=vmem_limit),
        cost_estimate=pl.CostEstimate(
            flops=16 * kinds * height * full * share,
            bytes_accessed=2 * kinds * full * (4 * height + share),
            transcendentals=4 * height * share,
        ),
        name="gradient",
    )(spot, *tokens, *weights, out_proj, in_proj)


def tie(values, *after):
    count = len(values)
    return lax.optimization_barrier((*values, *after))[:count]


def rounds(tokens, cotangent, gate_weight, down_weight, gram_in, queries, me):
    z = me["z"]
    both = jnp.stack([tokens, cotangent])
    depth, width = gate_weight.shape
    share = width // 4
    cut = jnp.stack(
        [gate_weight.T.reshape(4, share, depth), down_weight.T.reshape(4, share, depth)], axis=1
    )
    piece = [lax.dynamic_index_in_dim(cut, (z + s) % 4, 0, False) for s in range(4)]
    cycles, band_rows, _, band_cols = gram_in.shape
    count = queries.shape[0]
    below = gram_in[1:, :, 0, :].reshape((cycles - 1) * band_rows, band_cols)
    head = queries[:, 0, :]
    head = jnp.concatenate([head[: count // 2], head[count // 2 :]], axis=1)
    small = jnp.concatenate([gram_in[0, :, 0, :], head], axis=0)

    up1, down1 = shift(both, "z", 1, False), shift(both, "z", -1, False)
    y_own = shift(both, "y", 1)
    wx0 = shift(piece[0], "x", 1)
    wz1 = shift(piece[1], "z", 1)
    up1, down1, wz1, y_own, wx0, p3 = tie((up1, down1, wz1, y_own, wx0, piece[3]))

    slot_a = jnp.where(z < 2, down1, up1)
    up2, down2 = shift(up1, "z", 1, False), shift(down1, "z", -1, False)
    y_a = shift(slot_a, "y", 1)
    wx1 = shift(wz1, "x", 1)
    wz3 = shift(p3, "z", 3)
    up2, down2, wz3, y_a, wx1, p2 = tie((up2, down2, wz3, y_a, wx1, piece[2]))

    slot_b = jnp.where(z == 0, down2, jnp.where(z == 1, up1, jnp.where(z == 2, down1, up2)))
    last = shift(jnp.where(z == 2, up2, down2), "z", 1, False, (-1, 0, 3, -1))
    y_b = shift(slot_b, "y", 1)
    wx3 = shift(wz3, "x", 1)
    wz2 = shift(p2, "z", 2)
    below_y = shift(below, "y", 1)
    group = jnp.stack([both, y_own, slot_a, y_a])
    last, wz2, y_b, wx3, below_y, group, small = tie(
        (last, wz2, y_b, wx3, below_y, group, small)
    )

    slot_c = jnp.where(z == 0, last, jnp.where(z == 1, down2, jnp.where(z == 2, up2, last)))
    y_c = shift(slot_c, "y", 1)
    wx2 = shift(wz2, "x", 1)
    core_1 = shift(group, "core", 1)
    small = jnp.concatenate([small, shift(small, "z", 0, False, (1, 0, 3, 2))], axis=0)
    small = jnp.concatenate([small, shift(small, "z", 0, False, (2, 3, 0, 1))], axis=0)
    c_b = shift(slot_b, "core", 1)
    y_c, wx2, core_1, c_b, small = tie((y_c, wx2, core_1, c_b, small))

    cy_b = shift(y_b, "core", 1)
    c_c = shift(slot_c, "core", 1)
    cy_c = shift(y_c, "core", 1)
    cy_b, c_c, cy_c, small, below, below_y = tie((cy_b, c_c, cy_c, small, below, below_y))
    across = shift(small, "x", 1)
    below_c = shift(below, "core", 1)
    below_cy = shift(below_y, "core", 1)
    belows = [below, below_c, below_y, below_cy]
    pieces = [both, y_own, slot_a, y_a, slot_b, y_b, slot_c, y_c, core_1, c_b, cy_b, c_c, cy_c]
    weights = [piece[0], wx0, wz1, wx1, wz2, wx2, wz3, wx3]
    return pieces, weights, small, across, belows


def local(
    tokens,
    cotangent,
    gate_weight,
    down_weight,
    proj_in,
    proj_out,
    lengths,
    loss_mask,
    gram_in,
    queries,
):
    row_index, col_index = lax.axis_index("rows"), lax.axis_index("cols")
    me = {"z": row_index // 2, "x": row_index % 2, "y": col_index // 2, "core": col_index % 2}
    pieces, weights, small, across, belows = rounds(
        tokens, cotangent, gate_weight, down_weight, gram_in, queries, me
    )
    share = weights[0].shape[1]
    out_proj = lax.dynamic_slice_in_dim(proj_out, me["z"] * share, share, 0)
    spot = jnp.stack([me["z"], me["x"], me["y"], me["core"]]).astype(jnp.int32)
    outer, proj_inner = gradient(spot, pieces, weights, out_proj, proj_in)
    tied = tie((outer, small, across, *belows))
    outer, small, across, belows = tied[0], tied[1], tied[2], tied[3:]
    band_rows, count = gram_in.shape[1], queries.shape[0]
    rows = band_rows + count // 2
    parts = [side[i * rows : (i + 1) * rows] for i in range(4) for side in (small, across)]
    diag = jnp.concatenate([part[:band_rows] for part in parts], axis=0)
    heads = jnp.concatenate([part[band_rows:] for part in parts], axis=0)
    diag_y = shift(diag, "y", 1)
    proj_outer = outer[0]
    table = jnp.array(slot_of, jnp.int32)
    for s in range(1, 4):
        part = lax.dynamic_index_in_dim(outer, table[me["z"], s], 0, False)
        proj_outer = proj_outer + shift(part, "z", -s)
    over_y, over_core = shift(proj_outer, "y", 1), shift(proj_outer, "core", 1)
    proj_outer = (proj_outer + over_core) + (over_y + shift(proj_outer, "both", 1))
    features = sequence_features(proj_inner, proj_outer, lengths, loss_mask)
    cycles, band_rows, _, band_cols = gram_in.shape
    seqs = features.shape[0]
    features = features.reshape(seqs * cycles, -1)
    mine = [
        lax.dynamic_slice_in_dim(features, (2 * i + me["core"]) * band_cols, band_cols, 1)
        for i in range(2)
    ]
    mine = jnp.concatenate(mine, axis=1)
    pair = jnp.concatenate([mine, shift(mine, "x", 1)], axis=0)
    diag, diag_y, pair = tie((diag, diag_y, pair))
    diags = [diag, shift(diag, "core", 1), diag_y, shift(diag_y, "core", 1)]
    near = jnp.concatenate([pair] + [shift(pair, "z", s) for s in range(1, 4)], axis=0)
    far = shift(near, "core", 1)
    share = cycles / near.shape[0]
    where = jnp.stack([row_index, col_index]).astype(jnp.int32)
    part, query_next, scores, own = panel(
        where, diags, belows, near, far, heads, queries.reshape(-1, band_rows), seqs, share
    )
    col = lax.dynamic_slice_in_dim(near, me["y"] * band_cols, band_cols, 1)
    gram_next = gram_update(gram_in, own, col, part, share)
    return gram_next, query_next.reshape(queries.shape), scores


def solution(mesh):
    fits = mesh.shape["rows"] == 8 and mesh.shape["cols"] == 4
    return jax.shard_map(
        local if fits else general,
        mesh=mesh,
        in_specs=(
            P("rows", "cols"),
            P("rows", "cols"),
            P("rows", "cols"),
            P("rows", "cols"),
            P(),
            P("cols", None),
            P("rows"),
            P("rows", None),
            P(None, "rows", None, "cols"),
            P("cols", None, "rows"),
        ),
        out_specs=(P(None, "rows", None, "cols"), P("cols", None, "rows"), P("cols", "rows")),
        check_vma=False,
    )
```

```python
import functools
import jax
import jax.numpy as jnp
from jax import lax
from jax.experimental import pallas as pl
from jax.experimental.pallas import tpu as pltpu
from jax.sharding import PartitionSpec as P

highest = lax.Precision.HIGHEST
vmem_limit = 56 * 1024 * 1024
block = 128


def eliminate(rows):
    shape = (8, block)
    sub = lax.broadcasted_iota(jnp.int32, shape, 0)
    lane = lax.broadcasted_iota(jnp.int32, shape, 1)
    count = block // 8

    def row_of(x, k):
        return jnp.broadcast_to(x[k : k + 1, :], shape)

    for p in range(count):
        base = 8 * p
        inside = (lane >= base) & (lane < base + 8)

        def columns(q):
            return [jnp.broadcast_to(rows[q][:, base + k : base + k + 1], shape) for k in range(8)]

        cols = columns(p)
        own = jnp.where(inside, jnp.where(lane - base == sub, 1.0, 0.0), rows[p])
        heads, tops, scale = [], [], jnp.zeros(shape, jnp.float32)
        for k in range(0, 8, 2):
            a, b, d = row_of(cols[k], k), row_of(cols[k + 1], k), row_of(cols[k + 1], k + 1)
            det = a * d - b * b
            inverse = 1.0 / det
            single = 1.0 / a

            def solve(u, v):
                return (d * u - b * v) * inverse, (a * v - b * u) * inverse

            pairs = [solve(row_of(cols[j], k), row_of(cols[j], k + 1)) for j in range(k + 2, 8)]
            upper = row_of(own, k)
            top = solve(upper, row_of(own, k + 1))
            heads.append(pairs)
            tops.append(top)
            c0 = jnp.where(sub > k + 1, cols[k], 0.0)
            c1 = jnp.where(sub > k + 1, cols[k + 1], 0.0)
            for j in range(k + 2, 8):
                h0, h1 = pairs[j - k - 2]
                cols[j] = cols[j] - (c0 * h0 + c1 * h1)
            own = own - (c0 * top[0] + c1 * top[1])
            own = own - jnp.where(sub == k + 1, b * single, 0.0) * upper
            scale = jnp.where(sub == k, lax.rsqrt(a), scale)
            scale = jnp.where(sub == k + 1, lax.rsqrt(det * single), scale)
        for q in range(p + 1, count):
            other = columns(q)
            value = jnp.where(inside, 0.0, rows[q])
            for k in range(0, 8, 2):
                for j in range(k + 2, 8):
                    h0, h1 = heads[k // 2][j - k - 2]
                    other[j] = other[j] - (other[k] * h0 + other[k + 1] * h1)
                top = tops[k // 2]
                value = value - (other[k] * top[0] + other[k + 1] * top[1])
            rows[q] = value
        rows[p] = jnp.where(lane < base + 8, own * scale, 0.0)
    return rows


def mm(a, b):
    return jnp.dot(a, b, precision=highest, preferred_element_type=jnp.float32)


def mm_t(a, b):
    return lax.dot_general(
        a, b, (((1,), (1,)), ((), ())), precision=highest, preferred_element_type=jnp.float32
    )


def three_way(x):
    high = x.astype(jnp.bfloat16)
    rest = x - high.astype(jnp.float32)
    mid = rest.astype(jnp.bfloat16)
    return high, mid, (rest - mid.astype(jnp.float32)).astype(jnp.bfloat16)


def pack_left(x):
    high, mid, low = three_way(x)
    return jnp.concatenate([high, high, mid, high, low, mid], axis=0)


def pack_right(x):
    high, mid, low = three_way(x)
    return jnp.concatenate([high, mid, high, low, high, mid], axis=0)


def outer_sum(left, right):
    return lax.dot_general(
        left, right, (((0,), (0,)), ((), ())), preferred_element_type=jnp.float32
    )


def spans(start, stop, step):
    return [slice(at, min(at + step, stop)) for at in range(start, stop, step)]


def factor(work_ref, inv_ref, upper_ref, root_ref, beside=None):
    total, width = work_ref.shape
    blocks = width // block
    chunk = 4 * block
    eye = lax.broadcasted_iota(jnp.int32, (block, block), 0) == lax.broadcasted_iota(
        jnp.int32, (block, block), 1
    )
    across, along = [], []
    for here in spans(0, width, block):
        diagonal = jnp.where(eye, work_ref[here, here], 0.0)
        across.append(lax.rsqrt(jnp.sum(diagonal, axis=0, keepdims=True)))
        down = jnp.sum(diagonal, axis=1, keepdims=True)
        along.append(lax.rsqrt(down))
        root_ref[here, :] = jnp.broadcast_to(down * along[-1], (block, block))
    across = jnp.concatenate(across, axis=1)
    for i, here in enumerate(spans(0, width, block)):
        work_ref[here, :] = work_ref[here, :] * along[i] * across
    for here in spans(width, total, block):
        work_ref[here, :] = work_ref[here, :] * across

    def one(b, carry):
        off = pl.multiple_of(b * block, block)
        rows = [
            work_ref[pl.ds(pl.multiple_of(off + 8 * q, 8), 8), pl.ds(off, block)]
            for q in range(block // 8)
        ]
        if beside is not None:
            beside(b)
        rows = eliminate(rows)
        for half in range(2):

            @pl.when(b % 2 == half)
            def _():
                kept = slice(half * block, (half + 1) * block)
                for q in range(block // 8):
                    at = half * block + 8 * q
                    inv_ref[at : at + 8, kept] = rows[q]

        for s in range(blocks):

            @pl.when(b == s)
            def _():
                half = s % 2
                here = slice(s * block, (s + 1) * block)
                kept = slice(half * block, (half + 1) * block)
                inv = inv_ref[kept, kept]
                work_ref[here, here] = mm_t(work_ref[here, here], inv)
                if half == 0:
                    near = slice((s + 1) * block, (s + 2) * block)
                    across = mm_t(work_ref[near, here], inv)
                    work_ref[near, here] = across
                    work_ref[near, near] = work_ref[near, near] - mm_t(across, across)
                    return
                both = slice((s - 1) * block, (s + 1) * block)
                after = slice((s + 1) * block, width)
                old = slice(0, block)
                across = work_ref[here, (s - 1) * block : s * block]
                inv_ref[kept, old] = -mm(inv, mm(across, inv_ref[old, old]))
                inv = inv_ref[...]
                if s + 1 < blocks:
                    upper_ref[:, after] = mm(inv, work_ref[both, after])
                for these in spans((s + 1) * block, total, chunk):
                    solved = mm_t(work_ref[these, both], inv)
                    work_ref[these, both] = solved
                    if s + 1 < blocks:
                        work_ref[these, after] = work_ref[these, after] - mm(
                            solved, upper_ref[:, after]
                        )

        return carry

    inv_ref[:block, block:] = jnp.zeros((block, block), jnp.float32)
    lax.fori_loop(0, blocks, one, 0)


def factor_scratch(total, width):
    return [
        pltpu.VMEM((total, width), jnp.float32),
        pltpu.VMEM((2 * block, 2 * block), jnp.float32),
        pltpu.VMEM((2 * block, width), jnp.float32),
        pltpu.VMEM((width, block), jnp.float32),
    ]


def plain_kernel(rows_ref, out_ref, work_ref, inv_ref, upper_ref, root_ref):
    work_ref[...] = rows_ref[...]
    factor(work_ref, inv_ref, upper_ref, root_ref)
    width = work_ref.shape[1]
    out_ref[width:, :] = work_ref[width:, :]
    for here in spans(0, width, block):
        for there in spans(0, width, block):
            out_ref[here, there] = work_ref[here, there] * root_ref[here, :]


def plain_panel(rows):
    whole = pl.BlockSpec(memory_space=pltpu.VMEM)
    return pl.pallas_call(
        plain_kernel,
        out_shape=jax.ShapeDtypeStruct(rows.shape, jnp.float32),
        in_specs=[whole],
        out_specs=whole,
        scratch_shapes=factor_scratch(*rows.shape),
        compiler_params=pltpu.CompilerParams(vmem_limit_bytes=vmem_limit),
        name="plain_panel",
    )(rows)


def band_of(row, k):
    z, x = row // 2, row % 2
    step = k // 2
    near = (z // 2) * 2 + (z + step % 2) % 2
    return ((near + 2 * (step // 2)) % 4) * 2 + (x + k % 2) % 2


def panel_kernel(
    share,
    seqs,
    spot_ref,
    d0_ref,
    d1_ref,
    d2_ref,
    d3_ref,
    b0_ref,
    b1_ref,
    b2_ref,
    b3_ref,
    near_ref,
    far_ref,
    head_ref,
    query_ref,
    gram_ref,
    next_ref,
    score_ref,
    done_ref,
    work_ref,
    inv_ref,
    upper_ref,
    root_ref,
    feat_ref,
    slab_ref,
    left_ref,
    right_ref,
    slab_sem,
):
    total, width = work_ref.shape
    low, band = b0_ref.shape
    cycles = low // block + 1
    row, col = spot_ref[0], spot_ref[1]
    loads = []
    for h in range(band // block):
        there = gram_ref.at[:, h * block : (h + 1) * block]
        loads.append(pltpu.make_async_copy(there, slab_ref.at[h], slab_sem.at[h]))
    for copy in loads:
        copy.start()
    y, core = col // 2, col % 2
    queries = query_ref.shape[0] // cycles
    top = width + low
    diag_refs, below_refs = (d0_ref, d1_ref, d2_ref, d3_ref), (b0_ref, b1_ref, b2_ref, b3_ref)
    for i, (diag_ref, below_ref) in enumerate(zip(diag_refs, below_refs)):
        there = ((y + i // 2) % 2) * 2 + (core + i % 2) % 2
        lanes = pl.ds(pl.multiple_of(there * band, 128), band)
        work_ref[width:top, lanes] = below_ref[...]
        for k in range(8):
            at = band_of(row, k) * block
            work_ref[pl.ds(pl.multiple_of(at, block), block), lanes] = diag_ref[
                k * block : (k + 1) * block, :
            ]
    half = queries // 2
    for k in range(8):
        lanes = pl.ds(pl.multiple_of(band_of(row, k) * block, block), block)
        rows = slice(k * half, (k + 1) * half)
        work_ref[top : top + half, lanes] = head_ref[rows, :block]
        work_ref[top + half : top + queries, lanes] = head_ref[rows, block:]
    for far, ref in enumerate((near_ref, far_ref)):
        side = (core + far) % 2
        for i in range(4):
            feat_ref[(i // 2) * 4 + 2 * side + i % 2] = ref[:, i * 128 : (i + 1) * 128]
    every = feat_ref.shape[1] // cycles
    first = [feat_ref[i, pl.ds(0, every, stride=cycles), :] for i in range(width // 128)]
    right = pack_right(jnp.concatenate(first, axis=1))
    for i, here in enumerate(spans(0, width, block)):
        work_ref[here, :] = work_ref[here, :] + outer_sum(pack_left(first[i]), right) * share
    for a in range(cycles):
        mine = feat_ref[row, pl.ds(a, every, stride=cycles), :]
        left = pack_left(mine)
        left_ref[a] = left
        if a > 0:
            here = slice(width + (a - 1) * block, width + a * block)
            work_ref[here, :] = work_ref[here, :] + outer_sum(left, right) * share
    sides = band // block
    for h in range(sides):
        for k in range(cycles):
            other = feat_ref[sides * col + h, pl.ds(k, every, stride=cycles), :]
            at = (h * cycles + k) * block
            right_ref[:, at : at + block] = pack_right(other)
    for copy in loads:
        copy.wait()

    def beside(a):
        base = pl.multiple_of(a * block * cycles, block)
        for h in range(sides):
            across = slice(h * cycles * block, (h + 1) * cycles * block)
            update = outer_sum(left_ref[a], right_ref[:, across]) * share
            for k in range(1, cycles):
                here = pl.ds(base + k, block, stride=cycles)
                slab_ref[h, here, :] = (
                    slab_ref[h, here, :] + update[:, k * block : (k + 1) * block]
                )

    work_ref[top + queries :, :] = jnp.zeros((total - top - queries, width), jnp.float32)
    for i in range(width // 128):
        work_ref[top + queries : top + queries + seqs, i * 128 : (i + 1) * 128] = feat_ref[
            i, pl.ds(0, seqs, stride=cycles), :
        ]
    factor(work_ref, inv_ref, upper_ref, root_ref, beside)
    lanes = pl.ds(pl.multiple_of(col * band, 128), band)
    rows = pl.ds(pl.multiple_of(row * block, block), block)
    mine = work_ref[rows, lanes] * jnp.concatenate([root_ref[rows, :]] * (band // block), axis=1)
    row_at = row * block + lax.broadcasted_iota(jnp.int32, mine.shape, 0)
    col_at = col * band + lax.broadcasted_iota(jnp.int32, mine.shape, 1)
    mine = jnp.where(col_at <= row_at, mine, 0.0)
    stores = []
    for a in range(cycles):
        if a > 0:
            mine = work_ref[width + (a - 1) * block : width + a * block, lanes]
        for h in range(sides):
            here = pl.ds(a * block * cycles, block, stride=cycles)
            slab_ref[h, here, :] = mine[:, h * block : (h + 1) * block]
    for h in range(sides):
        there = done_ref.at[:, h * block : (h + 1) * block]
        stores.append(pltpu.make_async_copy(slab_ref.at[h], there, slab_sem.at[h]))
    for copy in stores:
        copy.start()
    solved = work_ref[top : top + queries, :]
    product = mm_t(solved, work_ref[width:top, :])
    next_ref[pl.ds(0, queries, stride=cycles), :] = work_ref[
        top : top + queries, pl.ds(pl.multiple_of(row * block, block), block)
    ]
    for a in range(1, cycles):
        here = pl.ds(a, queries, stride=cycles)
        next_ref[here, :] = query_ref[here, :] - product[:, (a - 1) * block : a * block]
    score_ref[...] = mm_t(solved, work_ref[top + queries : top + queries + 8, :])[:, :seqs]
    for copy in stores:
        copy.wait()


def panel(spot, diags, belows, near, far, heads, queries, gram, seqs, share):
    low, band = belows[0].shape
    width = diags[0].shape[0]
    cycles = low // block + 1
    count = queries.shape[0] // cycles
    total = -(-(width + low + count + 8) // block) * block
    whole = pl.BlockSpec(memory_space=pltpu.VMEM)
    return pl.pallas_call(
        functools.partial(panel_kernel, share, seqs),
        out_shape=[
            jax.ShapeDtypeStruct(queries.shape, jnp.float32),
            jax.ShapeDtypeStruct((count, seqs), jnp.float32),
            jax.ShapeDtypeStruct(gram.shape, jnp.float32),
        ],
        in_specs=[pl.BlockSpec(memory_space=pltpu.SMEM)] + [whole] * 12
        + [pl.BlockSpec(memory_space=pl.ANY)],
        out_specs=[whole] * 2 + [pl.BlockSpec(memory_space=pl.ANY)],
        scratch_shapes=factor_scratch(total, width)
        + [
            pltpu.VMEM((width // 128, near.shape[0], 128), jnp.float32),
            pltpu.VMEM((band // block, gram.shape[0], block), jnp.float32),
            pltpu.VMEM((cycles, 6 * near.shape[0] // cycles, block), jnp.bfloat16),
            pltpu.VMEM((6 * near.shape[0] // cycles, cycles * band), jnp.bfloat16),
            pltpu.SemaphoreType.DMA((band // block,)),
        ],
        compiler_params=pltpu.CompilerParams(vmem_limit_bytes=vmem_limit),
        name="panel_factor",
    )(spot, *diags, *belows, near, far, heads, queries, gram)


def sequence_features(proj_inner, proj_outer, lengths, loss_mask):
    seq_count, window = loss_mask.shape
    positions = jnp.arange(window, dtype=jnp.int32)
    token_live = (positions[None, :] >= (window - lengths)[:, None]).astype(
        jnp.float32
    ) * loss_mask.astype(jnp.float32)
    weighted = proj_inner.reshape(seq_count, window, -1) * token_live[:, :, None]
    features = jnp.einsum(
        "stk,stl->skl",
        weighted,
        proj_outer.reshape(seq_count, window, -1),
        precision=highest,
    )
    return features.reshape(seq_count, -1)


def general(
    tokens,
    cotangent,
    gate_weight,
    down_weight,
    proj_in,
    proj_out,
    lengths,
    loss_mask,
    gram_in,
    queries,
):
    row_index, col_index = lax.axis_index("rows"), lax.axis_index("cols")
    full_tokens = lax.all_gather(tokens, "cols", axis=1, tiled=True)
    full_cotangent = lax.all_gather(cotangent, "cols", axis=1, tiled=True)
    gate_pre = jnp.dot(
        full_tokens,
        lax.all_gather(gate_weight, "rows", axis=0, tiled=True),
        preferred_element_type=jnp.float32,
    )
    grad_hidden = jnp.dot(
        full_cotangent,
        lax.all_gather(down_weight, "rows", axis=0, tiled=True),
        preferred_element_type=jnp.float32,
    )
    grad_up = (grad_hidden * jax.nn.silu(gate_pre)).astype(jnp.bfloat16)
    outer_part = jnp.dot(grad_up, proj_out, preferred_element_type=jnp.float32)
    proj_inner = jnp.dot(full_tokens, proj_in, preferred_element_type=jnp.float32)
    proj_outer = lax.psum(outer_part, "cols")
    features = sequence_features(proj_inner, proj_outer, lengths, loss_mask)
    cycles, band_rows, _, band_cols = gram_in.shape
    every = lax.all_gather(features, "rows", axis=0, tiled=True)
    every = jnp.transpose(every.reshape(every.shape[0], cycles, -1), (1, 0, 2))
    own = lax.dynamic_slice_in_dim(every, row_index * band_rows, band_rows, 2)
    col = lax.dynamic_slice_in_dim(every, col_index * band_cols, band_cols, 2)
    panel_rows = lax.all_gather(gram_in[:, :, 0, :], "cols", axis=2, tiled=True)
    width = panel_rows.shape[2]
    diag = lax.all_gather(panel_rows[0], "rows", axis=0, tiled=True)
    heads = lax.all_gather(queries[:, 0, :], "rows", axis=1, tiled=True)
    below = panel_rows[1:].reshape((cycles - 1) * band_rows, width)
    share = 1.0 / every.shape[1]
    seqs, low, query_count = features.shape[0], below.shape[0], queries.shape[0]
    first = every[0]
    update = jnp.einsum("sr,sc->rc", first, first, precision=highest) * share
    more = jnp.einsum("asr,sc->arc", own[1:], first, precision=highest) * share
    used = width + low + query_count + seqs
    rows = [diag + update, below + more.reshape(low, width), heads, features[:, :width]]
    rows.append(jnp.zeros((-used % block, width), jnp.float32))
    done = plain_panel(jnp.concatenate(rows, axis=0))
    mine = lax.dynamic_slice_in_dim(done, row_index * band_rows, band_rows, 0)
    row_at = row_index * band_rows + lax.broadcasted_iota(jnp.int32, mine.shape, 0)
    mine = jnp.where(lax.broadcasted_iota(jnp.int32, mine.shape, 1) <= row_at, mine, 0.0)
    lower_part = done[width : width + low]
    solved = done[width + low : width + low + query_count]
    whitened = done[width + low + query_count : used]
    part = jnp.concatenate([mine, lower_part], axis=0)
    part = lax.dynamic_slice_in_dim(part, col_index * band_cols, band_cols, 1)
    updated = gram_in + jnp.einsum("asu,bsv->aubv", own, col, precision=highest) * share
    gram_next = updated.at[:, :, 0, :].set(part.reshape(cycles, band_rows, band_cols))
    tail = queries[:, 1:, :] - mm_t(solved, lower_part).reshape(query_count, cycles - 1, band_rows)
    own_head = lax.dynamic_slice_in_dim(solved, row_index * band_rows, band_rows, 1)
    query_next = jnp.concatenate([own_head[:, None, :], tail], axis=1)
    return gram_next, query_next, mm_t(solved, whitened)


sizes = {"z": 4, "x": 2, "y": 2, "core": 2}


def shift(value, axis, step, wrap=True, steps=None):
    names = ("z", "x", "y", "core")
    pairs = []
    for source in range(sizes["z"] * sizes["x"] * sizes["y"] * sizes["core"]):
        rest, at = source, []
        for name in reversed(names):
            at.append(rest % sizes[name])
            rest //= sizes[name]
        at = at[::-1]
        if axis == "both":
            pairs.append((source, source ^ 3))
            continue
        which = names.index(axis)
        there = at[which] + step
        if steps is not None:
            there = steps[at[which]]
        if wrap:
            there %= sizes[axis]
        elif not 0 <= there < sizes[axis]:
            continue
        at[which] = there
        target = 0
        for name, spot in zip(names, at):
            target = target * sizes[name] + spot
        pairs.append((source, target))
    return lax.ppermute(value, ("rows", "cols"), pairs)


slot_of = (((0, 3, 2, 1), (0, 2, 3, 1), (0, 1, 3, 2), (0, 1, 2, 3)))


def gradient_kernel(spot_ref, *refs):
    token_refs, refs = refs[:13], refs[13:]
    weight_refs, refs = refs[:8], refs[8:]
    out_proj_ref, in_proj_ref, outer_ref, inner_ref, token_buf, weight_buf, token_sem, weight_sem = refs
    z, x, y, core = (spot_ref[i] for i in range(4))
    height, band = token_refs[0].shape[1:]
    near, group = token_refs[:8], token_refs[8]
    far = [group.at[i] for i in range(4)] + list(token_refs[9:])
    depth = weight_refs[0].shape[2]
    weight_copies = []
    for i, ref in enumerate(weight_refs):
        row = ((z - i // 2) % 4) * 2 + (x + i % 2) % 2
        there = weight_buf.at[:, :, pl.ds(pl.multiple_of(row * depth, 128), depth)]
        weight_copies.append(pltpu.make_async_copy(ref, there, weight_sem.at[i]))
    token_copies = []
    for i in range(16):
        ref = (far if i % 2 else near)[i // 2]
        col = ((y + i % 4 // 2) % 2) * 2 + (core + i % 2) % 2
        slot = slice(i // 4 * height, (i // 4 + 1) * height)
        there = token_buf.at[:, slot, pl.ds(pl.multiple_of(col * band, 128), band)]
        token_copies.append(pltpu.make_async_copy(ref, there, token_sem.at[i]))
    for copy in weight_copies + token_copies:
        copy.start()
    for copy in weight_copies:
        copy.wait()
    for copy in token_copies:
        copy.wait()
    inner_ref[...] = jnp.dot(
        token_buf[0, :height], in_proj_ref[...], preferred_element_type=jnp.float32
    )
    over = (((1,), (1,)), ((), ()))
    gate = lax.dot_general(token_buf[0], weight_buf[0], over, preferred_element_type=jnp.float32)
    hidden = lax.dot_general(token_buf[1], weight_buf[1], over, preferred_element_type=jnp.float32)
    grad = (hidden * (gate / (1.0 + jnp.exp(-gate)))).astype(jnp.bfloat16)
    outer = jnp.dot(grad, out_proj_ref[...], preferred_element_type=jnp.float32)
    for s in range(4):
        outer_ref[s] = outer[s * height : (s + 1) * height]


def gradient(spot, tokens, weights, out_proj, in_proj):
    kinds, height, band = tokens[0].shape
    share, depth = weights[0].shape[1:]
    full = depth * 8
    hbm = pl.BlockSpec(memory_space=pl.ANY)
    whole = pl.BlockSpec(memory_space=pltpu.VMEM)
    return pl.pallas_call(
        gradient_kernel,
        out_shape=[
            jax.ShapeDtypeStruct((4, height, out_proj.shape[1]), jnp.float32),
            jax.ShapeDtypeStruct((height, in_proj.shape[1]), jnp.float32),
        ],
        in_specs=[pl.BlockSpec(memory_space=pltpu.SMEM)] + [hbm] * 21 + [whole] * 2,
        out_specs=[whole] * 2,
        scratch_shapes=[
            pltpu.VMEM((kinds, 4 * height, full), jnp.bfloat16),
            pltpu.VMEM((kinds, share, full), jnp.bfloat16),
            pltpu.SemaphoreType.DMA((16,)),
            pltpu.SemaphoreType.DMA((8,)),
        ],
        compiler_params=pltpu.CompilerParams(vmem_limit_bytes=vmem_limit),
        cost_estimate=pl.CostEstimate(
            flops=16 * kinds * height * full * share,
            bytes_accessed=2 * kinds * full * (4 * height + share),
            transcendentals=4 * height * share,
        ),
        name="gradient",
    )(spot, *tokens, *weights, out_proj, in_proj)


def tie(values, *after):
    count = len(values)
    return lax.optimization_barrier((*values, *after))[:count]


def rounds(tokens, cotangent, gate_weight, down_weight, gram_in, queries, me, early):
    z = me["z"]
    both = jnp.stack([tokens, cotangent])
    depth, width = gate_weight.shape
    share = width // 4
    cut = jnp.stack(
        [gate_weight.T.reshape(4, share, depth), down_weight.T.reshape(4, share, depth)], axis=1
    )
    piece = [lax.dynamic_index_in_dim(cut, (z + s) % 4, 0, False) for s in range(4)]
    cycles, band_rows, _, band_cols = gram_in.shape
    count = queries.shape[0]
    below = gram_in[1:, :, 0, :].reshape((cycles - 1) * band_rows, band_cols)
    head = queries[:, 0, :]
    head = jnp.concatenate([head[: count // 2], head[count // 2 :]], axis=1)
    small = jnp.concatenate([gram_in[0, :, 0, :], head], axis=0)

    up1, down1 = shift(both, "z", 1, False), shift(both, "z", -1, False)
    y_own = shift(both, "y", 1)
    wx0 = shift(piece[0], "x", 1)
    wz1 = shift(piece[1], "z", 1)
    up1, down1, wz1, y_own, wx0, p3 = tie((up1, down1, wz1, y_own, wx0, piece[3]))

    slot_a = jnp.where(z < 2, down1, up1)
    up2, down2 = shift(up1, "z", 1, False), shift(down1, "z", -1, False)
    y_a = shift(slot_a, "y", 1)
    wx1 = shift(wz1, "x", 1)
    wz3 = shift(p3, "z", 3)
    up2, down2, wz3, y_a, wx1, p2 = tie((up2, down2, wz3, y_a, wx1, piece[2]))

    slot_b = jnp.where(z == 0, down2, jnp.where(z == 1, up1, jnp.where(z == 2, down1, up2)))
    last = shift(jnp.where(z == 2, up2, down2), "z", 1, False, (-1, 0, 3, -1))
    y_b = shift(slot_b, "y", 1)
    wx3 = shift(wz3, "x", 1)
    wz2 = shift(p2, "z", 2)
    below_y = shift(below, "y", 1)
    group = jnp.stack([both, y_own, slot_a, y_a])
    last, wz2, y_b, wx3, below_y, group, small, *early = tie(
        (last, wz2, y_b, wx3, below_y, group, small, *early)
    )

    slot_c = jnp.where(z == 0, last, jnp.where(z == 1, down2, jnp.where(z == 2, up2, last)))
    y_c = shift(slot_c, "y", 1)
    wx2 = shift(wz2, "x", 1)
    core_1 = shift(group, "core", 1)
    small = jnp.concatenate([small, shift(small, "z", 0, False, (1, 0, 3, 2))], axis=0)
    small = jnp.concatenate([small, shift(small, "z", 0, False, (2, 3, 0, 1))], axis=0)
    c_b = shift(slot_b, "core", 1)
    y_c, wx2, core_1, c_b, small = tie((y_c, wx2, core_1, c_b, small))

    cy_b = shift(y_b, "core", 1)
    c_c = shift(slot_c, "core", 1)
    cy_c = shift(y_c, "core", 1)
    cy_b, c_c, cy_c, small, below, below_y = tie((cy_b, c_c, cy_c, small, below, below_y))
    across = shift(small, "x", 1)
    below_c = shift(below, "core", 1)
    below_cy = shift(below_y, "core", 1)
    belows = [below, below_c, below_y, below_cy]
    pieces = [both, y_own, slot_a, y_a, slot_b, y_b, slot_c, y_c, core_1, c_b, cy_b, c_c, cy_c]
    weights = [piece[0], wx0, wz1, wx1, wz2, wx2, wz3, wx3]
    return pieces, weights, small, across, belows, early


def local(
    tokens,
    cotangent,
    gate_weight,
    down_weight,
    proj_in,
    proj_out,
    lengths,
    loss_mask,
    gram_in,
    queries,
):
    row_index, col_index = lax.axis_index("rows"), lax.axis_index("cols")
    me = {"z": row_index // 2, "x": row_index % 2, "y": col_index // 2, "core": col_index % 2}
    share = gate_weight.shape[1] // 4
    out_proj = lax.dynamic_slice_in_dim(proj_out, me["z"] * share, share, 0)
    spot = jnp.stack([me["z"], me["x"], me["y"], me["core"]]).astype(jnp.int32)
    where = jnp.stack([row_index, col_index]).astype(jnp.int32)
    table = jnp.array(slot_of, jnp.int32)
    early = [spot, where, out_proj] + [table[me["z"], s] for s in range(1, 4)]
    pieces, weights, small, across, belows, early = rounds(
        tokens, cotangent, gate_weight, down_weight, gram_in, queries, me, early
    )
    spot, where, out_proj, *order = early
    outer, proj_inner = gradient(spot, pieces, weights, out_proj, proj_in)
    tied = tie((outer, small, across, *belows))
    outer, small, across, belows = tied[0], tied[1], tied[2], tied[3:]
    band_rows, count = gram_in.shape[1], queries.shape[0]
    rows = band_rows + count // 2
    parts = [side[i * rows : (i + 1) * rows] for i in range(4) for side in (small, across)]
    diag = jnp.concatenate([part[:band_rows] for part in parts], axis=0)
    heads = jnp.concatenate([part[band_rows:] for part in parts], axis=0)
    diag_y = shift(diag, "y", 1)
    proj_outer = outer[0]
    for s in range(1, 4):
        part = lax.dynamic_index_in_dim(outer, order[s - 1], 0, False)
        proj_outer = proj_outer + shift(part, "z", -s)
    over_y, over_core = shift(proj_outer, "y", 1), shift(proj_outer, "core", 1)
    proj_outer = (proj_outer + over_core) + (over_y + shift(proj_outer, "both", 1))
    features = sequence_features(proj_inner, proj_outer, lengths, loss_mask)
    cycles, band_rows, _, band_cols = gram_in.shape
    seqs = features.shape[0]
    features = features.reshape(seqs * cycles, -1)
    mine = [
        lax.dynamic_slice_in_dim(features, (2 * i + me["core"]) * band_cols, band_cols, 1)
        for i in range(2)
    ]
    mine = jnp.concatenate(mine, axis=1)
    pair = jnp.concatenate([mine, shift(mine, "x", 1)], axis=0)
    diag, diag_y, pair = tie((diag, diag_y, pair))
    diags = [diag, shift(diag, "core", 1), diag_y, shift(diag_y, "core", 1)]
    near = jnp.concatenate([pair] + [shift(pair, "z", s) for s in range(1, 4)], axis=0)
    far = shift(near, "core", 1)
    share = cycles / near.shape[0]
    query_next, scores, gram_next = panel(
        where,
        diags,
        belows,
        near,
        far,
        heads,
        queries.reshape(-1, band_rows),
        gram_in.reshape(-1, band_cols),
        seqs,
        share,
    )
    return gram_next.reshape(gram_in.shape), query_next.reshape(queries.shape), scores


def solution(mesh):
    fits = mesh.shape["rows"] == 8 and mesh.shape["cols"] == 4
    return jax.shard_map(
        local if fits else general,
        mesh=mesh,
        in_specs=(
            P("rows", "cols"),
            P("rows", "cols"),
            P("rows", "cols"),
            P("rows", "cols"),
            P(),
            P("cols", None),
            P("rows"),
            P("rows", None),
            P(None, "rows", None, "cols"),
            P("cols", None, "rows"),
        ),
        out_specs=(P(None, "rows", None, "cols"), P("cols", None, "rows"), P("cols", "rows")),
        check_vma=False,
    )
```

```python
import functools
import jax
import jax.numpy as jnp
from jax import lax
from jax.experimental import pallas as pl
from jax.experimental.pallas import tpu as pltpu
from jax.sharding import PartitionSpec as P

highest = lax.Precision.HIGHEST
vmem_limit = 56 * 1024 * 1024
block = 128


def eliminate(rows):
    shape = (8, block)
    sub = lax.broadcasted_iota(jnp.int32, shape, 0)
    lane = lax.broadcasted_iota(jnp.int32, shape, 1)
    count = block // 8

    def row_of(x, k):
        return jnp.broadcast_to(x[k : k + 1, :], shape)

    for p in range(count):
        base = 8 * p
        inside = (lane >= base) & (lane < base + 8)

        def columns(q):
            return [jnp.broadcast_to(rows[q][:, base + k : base + k + 1], shape) for k in range(8)]

        cols = columns(p)
        own = jnp.where(inside, jnp.where(lane - base == sub, 1.0, 0.0), rows[p])
        heads, tops, scale = [], [], jnp.zeros(shape, jnp.float32)
        for k in range(0, 8, 2):
            a, b, d = row_of(cols[k], k), row_of(cols[k + 1], k), row_of(cols[k + 1], k + 1)
            det = a * d - b * b
            inverse = 1.0 / det
            single = 1.0 / a

            def solve(u, v):
                return (d * u - b * v) * inverse, (a * v - b * u) * inverse

            pairs = [solve(row_of(cols[j], k), row_of(cols[j], k + 1)) for j in range(k + 2, 8)]
            upper = row_of(own, k)
            top = solve(upper, row_of(own, k + 1))
            heads.append(pairs)
            tops.append(top)
            c0 = jnp.where(sub > k + 1, cols[k], 0.0)
            c1 = jnp.where(sub > k + 1, cols[k + 1], 0.0)
            for j in range(k + 2, 8):
                h0, h1 = pairs[j - k - 2]
                cols[j] = cols[j] - (c0 * h0 + c1 * h1)
            own = own - (c0 * top[0] + c1 * top[1])
            own = own - jnp.where(sub == k + 1, b * single, 0.0) * upper
            scale = jnp.where(sub == k, lax.rsqrt(a), scale)
            scale = jnp.where(sub == k + 1, lax.rsqrt(det * single), scale)
        for q in range(p + 1, count):
            other = columns(q)
            value = jnp.where(inside, 0.0, rows[q])
            for k in range(0, 8, 2):
                for j in range(k + 2, 8):
                    h0, h1 = heads[k // 2][j - k - 2]
                    other[j] = other[j] - (other[k] * h0 + other[k + 1] * h1)
                top = tops[k // 2]
                value = value - (other[k] * top[0] + other[k + 1] * top[1])
            rows[q] = value
        rows[p] = jnp.where(lane < base + 8, own * scale, 0.0)
    return rows


def mm(a, b):
    return jnp.dot(a, b, precision=highest, preferred_element_type=jnp.float32)


def mm_t(a, b):
    return lax.dot_general(
        a, b, (((1,), (1,)), ((), ())), precision=highest, preferred_element_type=jnp.float32
    )


def three_way(x):
    high = x.astype(jnp.bfloat16)
    rest = x - high.astype(jnp.float32)
    mid = rest.astype(jnp.bfloat16)
    return high, mid, (rest - mid.astype(jnp.float32)).astype(jnp.bfloat16)


def pack_left(x):
    high, mid, low = three_way(x)
    return jnp.concatenate([high, high, mid, high, low, mid], axis=0)


def pack_right(x):
    high, mid, low = three_way(x)
    return jnp.concatenate([high, mid, high, low, high, mid], axis=0)


def outer_sum(left, right):
    return lax.dot_general(
        left, right, (((0,), (0,)), ((), ())), preferred_element_type=jnp.float32
    )


def spans(start, stop, step):
    return [slice(at, min(at + step, stop)) for at in range(start, stop, step)]


def factor(work_ref, inv_ref, upper_ref, root_ref):
    total, width = work_ref.shape
    blocks = width // block
    chunk = 4 * block
    eye = lax.broadcasted_iota(jnp.int32, (block, block), 0) == lax.broadcasted_iota(
        jnp.int32, (block, block), 1
    )
    across, along = [], []
    for here in spans(0, width, block):
        diagonal = jnp.where(eye, work_ref[here, here], 0.0)
        across.append(lax.rsqrt(jnp.sum(diagonal, axis=0, keepdims=True)))
        down = jnp.sum(diagonal, axis=1, keepdims=True)
        along.append(lax.rsqrt(down))
        root_ref[here, :] = jnp.broadcast_to(down * along[-1], (block, block))
    across = jnp.concatenate(across, axis=1)
    for i, here in enumerate(spans(0, width, block)):
        work_ref[here, :] = work_ref[here, :] * along[i] * across
    for here in spans(width, total, block):
        work_ref[here, :] = work_ref[here, :] * across

    def one(b, carry):
        off = pl.multiple_of(b * block, block)
        rows = [
            work_ref[pl.ds(pl.multiple_of(off + 8 * q, 8), 8), pl.ds(off, block)]
            for q in range(block // 8)
        ]
        rows = eliminate(rows)
        for half in range(2):

            @pl.when(b % 2 == half)
            def _():
                kept = slice(half * block, (half + 1) * block)
                for q in range(block // 8):
                    at = half * block + 8 * q
                    inv_ref[at : at + 8, kept] = rows[q]

        for s in range(blocks):

            @pl.when(b == s)
            def _():
                half = s % 2
                here = slice(s * block, (s + 1) * block)
                kept = slice(half * block, (half + 1) * block)
                inv = inv_ref[kept, kept]
                work_ref[here, here] = mm_t(work_ref[here, here], inv)
                if half == 0:
                    near = slice((s + 1) * block, (s + 2) * block)
                    across = mm_t(work_ref[near, here], inv)
                    work_ref[near, here] = across
                    work_ref[near, near] = work_ref[near, near] - mm_t(across, across)
                    return
                both = slice((s - 1) * block, (s + 1) * block)
                after = slice((s + 1) * block, width)
                old = slice(0, block)
                across = work_ref[here, (s - 1) * block : s * block]
                inv_ref[kept, old] = -mm(inv, mm(across, inv_ref[old, old]))
                inv = inv_ref[...]
                if s + 1 < blocks:
                    upper_ref[:, after] = mm(inv, work_ref[both, after])
                for these in spans((s + 1) * block, total, chunk):
                    solved = mm_t(work_ref[these, both], inv)
                    work_ref[these, both] = solved
                    if s + 1 < blocks:
                        work_ref[these, after] = work_ref[these, after] - mm(
                            solved, upper_ref[:, after]
                        )

        return carry

    inv_ref[:block, block:] = jnp.zeros((block, block), jnp.float32)
    lax.fori_loop(0, blocks, one, 0)


def factor_scratch(total, width):
    return [
        pltpu.VMEM((total, width), jnp.float32),
        pltpu.VMEM((2 * block, 2 * block), jnp.float32),
        pltpu.VMEM((2 * block, width), jnp.float32),
        pltpu.VMEM((width, block), jnp.float32),
    ]


def plain_kernel(rows_ref, out_ref, work_ref, inv_ref, upper_ref, root_ref):
    work_ref[...] = rows_ref[...]
    factor(work_ref, inv_ref, upper_ref, root_ref)
    width = work_ref.shape[1]
    out_ref[width:, :] = work_ref[width:, :]
    for here in spans(0, width, block):
        for there in spans(0, width, block):
            out_ref[here, there] = work_ref[here, there] * root_ref[here, :]


def plain_panel(rows):
    whole = pl.BlockSpec(memory_space=pltpu.VMEM)
    return pl.pallas_call(
        plain_kernel,
        out_shape=jax.ShapeDtypeStruct(rows.shape, jnp.float32),
        in_specs=[whole],
        out_specs=whole,
        scratch_shapes=factor_scratch(*rows.shape),
        compiler_params=pltpu.CompilerParams(vmem_limit_bytes=vmem_limit),
        name="plain_panel",
    )(rows)


def band_of(row, k):
    z, x = row // 2, row % 2
    step = k // 2
    near = (z // 2) * 2 + (z + step % 2) % 2
    return ((near + 2 * (step // 2)) % 4) * 2 + (x + k % 2) % 2


def panel_kernel(
    share,
    seqs,
    spot_ref,
    d0_ref,
    d1_ref,
    d2_ref,
    d3_ref,
    b0_ref,
    b1_ref,
    b2_ref,
    b3_ref,
    near_ref,
    far_ref,
    head_ref,
    query_ref,
    part_ref,
    next_ref,
    score_ref,
    own_ref,
    work_ref,
    inv_ref,
    upper_ref,
    root_ref,
    feat_ref,
):
    total, width = work_ref.shape
    low, band = b0_ref.shape
    cycles = low // block + 1
    row, col = spot_ref[0], spot_ref[1]
    y, core = col // 2, col % 2
    queries = query_ref.shape[0] // cycles
    top = width + low
    diag_refs, below_refs = (d0_ref, d1_ref, d2_ref, d3_ref), (b0_ref, b1_ref, b2_ref, b3_ref)
    for i, (diag_ref, below_ref) in enumerate(zip(diag_refs, below_refs)):
        there = ((y + i // 2) % 2) * 2 + (core + i % 2) % 2
        lanes = pl.ds(pl.multiple_of(there * band, 128), band)
        work_ref[width:top, lanes] = below_ref[...]
        for k in range(8):
            at = band_of(row, k) * block
            work_ref[pl.ds(pl.multiple_of(at, block), block), lanes] = diag_ref[
                k * block : (k + 1) * block, :
            ]
    half = queries // 2
    for k in range(8):
        lanes = pl.ds(pl.multiple_of(band_of(row, k) * block, block), block)
        rows = slice(k * half, (k + 1) * half)
        work_ref[top : top + half, lanes] = head_ref[rows, :block]
        work_ref[top + half : top + queries, lanes] = head_ref[rows, block:]
    for far, ref in enumerate((near_ref, far_ref)):
        side = (core + far) % 2
        for i in range(4):
            feat_ref[(i // 2) * 4 + 2 * side + i % 2] = ref[:, i * 128 : (i + 1) * 128]
    every = feat_ref.shape[1] // cycles
    first = [feat_ref[i, pl.ds(0, every, stride=cycles), :] for i in range(width // 128)]
    right = pack_right(jnp.concatenate(first, axis=1))
    for i, here in enumerate(spans(0, width, block)):
        work_ref[here, :] = work_ref[here, :] + outer_sum(pack_left(first[i]), right) * share
    for a in range(cycles):
        mine = feat_ref[row, pl.ds(a, every, stride=cycles), :]
        own_ref[a] = mine
        if a > 0:
            here = slice(width + (a - 1) * block, width + a * block)
            work_ref[here, :] = work_ref[here, :] + outer_sum(pack_left(mine), right) * share
    work_ref[top + queries :, :] = jnp.zeros((total - top - queries, width), jnp.float32)
    for i in range(width // 128):
        work_ref[top + queries : top + queries + seqs, i * 128 : (i + 1) * 128] = feat_ref[
            i, pl.ds(0, seqs, stride=cycles), :
        ]
    factor(work_ref, inv_ref, upper_ref, root_ref)
    lanes = pl.ds(pl.multiple_of(col * band, 128), band)
    rows = pl.ds(pl.multiple_of(row * block, block), block)
    mine = work_ref[rows, lanes] * jnp.concatenate([root_ref[rows, :]] * (band // block), axis=1)
    row_at = row * block + lax.broadcasted_iota(jnp.int32, mine.shape, 0)
    col_at = col * band + lax.broadcasted_iota(jnp.int32, mine.shape, 1)
    part_ref[:block, :] = jnp.where(col_at <= row_at, mine, 0.0)
    part_ref[block:, :] = work_ref[width:top, lanes]
    solved = work_ref[top : top + queries, :]
    product = mm_t(solved, work_ref[width:top, :])
    next_ref[pl.ds(0, queries, stride=cycles), :] = work_ref[
        top : top + queries, pl.ds(pl.multiple_of(row * block, block), block)
    ]
    for a in range(1, cycles):
        here = pl.ds(a, queries, stride=cycles)
        next_ref[here, :] = query_ref[here, :] - product[:, (a - 1) * block : a * block]
    score_ref[...] = mm_t(solved, work_ref[top + queries : top + queries + 8, :])[:, :seqs]


def panel(spot, diags, belows, near, far, heads, queries, seqs, share):
    low, band = belows[0].shape
    width = diags[0].shape[0]
    cycles = low // block + 1
    count = queries.shape[0] // cycles
    total = -(-(width + low + count + 8) // block) * block
    whole = pl.BlockSpec(memory_space=pltpu.VMEM)
    return pl.pallas_call(
        functools.partial(panel_kernel, share, seqs),
        out_shape=[
            jax.ShapeDtypeStruct((cycles * block, band), jnp.float32),
            jax.ShapeDtypeStruct(queries.shape, jnp.float32),
            jax.ShapeDtypeStruct((count, seqs), jnp.float32),
            jax.ShapeDtypeStruct((cycles, near.shape[0] // cycles, block), jnp.float32),
        ],
        in_specs=[pl.BlockSpec(memory_space=pltpu.SMEM)] + [whole] * 12,
        out_specs=[whole] * 4,
        scratch_shapes=factor_scratch(total, width)
        + [pltpu.VMEM((width // 128, near.shape[0], 128), jnp.float32)],
        compiler_params=pltpu.CompilerParams(vmem_limit_bytes=vmem_limit),
        name="panel_factor",
    )(spot, *diags, *belows, near, far, heads, queries)


def gram_kernel(share, gram_ref, own_ref, col_ref, panel_ref, out_ref, right_ref):
    steps, seqs, count = own_ref.shape
    cycles, lanes = col_ref.shape[0] // seqs, col_ref.shape[1]

    @pl.when(pl.program_id(1) == 0)
    def _():
        for b in range(cycles):
            side = pack_right(col_ref[pl.ds(b, seqs, stride=cycles), :])
            right_ref[:, b * lanes : (b + 1) * lanes] = side

    right = right_ref[...]
    for a in range(steps):
        base = a * count * cycles
        out_ref[pl.ds(base, count, stride=cycles), :] = panel_ref[a]
        update = outer_sum(pack_left(own_ref[a]), right) * share
        for b in range(1, cycles):
            here = pl.ds(base + b, count, stride=cycles)
            out_ref[here, :] = gram_ref[here, :] + update[:, b * lanes : (b + 1) * lanes]


def gram_update(gram_in, own, col, part, share):
    cycles, seqs, count = own.shape
    rows, width = col.shape
    lanes = 128
    steps = 2 if cycles % 2 == 0 else 1
    gram = gram_in.reshape(cycles * count * cycles, width)
    tall = pl.BlockSpec((steps * count * cycles, lanes), lambda v, a: (a, v))
    return pl.pallas_call(
        functools.partial(gram_kernel, share),
        out_shape=jax.ShapeDtypeStruct(gram.shape, jnp.float32),
        grid=(width // lanes, cycles // steps),
        in_specs=[
            tall,
            pl.BlockSpec((steps, seqs, count), lambda v, a: (a, 0, 0)),
            pl.BlockSpec((rows, lanes), lambda v, a: (0, v)),
            pl.BlockSpec((steps, count, lanes), lambda v, a: (a, 0, v)),
        ],
        out_specs=tall,
        scratch_shapes=[pltpu.VMEM((6 * seqs, cycles * lanes), jnp.bfloat16)],
        compiler_params=pltpu.CompilerParams(vmem_limit_bytes=vmem_limit),
        name="gram_update",
    )(gram, own, col, part.reshape(cycles, count, width)).reshape(gram_in.shape)


def sequence_features(proj_inner, proj_outer, lengths, loss_mask):
    seq_count, window = loss_mask.shape
    positions = jnp.arange(window, dtype=jnp.int32)
    token_live = (positions[None, :] >= (window - lengths)[:, None]).astype(
        jnp.float32
    ) * loss_mask.astype(jnp.float32)
    weighted = proj_inner.reshape(seq_count, window, -1) * token_live[:, :, None]
    features = jnp.einsum(
        "stk,stl->skl",
        weighted,
        proj_outer.reshape(seq_count, window, -1),
        precision=highest,
    )
    return features.reshape(seq_count, -1)


def general(
    tokens,
    cotangent,
    gate_weight,
    down_weight,
    proj_in,
    proj_out,
    lengths,
    loss_mask,
    gram_in,
    queries,
):
    row_index, col_index = lax.axis_index("rows"), lax.axis_index("cols")
    full_tokens = lax.all_gather(tokens, "cols", axis=1, tiled=True)
    full_cotangent = lax.all_gather(cotangent, "cols", axis=1, tiled=True)
    gate_pre = jnp.dot(
        full_tokens,
        lax.all_gather(gate_weight, "rows", axis=0, tiled=True),
        preferred_element_type=jnp.float32,
    )
    grad_hidden = jnp.dot(
        full_cotangent,
        lax.all_gather(down_weight, "rows", axis=0, tiled=True),
        preferred_element_type=jnp.float32,
    )
    grad_up = (grad_hidden * jax.nn.silu(gate_pre)).astype(jnp.bfloat16)
    outer_part = jnp.dot(grad_up, proj_out, preferred_element_type=jnp.float32)
    proj_inner = jnp.dot(full_tokens, proj_in, preferred_element_type=jnp.float32)
    proj_outer = lax.psum(outer_part, "cols")
    features = sequence_features(proj_inner, proj_outer, lengths, loss_mask)
    cycles, band_rows, _, band_cols = gram_in.shape
    every = lax.all_gather(features, "rows", axis=0, tiled=True)
    every = jnp.transpose(every.reshape(every.shape[0], cycles, -1), (1, 0, 2))
    own = lax.dynamic_slice_in_dim(every, row_index * band_rows, band_rows, 2)
    col = lax.dynamic_slice_in_dim(every, col_index * band_cols, band_cols, 2)
    panel_rows = lax.all_gather(gram_in[:, :, 0, :], "cols", axis=2, tiled=True)
    width = panel_rows.shape[2]
    diag = lax.all_gather(panel_rows[0], "rows", axis=0, tiled=True)
    heads = lax.all_gather(queries[:, 0, :], "rows", axis=1, tiled=True)
    below = panel_rows[1:].reshape((cycles - 1) * band_rows, width)
    share = 1.0 / every.shape[1]
    seqs, low, query_count = features.shape[0], below.shape[0], queries.shape[0]
    first = every[0]
    update = jnp.einsum("sr,sc->rc", first, first, precision=highest) * share
    more = jnp.einsum("asr,sc->arc", own[1:], first, precision=highest) * share
    used = width + low + query_count + seqs
    rows = [diag + update, below + more.reshape(low, width), heads, features[:, :width]]
    rows.append(jnp.zeros((-used % block, width), jnp.float32))
    done = plain_panel(jnp.concatenate(rows, axis=0))
    mine = lax.dynamic_slice_in_dim(done, row_index * band_rows, band_rows, 0)
    row_at = row_index * band_rows + lax.broadcasted_iota(jnp.int32, mine.shape, 0)
    mine = jnp.where(lax.broadcasted_iota(jnp.int32, mine.shape, 1) <= row_at, mine, 0.0)
    lower_part = done[width : width + low]
    solved = done[width + low : width + low + query_count]
    whitened = done[width + low + query_count : used]
    part = jnp.concatenate([mine, lower_part], axis=0)
    part = lax.dynamic_slice_in_dim(part, col_index * band_cols, band_cols, 1)
    updated = gram_in + jnp.einsum("asu,bsv->aubv", own, col, precision=highest) * share
    gram_next = updated.at[:, :, 0, :].set(part.reshape(cycles, band_rows, band_cols))
    tail = queries[:, 1:, :] - mm_t(solved, lower_part).reshape(query_count, cycles - 1, band_rows)
    own_head = lax.dynamic_slice_in_dim(solved, row_index * band_rows, band_rows, 1)
    query_next = jnp.concatenate([own_head[:, None, :], tail], axis=1)
    return gram_next, query_next, mm_t(solved, whitened)


sizes = {"z": 4, "x": 2, "y": 2, "core": 2}


def shift(value, axis, step, wrap=True, steps=None):
    names = ("z", "x", "y", "core")
    pairs = []
    for source in range(sizes["z"] * sizes["x"] * sizes["y"] * sizes["core"]):
        rest, at = source, []
        for name in reversed(names):
            at.append(rest % sizes[name])
            rest //= sizes[name]
        at = at[::-1]
        if axis == "both":
            pairs.append((source, source ^ 3))
            continue
        which = names.index(axis)
        there = at[which] + step
        if steps is not None:
            there = steps[at[which]]
        if wrap:
            there %= sizes[axis]
        elif not 0 <= there < sizes[axis]:
            continue
        at[which] = there
        target = 0
        for name, spot in zip(names, at):
            target = target * sizes[name] + spot
        pairs.append((source, target))
    return lax.ppermute(value, ("rows", "cols"), pairs)


slot_of = (((0, 3, 2, 1), (0, 2, 3, 1), (0, 1, 3, 2), (0, 1, 2, 3)))


def gradient_kernel(spot_ref, *refs):
    token_refs, refs = refs[:13], refs[13:]
    weight_refs, refs = refs[:8], refs[8:]
    out_proj_ref, in_proj_ref, outer_ref, inner_ref, weight_buf, weight_sem = refs
    z, x, y, core = (spot_ref[i] for i in range(4))
    height, band = token_refs[0].shape[1:]
    depth = weight_refs[0].shape[2]
    copies = []
    for i, ref in enumerate(weight_refs):
        row = ((z - i // 2) % 4) * 2 + (x + i % 2) % 2
        there = weight_buf.at[:, :, pl.ds(pl.multiple_of(row * depth, 128), depth)]
        copies.append(pltpu.make_async_copy(ref, there, weight_sem.at[i]))
    for copy in copies:
        copy.start()
    near, group = token_refs[:8], token_refs[8]
    far = [group.at[i] for i in range(4)] + list(token_refs[9:])
    sides = [far, near]
    starts = []
    for j in range(4):
        col = ((y + j // 2) % 2) * 2 + (core + j % 2) % 2
        starts.append(pl.multiple_of(col * band, 128))
    inner = jnp.zeros(inner_ref.shape, jnp.float32)
    for j in range(4):
        piece = sides[(j + 1) % 2][j // 2][0]
        inner = inner + jnp.dot(
            piece, in_proj_ref[pl.ds(starts[j], band), :], preferred_element_type=jnp.float32
        )
    inner_ref[...] = inner
    for copy in copies:
        copy.wait()

    def product(kind):
        result = None
        for j in range(4):
            rows = [sides[(j + 1) % 2][2 * s + j // 2][kind] for s in range(4)]
            term = lax.dot_general(
                jnp.concatenate(rows, axis=0),
                weight_buf[kind, :, pl.ds(starts[j], band)],
                (((1,), (1,)), ((), ())),
                preferred_element_type=jnp.float32,
            )
            result = term if result is None else result + term
        return result

    gate, hidden = product(0), product(1)
    grad = (hidden * (gate / (1.0 + jnp.exp(-gate)))).astype(jnp.bfloat16)
    outer = jnp.dot(grad, out_proj_ref[...], preferred_element_type=jnp.float32)
    for s in range(4):
        outer_ref[s] = outer[s * height : (s + 1) * height]


def gradient(spot, tokens, weights, out_proj, in_proj):
    kinds, height, band = tokens[0].shape
    share, depth = weights[0].shape[1:]
    full = depth * 8
    hbm = pl.BlockSpec(memory_space=pl.ANY)
    whole = pl.BlockSpec(memory_space=pltpu.VMEM)
    return pl.pallas_call(
        gradient_kernel,
        out_shape=[
            jax.ShapeDtypeStruct((4, height, out_proj.shape[1]), jnp.float32),
            jax.ShapeDtypeStruct((height, in_proj.shape[1]), jnp.float32),
        ],
        in_specs=[pl.BlockSpec(memory_space=pltpu.SMEM)] + [whole] * 13 + [hbm] * 8 + [whole] * 2,
        out_specs=[whole] * 2,
        scratch_shapes=[
            pltpu.VMEM((kinds, share, full), jnp.bfloat16),
            pltpu.SemaphoreType.DMA((8,)),
        ],
        compiler_params=pltpu.CompilerParams(vmem_limit_bytes=vmem_limit),
        cost_estimate=pl.CostEstimate(
            flops=16 * kinds * height * full * share,
            bytes_accessed=2 * kinds * full * (4 * height + share),
            transcendentals=4 * height * share,
        ),
        name="gradient",
    )(spot, *tokens, *weights, out_proj, in_proj)


def tie(values, *after):
    count = len(values)
    return lax.optimization_barrier((*values, *after))[:count]


def rounds(tokens, cotangent, gate_weight, down_weight, gram_in, queries, me, early):
    z = me["z"]
    both = jnp.stack([tokens, cotangent])
    depth, width = gate_weight.shape
    share = width // 4
    cut = jnp.stack(
        [gate_weight.T.reshape(4, share, depth), down_weight.T.reshape(4, share, depth)], axis=1
    )
    piece = [lax.dynamic_index_in_dim(cut, (z + s) % 4, 0, False) for s in range(4)]
    cycles, band_rows, _, band_cols = gram_in.shape
    count = queries.shape[0]
    below = gram_in[1:, :, 0, :].reshape((cycles - 1) * band_rows, band_cols)
    head = queries[:, 0, :]
    head = jnp.concatenate([head[: count // 2], head[count // 2 :]], axis=1)
    small = jnp.concatenate([gram_in[0, :, 0, :], head], axis=0)

    up1, down1 = shift(both, "z", 1, False), shift(both, "z", -1, False)
    y_own = shift(both, "y", 1)
    wx0 = shift(piece[0], "x", 1)
    wz1 = shift(piece[1], "z", 1)
    up1, down1, wz1, y_own, wx0, p3 = tie((up1, down1, wz1, y_own, wx0, piece[3]))

    slot_a = jnp.where(z < 2, down1, up1)
    up2, down2 = shift(up1, "z", 1, False), shift(down1, "z", -1, False)
    y_a = shift(slot_a, "y", 1)
    wx1 = shift(wz1, "x", 1)
    wz3 = shift(p3, "z", 3)
    up2, down2, wz3, y_a, wx1, p2 = tie((up2, down2, wz3, y_a, wx1, piece[2]))

    slot_b = jnp.where(z == 0, down2, jnp.where(z == 1, up1, jnp.where(z == 2, down1, up2)))
    last = shift(jnp.where(z == 2, up2, down2), "z", 1, False, (-1, 0, 3, -1))
    y_b = shift(slot_b, "y", 1)
    wx3 = shift(wz3, "x", 1)
    wz2 = shift(p2, "z", 2)
    below_y = shift(below, "y", 1)
    group = jnp.stack([both, y_own, slot_a, y_a])
    last, wz2, y_b, wx3, below_y, group, small, *early = tie(
        (last, wz2, y_b, wx3, below_y, group, small, *early)
    )

    slot_c = jnp.where(z == 0, last, jnp.where(z == 1, down2, jnp.where(z == 2, up2, last)))
    y_c = shift(slot_c, "y", 1)
    wx2 = shift(wz2, "x", 1)
    core_1 = shift(group, "core", 1)
    small = jnp.concatenate([small, shift(small, "z", 0, False, (1, 0, 3, 2))], axis=0)
    small = jnp.concatenate([small, shift(small, "z", 0, False, (2, 3, 0, 1))], axis=0)
    c_b = shift(slot_b, "core", 1)
    y_c, wx2, core_1, c_b, small = tie((y_c, wx2, core_1, c_b, small))

    cy_b = shift(y_b, "core", 1)
    c_c = shift(slot_c, "core", 1)
    cy_c = shift(y_c, "core", 1)
    cy_b, c_c, cy_c, small, below, below_y = tie((cy_b, c_c, cy_c, small, below, below_y))
    across = shift(small, "x", 1)
    below_c = shift(below, "core", 1)
    below_cy = shift(below_y, "core", 1)
    belows = [below, below_c, below_y, below_cy]
    pieces = [both, y_own, slot_a, y_a, slot_b, y_b, slot_c, y_c, core_1, c_b, cy_b, c_c, cy_c]
    weights = [piece[0], wx0, wz1, wx1, wz2, wx2, wz3, wx3]
    return pieces, weights, small, across, belows, early


def local(
    tokens,
    cotangent,
    gate_weight,
    down_weight,
    proj_in,
    proj_out,
    lengths,
    loss_mask,
    gram_in,
    queries,
):
    row_index, col_index = lax.axis_index("rows"), lax.axis_index("cols")
    me = {"z": row_index // 2, "x": row_index % 2, "y": col_index // 2, "core": col_index % 2}
    share = gate_weight.shape[1] // 4
    out_proj = lax.dynamic_slice_in_dim(proj_out, me["z"] * share, share, 0)
    spot = jnp.stack([me["z"], me["x"], me["y"], me["core"]]).astype(jnp.int32)
    where = jnp.stack([row_index, col_index]).astype(jnp.int32)
    table = jnp.array(slot_of, jnp.int32)
    early = [spot, where, out_proj] + [table[me["z"], s] for s in range(1, 4)]
    pieces, weights, small, across, belows, early = rounds(
        tokens, cotangent, gate_weight, down_weight, gram_in, queries, me, early
    )
    spot, where, out_proj, *order = early
    outer, proj_inner = gradient(spot, pieces, weights, out_proj, proj_in)
    tied = tie((outer, small, across, *belows))
    outer, small, across, belows = tied[0], tied[1], tied[2], tied[3:]
    band_rows, count = gram_in.shape[1], queries.shape[0]
    rows = band_rows + count // 2
    parts = [side[i * rows : (i + 1) * rows] for i in range(4) for side in (small, across)]
    diag = jnp.concatenate([part[:band_rows] for part in parts], axis=0)
    heads = jnp.concatenate([part[band_rows:] for part in parts], axis=0)
    proj_outer = outer[0]
    for s in range(1, 4):
        part = lax.dynamic_index_in_dim(outer, order[s - 1], 0, False)
        proj_outer = proj_outer + shift(part, "z", -s)
    over_y, over_core = shift(proj_outer, "y", 1), shift(proj_outer, "core", 1)
    proj_outer = (proj_outer + over_core) + (over_y + shift(proj_outer, "both", 1))
    diag, proj_outer = tie((diag, proj_outer))
    diag_y = shift(diag, "y", 1)
    features = sequence_features(proj_inner, proj_outer, lengths, loss_mask)
    cycles, band_rows, _, band_cols = gram_in.shape
    seqs = features.shape[0]
    features = features.reshape(seqs * cycles, -1)
    mine = [
        lax.dynamic_slice_in_dim(features, (2 * i + me["core"]) * band_cols, band_cols, 1)
        for i in range(2)
    ]
    mine = jnp.concatenate(mine, axis=1)
    pair = jnp.concatenate([mine, shift(mine, "x", 1)], axis=0)
    near = jnp.concatenate([pair] + [shift(pair, "z", s) for s in range(1, 4)], axis=0)
    diag, diag_y, near = tie((diag, diag_y, near))
    far = shift(near, "core", 1)
    diags = [diag, shift(diag, "core", 1), diag_y, shift(diag_y, "core", 1)]
    share = cycles / near.shape[0]
    part, query_next, scores, own = panel(
        where, diags, belows, near, far, heads, queries.reshape(-1, band_rows), seqs, share
    )
    col = lax.dynamic_slice_in_dim(near, me["y"] * band_cols, band_cols, 1)
    gram_next = gram_update(gram_in, own, col, part, share)
    return gram_next, query_next.reshape(queries.shape), scores


def solution(mesh):
    fits = mesh.shape["rows"] == 8 and mesh.shape["cols"] == 4
    return jax.shard_map(
        local if fits else general,
        mesh=mesh,
        in_specs=(
            P("rows", "cols"),
            P("rows", "cols"),
            P("rows", "cols"),
            P("rows", "cols"),
            P(),
            P("cols", None),
            P("rows"),
            P("rows", None),
            P(None, "rows", None, "cols"),
            P("cols", None, "rows"),
        ),
        out_specs=(P(None, "rows", None, "cols"), P("cols", None, "rows"), P("cols", "rows")),
        check_vma=False,
    )
```

```python
import functools
import jax
import jax.numpy as jnp
from jax import lax
from jax.experimental import pallas as pl
from jax.experimental.pallas import tpu as pltpu
from jax.sharding import PartitionSpec as P

highest = lax.Precision.HIGHEST
vmem_limit = 56 * 1024 * 1024
block = 128


def eliminate(rows):
    shape = (8, block)
    sub = lax.broadcasted_iota(jnp.int32, shape, 0)
    lane = lax.broadcasted_iota(jnp.int32, shape, 1)
    count = block // 8

    def row_of(x, k):
        return jnp.broadcast_to(x[k : k + 1, :], shape)

    for p in range(count):
        base = 8 * p
        inside = (lane >= base) & (lane < base + 8)

        def columns(q):
            return [jnp.broadcast_to(rows[q][:, base + k : base + k + 1], shape) for k in range(8)]

        cols = columns(p)
        own = jnp.where(inside, jnp.where(lane - base == sub, 1.0, 0.0), rows[p])
        heads, tops, scale = [], [], jnp.zeros(shape, jnp.float32)
        for k in range(0, 8, 2):
            a, b, d = row_of(cols[k], k), row_of(cols[k + 1], k), row_of(cols[k + 1], k + 1)
            det = a * d - b * b
            inverse = 1.0 / det
            single = 1.0 / a

            def solve(u, v):
                return (d * u - b * v) * inverse, (a * v - b * u) * inverse

            pairs = [solve(row_of(cols[j], k), row_of(cols[j], k + 1)) for j in range(k + 2, 8)]
            upper = row_of(own, k)
            top = solve(upper, row_of(own, k + 1))
            heads.append(pairs)
            tops.append(top)
            c0 = jnp.where(sub > k + 1, cols[k], 0.0)
            c1 = jnp.where(sub > k + 1, cols[k + 1], 0.0)
            for j in range(k + 2, 8):
                h0, h1 = pairs[j - k - 2]
                cols[j] = cols[j] - (c0 * h0 + c1 * h1)
            own = own - (c0 * top[0] + c1 * top[1])
            own = own - jnp.where(sub == k + 1, b * single, 0.0) * upper
            scale = jnp.where(sub == k, lax.rsqrt(a), scale)
            scale = jnp.where(sub == k + 1, lax.rsqrt(det * single), scale)
        for q in range(p + 1, count):
            other = columns(q)
            value = jnp.where(inside, 0.0, rows[q])
            for k in range(0, 8, 2):
                for j in range(k + 2, 8):
                    h0, h1 = heads[k // 2][j - k - 2]
                    other[j] = other[j] - (other[k] * h0 + other[k + 1] * h1)
                top = tops[k // 2]
                value = value - (other[k] * top[0] + other[k + 1] * top[1])
            rows[q] = value
        rows[p] = jnp.where(lane < base + 8, own * scale, 0.0)
    return rows


def mm(a, b):
    return jnp.dot(a, b, precision=highest, preferred_element_type=jnp.float32)


def mm_t(a, b):
    return lax.dot_general(
        a, b, (((1,), (1,)), ((), ())), precision=highest, preferred_element_type=jnp.float32
    )


def three_way(x):
    high = x.astype(jnp.bfloat16)
    rest = x - high.astype(jnp.float32)
    mid = rest.astype(jnp.bfloat16)
    return high, mid, (rest - mid.astype(jnp.float32)).astype(jnp.bfloat16)


def pack_left(x):
    high, mid, low = three_way(x)
    return jnp.concatenate([high, high, mid, high, low, mid], axis=0)


def pack_right(x):
    high, mid, low = three_way(x)
    return jnp.concatenate([high, mid, high, low, high, mid], axis=0)


def outer_sum(left, right):
    return lax.dot_general(
        left, right, (((0,), (0,)), ((), ())), preferred_element_type=jnp.float32
    )


def spans(start, stop, step):
    return [slice(at, min(at + step, stop)) for at in range(start, stop, step)]


def factor(work_ref, inv_ref, upper_ref, root_ref):
    total, width = work_ref.shape
    blocks = width // block
    chunk = 4 * block
    eye = lax.broadcasted_iota(jnp.int32, (block, block), 0) == lax.broadcasted_iota(
        jnp.int32, (block, block), 1
    )
    across, along = [], []
    for here in spans(0, width, block):
        diagonal = jnp.where(eye, work_ref[here, here], 0.0)
        across.append(lax.rsqrt(jnp.sum(diagonal, axis=0, keepdims=True)))
        down = jnp.sum(diagonal, axis=1, keepdims=True)
        along.append(lax.rsqrt(down))
        root_ref[here, :] = jnp.broadcast_to(down * along[-1], (block, block))
    across = jnp.concatenate(across, axis=1)
    for i, here in enumerate(spans(0, width, block)):
        work_ref[here, :] = work_ref[here, :] * along[i] * across
    for here in spans(width, total, block):
        work_ref[here, :] = work_ref[here, :] * across

    def one(b, carry):
        off = pl.multiple_of(b * block, block)
        rows = [
            work_ref[pl.ds(pl.multiple_of(off + 8 * q, 8), 8), pl.ds(off, block)]
            for q in range(block // 8)
        ]
        rows = eliminate(rows)
        for half in range(2):

            @pl.when(b % 2 == half)
            def _():
                kept = slice(half * block, (half + 1) * block)
                for q in range(block // 8):
                    at = half * block + 8 * q
                    inv_ref[at : at + 8, kept] = rows[q]

        for s in range(blocks):

            @pl.when(b == s)
            def _():
                half = s % 2
                here = slice(s * block, (s + 1) * block)
                kept = slice(half * block, (half + 1) * block)
                inv = inv_ref[kept, kept]
                work_ref[here, here] = mm_t(work_ref[here, here], inv)
                if half == 0:
                    near = slice((s + 1) * block, (s + 2) * block)
                    across = mm_t(work_ref[near, here], inv)
                    work_ref[near, here] = across
                    work_ref[near, near] = work_ref[near, near] - mm_t(across, across)
                    return
                both = slice((s - 1) * block, (s + 1) * block)
                after = slice((s + 1) * block, width)
                old = slice(0, block)
                across = work_ref[here, (s - 1) * block : s * block]
                inv_ref[kept, old] = -mm(inv, mm(across, inv_ref[old, old]))
                inv = inv_ref[...]
                if s + 1 < blocks:
                    upper_ref[:, after] = mm(inv, work_ref[both, after])
                for these in spans((s + 1) * block, total, chunk):
                    solved = mm_t(work_ref[these, both], inv)
                    work_ref[these, both] = solved
                    if s + 1 < blocks:
                        work_ref[these, after] = work_ref[these, after] - mm(
                            solved, upper_ref[:, after]
                        )

        return carry

    inv_ref[:block, block:] = jnp.zeros((block, block), jnp.float32)
    lax.fori_loop(0, blocks, one, 0)


def factor_scratch(total, width):
    return [
        pltpu.VMEM((total, width), jnp.float32),
        pltpu.VMEM((2 * block, 2 * block), jnp.float32),
        pltpu.VMEM((2 * block, width), jnp.float32),
        pltpu.VMEM((width, block), jnp.float32),
    ]


def plain_kernel(rows_ref, out_ref, work_ref, inv_ref, upper_ref, root_ref):
    work_ref[...] = rows_ref[...]
    factor(work_ref, inv_ref, upper_ref, root_ref)
    width = work_ref.shape[1]
    out_ref[width:, :] = work_ref[width:, :]
    for here in spans(0, width, block):
        for there in spans(0, width, block):
            out_ref[here, there] = work_ref[here, there] * root_ref[here, :]


def plain_panel(rows):
    whole = pl.BlockSpec(memory_space=pltpu.VMEM)
    return pl.pallas_call(
        plain_kernel,
        out_shape=jax.ShapeDtypeStruct(rows.shape, jnp.float32),
        in_specs=[whole],
        out_specs=whole,
        scratch_shapes=factor_scratch(*rows.shape),
        compiler_params=pltpu.CompilerParams(vmem_limit_bytes=vmem_limit),
        name="plain_panel",
    )(rows)


def band_of(row, k):
    z, x = row // 2, row % 2
    step = k // 2
    near = (z // 2) * 2 + (z + step % 2) % 2
    return ((near + 2 * (step // 2)) % 4) * 2 + (x + k % 2) % 2


def panel_kernel(
    share,
    seqs,
    spot_ref,
    d0_ref,
    d1_ref,
    d2_ref,
    d3_ref,
    b0_ref,
    b1_ref,
    b2_ref,
    b3_ref,
    near_ref,
    far_ref,
    head_ref,
    query_ref,
    part_ref,
    next_ref,
    score_ref,
    own_ref,
    work_ref,
    inv_ref,
    upper_ref,
    root_ref,
    feat_ref,
    load_sem,
):
    total, width = work_ref.shape
    low, band = b0_ref.shape
    cycles = low // block + 1
    row, col = spot_ref[0], spot_ref[1]
    y, core = col // 2, col % 2
    queries = query_ref.shape[0] // cycles
    top = width + low
    diag_refs, below_refs = (d0_ref, d1_ref, d2_ref, d3_ref), (b0_ref, b1_ref, b2_ref, b3_ref)
    loads = []
    for i, (diag_ref, below_ref) in enumerate(zip(diag_refs, below_refs)):
        there = ((y + i // 2) % 2) * 2 + (core + i % 2) % 2
        lanes = pl.ds(pl.multiple_of(there * band, 128), band)
        pairs = [(below_ref, work_ref.at[pl.ds(width, low), lanes])]
        for k in range(8):
            at = pl.multiple_of(band_of(row, k) * block, block)
            source = diag_ref.at[pl.ds(k * block, block), :]
            pairs.append((source, work_ref.at[pl.ds(at, block), lanes]))
        for source, target in pairs:
            loads.append(pltpu.make_async_copy(source, target, load_sem.at[len(loads)]))
    for copy in loads:
        copy.start()
    half = queries // 2
    for k in range(8):
        lanes = pl.ds(pl.multiple_of(band_of(row, k) * block, block), block)
        rows = slice(k * half, (k + 1) * half)
        work_ref[top : top + half, lanes] = head_ref[rows, :block]
        work_ref[top + half : top + queries, lanes] = head_ref[rows, block:]
    for far, ref in enumerate((near_ref, far_ref)):
        side = (core + far) % 2
        for i in range(4):
            feat_ref[(i // 2) * 4 + 2 * side + i % 2] = ref[:, i * 128 : (i + 1) * 128]
    every = feat_ref.shape[1] // cycles
    first = [feat_ref[i, pl.ds(0, every, stride=cycles), :] for i in range(width // 128)]
    right = pack_right(jnp.concatenate(first, axis=1))
    for copy in loads:
        copy.wait()
    for i, here in enumerate(spans(0, width, block)):
        work_ref[here, :] = work_ref[here, :] + outer_sum(pack_left(first[i]), right) * share
    for a in range(cycles):
        mine = feat_ref[row, pl.ds(a, every, stride=cycles), :]
        own_ref[a] = mine
        if a > 0:
            here = slice(width + (a - 1) * block, width + a * block)
            work_ref[here, :] = work_ref[here, :] + outer_sum(pack_left(mine), right) * share
    work_ref[top + queries :, :] = jnp.zeros((total - top - queries, width), jnp.float32)
    for i in range(width // 128):
        work_ref[top + queries : top + queries + seqs, i * 128 : (i + 1) * 128] = feat_ref[
            i, pl.ds(0, seqs, stride=cycles), :
        ]
    factor(work_ref, inv_ref, upper_ref, root_ref)
    lanes = pl.ds(pl.multiple_of(col * band, 128), band)
    rows = pl.ds(pl.multiple_of(row * block, block), block)
    mine = work_ref[rows, lanes] * jnp.concatenate([root_ref[rows, :]] * (band // block), axis=1)
    row_at = row * block + lax.broadcasted_iota(jnp.int32, mine.shape, 0)
    col_at = col * band + lax.broadcasted_iota(jnp.int32, mine.shape, 1)
    part_ref[:block, :] = jnp.where(col_at <= row_at, mine, 0.0)
    part_ref[block:, :] = work_ref[width:top, lanes]
    solved = work_ref[top : top + queries, :]
    product = mm_t(solved, work_ref[width:top, :])
    next_ref[pl.ds(0, queries, stride=cycles), :] = work_ref[
        top : top + queries, pl.ds(pl.multiple_of(row * block, block), block)
    ]
    for a in range(1, cycles):
        here = pl.ds(a, queries, stride=cycles)
        next_ref[here, :] = query_ref[here, :] - product[:, (a - 1) * block : a * block]
    score_ref[...] = mm_t(solved, work_ref[top + queries : top + queries + 8, :])[:, :seqs]


def panel(spot, diags, belows, near, far, heads, queries, seqs, share):
    low, band = belows[0].shape
    width = diags[0].shape[0]
    cycles = low // block + 1
    count = queries.shape[0] // cycles
    total = -(-(width + low + count + 8) // block) * block
    whole = pl.BlockSpec(memory_space=pltpu.VMEM)
    return pl.pallas_call(
        functools.partial(panel_kernel, share, seqs),
        out_shape=[
            jax.ShapeDtypeStruct((cycles * block, band), jnp.float32),
            jax.ShapeDtypeStruct(queries.shape, jnp.float32),
            jax.ShapeDtypeStruct((count, seqs), jnp.float32),
            jax.ShapeDtypeStruct((cycles, near.shape[0] // cycles, block), jnp.float32),
        ],
        in_specs=[pl.BlockSpec(memory_space=pltpu.SMEM)] + [pl.BlockSpec(memory_space=pl.ANY)] * 8
        + [whole] * 4,
        out_specs=[whole] * 4,
        scratch_shapes=factor_scratch(total, width)
        + [
            pltpu.VMEM((width // 128, near.shape[0], 128), jnp.float32),
            pltpu.SemaphoreType.DMA((36,)),
        ],
        compiler_params=pltpu.CompilerParams(vmem_limit_bytes=vmem_limit),
        name="panel_factor",
    )(spot, *diags, *belows, near, far, heads, queries)


def gram_kernel(share, gram_ref, own_ref, col_ref, panel_ref, out_ref, right_ref):
    steps, seqs, count = own_ref.shape
    cycles, lanes = col_ref.shape[0] // seqs, col_ref.shape[1]

    @pl.when(pl.program_id(1) == 0)
    def _():
        for b in range(cycles):
            side = pack_right(col_ref[pl.ds(b, seqs, stride=cycles), :])
            right_ref[:, b * lanes : (b + 1) * lanes] = side

    right = right_ref[...]
    for a in range(steps):
        base = a * count * cycles
        out_ref[pl.ds(base, count, stride=cycles), :] = panel_ref[a]
        update = outer_sum(pack_left(own_ref[a]), right) * share
        for b in range(1, cycles):
            here = pl.ds(base + b, count, stride=cycles)
            out_ref[here, :] = gram_ref[here, :] + update[:, b * lanes : (b + 1) * lanes]


def gram_update(gram_in, own, col, part, share):
    cycles, seqs, count = own.shape
    rows, width = col.shape
    lanes = 128
    steps = 2 if cycles % 2 == 0 else 1
    gram = gram_in.reshape(cycles * count * cycles, width)
    tall = pl.BlockSpec((steps * count * cycles, lanes), lambda v, a: (a, v))
    return pl.pallas_call(
        functools.partial(gram_kernel, share),
        out_shape=jax.ShapeDtypeStruct(gram.shape, jnp.float32),
        grid=(width // lanes, cycles // steps),
        in_specs=[
            tall,
            pl.BlockSpec((steps, seqs, count), lambda v, a: (a, 0, 0)),
            pl.BlockSpec((rows, lanes), lambda v, a: (0, v)),
            pl.BlockSpec((steps, count, lanes), lambda v, a: (a, 0, v)),
        ],
        out_specs=tall,
        scratch_shapes=[pltpu.VMEM((6 * seqs, cycles * lanes), jnp.bfloat16)],
        compiler_params=pltpu.CompilerParams(vmem_limit_bytes=vmem_limit),
        name="gram_update",
    )(gram, own, col, part.reshape(cycles, count, width)).reshape(gram_in.shape)


def sequence_features(proj_inner, proj_outer, lengths, loss_mask):
    seq_count, window = loss_mask.shape
    positions = jnp.arange(window, dtype=jnp.int32)
    token_live = (positions[None, :] >= (window - lengths)[:, None]).astype(
        jnp.float32
    ) * loss_mask.astype(jnp.float32)
    weighted = proj_inner.reshape(seq_count, window, -1) * token_live[:, :, None]
    features = jnp.einsum(
        "stk,stl->skl",
        weighted,
        proj_outer.reshape(seq_count, window, -1),
        precision=highest,
    )
    return features.reshape(seq_count, -1)


def general(
    tokens,
    cotangent,
    gate_weight,
    down_weight,
    proj_in,
    proj_out,
    lengths,
    loss_mask,
    gram_in,
    queries,
):
    row_index, col_index = lax.axis_index("rows"), lax.axis_index("cols")
    full_tokens = lax.all_gather(tokens, "cols", axis=1, tiled=True)
    full_cotangent = lax.all_gather(cotangent, "cols", axis=1, tiled=True)
    gate_pre = jnp.dot(
        full_tokens,
        lax.all_gather(gate_weight, "rows", axis=0, tiled=True),
        preferred_element_type=jnp.float32,
    )
    grad_hidden = jnp.dot(
        full_cotangent,
        lax.all_gather(down_weight, "rows", axis=0, tiled=True),
        preferred_element_type=jnp.float32,
    )
    grad_up = (grad_hidden * jax.nn.silu(gate_pre)).astype(jnp.bfloat16)
    outer_part = jnp.dot(grad_up, proj_out, preferred_element_type=jnp.float32)
    proj_inner = jnp.dot(full_tokens, proj_in, preferred_element_type=jnp.float32)
    proj_outer = lax.psum(outer_part, "cols")
    features = sequence_features(proj_inner, proj_outer, lengths, loss_mask)
    cycles, band_rows, _, band_cols = gram_in.shape
    every = lax.all_gather(features, "rows", axis=0, tiled=True)
    every = jnp.transpose(every.reshape(every.shape[0], cycles, -1), (1, 0, 2))
    own = lax.dynamic_slice_in_dim(every, row_index * band_rows, band_rows, 2)
    col = lax.dynamic_slice_in_dim(every, col_index * band_cols, band_cols, 2)
    panel_rows = lax.all_gather(gram_in[:, :, 0, :], "cols", axis=2, tiled=True)
    width = panel_rows.shape[2]
    diag = lax.all_gather(panel_rows[0], "rows", axis=0, tiled=True)
    heads = lax.all_gather(queries[:, 0, :], "rows", axis=1, tiled=True)
    below = panel_rows[1:].reshape((cycles - 1) * band_rows, width)
    share = 1.0 / every.shape[1]
    seqs, low, query_count = features.shape[0], below.shape[0], queries.shape[0]
    first = every[0]
    update = jnp.einsum("sr,sc->rc", first, first, precision=highest) * share
    more = jnp.einsum("asr,sc->arc", own[1:], first, precision=highest) * share
    used = width + low + query_count + seqs
    rows = [diag + update, below + more.reshape(low, width), heads, features[:, :width]]
    rows.append(jnp.zeros((-used % block, width), jnp.float32))
    done = plain_panel(jnp.concatenate(rows, axis=0))
    mine = lax.dynamic_slice_in_dim(done, row_index * band_rows, band_rows, 0)
    row_at = row_index * band_rows + lax.broadcasted_iota(jnp.int32, mine.shape, 0)
    mine = jnp.where(lax.broadcasted_iota(jnp.int32, mine.shape, 1) <= row_at, mine, 0.0)
    lower_part = done[width : width + low]
    solved = done[width + low : width + low + query_count]
    whitened = done[width + low + query_count : used]
    part = jnp.concatenate([mine, lower_part], axis=0)
    part = lax.dynamic_slice_in_dim(part, col_index * band_cols, band_cols, 1)
    updated = gram_in + jnp.einsum("asu,bsv->aubv", own, col, precision=highest) * share
    gram_next = updated.at[:, :, 0, :].set(part.reshape(cycles, band_rows, band_cols))
    tail = queries[:, 1:, :] - mm_t(solved, lower_part).reshape(query_count, cycles - 1, band_rows)
    own_head = lax.dynamic_slice_in_dim(solved, row_index * band_rows, band_rows, 1)
    query_next = jnp.concatenate([own_head[:, None, :], tail], axis=1)
    return gram_next, query_next, mm_t(solved, whitened)


sizes = {"z": 4, "x": 2, "y": 2, "core": 2}


def shift(value, axis, step, wrap=True, steps=None):
    names = ("z", "x", "y", "core")
    pairs = []
    for source in range(sizes["z"] * sizes["x"] * sizes["y"] * sizes["core"]):
        rest, at = source, []
        for name in reversed(names):
            at.append(rest % sizes[name])
            rest //= sizes[name]
        at = at[::-1]
        if axis == "both":
            pairs.append((source, source ^ 3))
            continue
        which = names.index(axis)
        there = at[which] + step
        if steps is not None:
            there = steps[at[which]]
        if wrap:
            there %= sizes[axis]
        elif not 0 <= there < sizes[axis]:
            continue
        at[which] = there
        target = 0
        for name, spot in zip(names, at):
            target = target * sizes[name] + spot
        pairs.append((source, target))
    return lax.ppermute(value, ("rows", "cols"), pairs)


slot_of = (((0, 3, 2, 1), (0, 2, 3, 1), (0, 1, 3, 2), (0, 1, 2, 3)))


def gradient_kernel(spot_ref, *refs):
    token_refs, refs = refs[:13], refs[13:]
    weight_refs, refs = refs[:8], refs[8:]
    out_proj_ref, in_proj_ref, outer_ref, inner_ref, weight_buf, weight_sem = refs
    z, x, y, core = (spot_ref[i] for i in range(4))
    height, band = token_refs[0].shape[1:]
    depth = weight_refs[0].shape[2]
    copies = []
    for i, ref in enumerate(weight_refs):
        row = ((z - i // 2) % 4) * 2 + (x + i % 2) % 2
        there = weight_buf.at[:, :, pl.ds(pl.multiple_of(row * depth, 128), depth)]
        copies.append(pltpu.make_async_copy(ref, there, weight_sem.at[i]))
    for copy in copies:
        copy.start()
    near, group = token_refs[:8], token_refs[8]
    far = [group.at[i] for i in range(4)] + list(token_refs[9:])
    sides = [far, near]
    starts = []
    for j in range(4):
        col = ((y + j // 2) % 2) * 2 + (core + j % 2) % 2
        starts.append(pl.multiple_of(col * band, 128))
    inner = jnp.zeros(inner_ref.shape, jnp.float32)
    for j in range(4):
        piece = sides[(j + 1) % 2][j // 2][0]
        inner = inner + jnp.dot(
            piece, in_proj_ref[pl.ds(starts[j], band), :], preferred_element_type=jnp.float32
        )
    inner_ref[...] = inner
    for copy in copies:
        copy.wait()

    def product(kind):
        result = None
        for j in range(4):
            rows = [sides[(j + 1) % 2][2 * s + j // 2][kind] for s in range(4)]
            term = lax.dot_general(
                jnp.concatenate(rows, axis=0),
                weight_buf[kind, :, pl.ds(starts[j], band)],
                (((1,), (1,)), ((), ())),
                preferred_element_type=jnp.float32,
            )
            result = term if result is None else result + term
        return result

    gate, hidden = product(0), product(1)
    grad = (hidden * (gate / (1.0 + jnp.exp(-gate)))).astype(jnp.bfloat16)
    outer = jnp.dot(grad, out_proj_ref[...], preferred_element_type=jnp.float32)
    for s in range(4):
        outer_ref[s] = outer[s * height : (s + 1) * height]


def gradient(spot, tokens, weights, out_proj, in_proj):
    kinds, height, band = tokens[0].shape
    share, depth = weights[0].shape[1:]
    full = depth * 8
    hbm = pl.BlockSpec(memory_space=pl.ANY)
    whole = pl.BlockSpec(memory_space=pltpu.VMEM)
    return pl.pallas_call(
        gradient_kernel,
        out_shape=[
            jax.ShapeDtypeStruct((4, height, out_proj.shape[1]), jnp.float32),
            jax.ShapeDtypeStruct((height, in_proj.shape[1]), jnp.float32),
        ],
        in_specs=[pl.BlockSpec(memory_space=pltpu.SMEM)] + [whole] * 13 + [hbm] * 8 + [whole] * 2,
        out_specs=[whole] * 2,
        scratch_shapes=[
            pltpu.VMEM((kinds, share, full), jnp.bfloat16),
            pltpu.SemaphoreType.DMA((8,)),
        ],
        compiler_params=pltpu.CompilerParams(vmem_limit_bytes=vmem_limit),
        cost_estimate=pl.CostEstimate(
            flops=16 * kinds * height * full * share,
            bytes_accessed=2 * kinds * full * (4 * height + share),
            transcendentals=4 * height * share,
        ),
        name="gradient",
    )(spot, *tokens, *weights, out_proj, in_proj)


def tie(values, *after):
    count = len(values)
    return lax.optimization_barrier((*values, *after))[:count]


def rounds(tokens, cotangent, gate_weight, down_weight, gram_in, queries, me, early):
    z = me["z"]
    both = jnp.stack([tokens, cotangent])
    depth, width = gate_weight.shape
    share = width // 4
    cut = jnp.stack(
        [gate_weight.T.reshape(4, share, depth), down_weight.T.reshape(4, share, depth)], axis=1
    )
    piece = [lax.dynamic_index_in_dim(cut, (z + s) % 4, 0, False) for s in range(4)]
    cycles, band_rows, _, band_cols = gram_in.shape
    count = queries.shape[0]
    below = gram_in[1:, :, 0, :].reshape((cycles - 1) * band_rows, band_cols)
    head = queries[:, 0, :]
    head = jnp.concatenate([head[: count // 2], head[count // 2 :]], axis=1)
    small = jnp.concatenate([gram_in[0, :, 0, :], head], axis=0)

    up1, down1 = shift(both, "z", 1, False), shift(both, "z", -1, False)
    y_own = shift(both, "y", 1)
    wx0 = shift(piece[0], "x", 1)
    wz1 = shift(piece[1], "z", 1)
    up1, down1, wz1, y_own, wx0, p3 = tie((up1, down1, wz1, y_own, wx0, piece[3]))

    slot_a = jnp.where(z < 2, down1, up1)
    up2, down2 = shift(up1, "z", 1, False), shift(down1, "z", -1, False)
    y_a = shift(slot_a, "y", 1)
    wx1 = shift(wz1, "x", 1)
    wz3 = shift(p3, "z", 3)
    up2, down2, wz3, y_a, wx1, p2 = tie((up2, down2, wz3, y_a, wx1, piece[2]))

    slot_b = jnp.where(z == 0, down2, jnp.where(z == 1, up1, jnp.where(z == 2, down1, up2)))
    last = shift(jnp.where(z == 2, up2, down2), "z", 1, False, (-1, 0, 3, -1))
    y_b = shift(slot_b, "y", 1)
    wx3 = shift(wz3, "x", 1)
    wz2 = shift(p2, "z", 2)
    below_y = shift(below, "y", 1)
    group = jnp.stack([both, y_own, slot_a, y_a])
    last, wz2, y_b, wx3, below_y, group, small, *early = tie(
        (last, wz2, y_b, wx3, below_y, group, small, *early)
    )

    slot_c = jnp.where(z == 0, last, jnp.where(z == 1, down2, jnp.where(z == 2, up2, last)))
    y_c = shift(slot_c, "y", 1)
    wx2 = shift(wz2, "x", 1)
    core_1 = shift(group, "core", 1)
    small = jnp.concatenate([small, shift(small, "z", 0, False, (1, 0, 3, 2))], axis=0)
    small = jnp.concatenate([small, shift(small, "z", 0, False, (2, 3, 0, 1))], axis=0)
    c_b = shift(slot_b, "core", 1)
    y_c, wx2, core_1, c_b, small = tie((y_c, wx2, core_1, c_b, small))

    cy_b = shift(y_b, "core", 1)
    c_c = shift(slot_c, "core", 1)
    cy_c = shift(y_c, "core", 1)
    cy_b, c_c, cy_c, small, below, below_y = tie((cy_b, c_c, cy_c, small, below, below_y))
    across = shift(small, "x", 1)
    below_c = shift(below, "core", 1)
    below_cy = shift(below_y, "core", 1)
    belows = [below, below_c, below_y, below_cy]
    pieces = [both, y_own, slot_a, y_a, slot_b, y_b, slot_c, y_c, core_1, c_b, cy_b, c_c, cy_c]
    weights = [piece[0], wx0, wz1, wx1, wz2, wx2, wz3, wx3]
    return pieces, weights, small, across, belows, early


def local(
    tokens,
    cotangent,
    gate_weight,
    down_weight,
    proj_in,
    proj_out,
    lengths,
    loss_mask,
    gram_in,
    queries,
):
    row_index, col_index = lax.axis_index("rows"), lax.axis_index("cols")
    me = {"z": row_index // 2, "x": row_index % 2, "y": col_index // 2, "core": col_index % 2}
    share = gate_weight.shape[1] // 4
    out_proj = lax.dynamic_slice_in_dim(proj_out, me["z"] * share, share, 0)
    spot = jnp.stack([me["z"], me["x"], me["y"], me["core"]]).astype(jnp.int32)
    where = jnp.stack([row_index, col_index]).astype(jnp.int32)
    table = jnp.array(slot_of, jnp.int32)
    early = [spot, where, out_proj] + [table[me["z"], s] for s in range(1, 4)]
    pieces, weights, small, across, belows, early = rounds(
        tokens, cotangent, gate_weight, down_weight, gram_in, queries, me, early
    )
    spot, where, out_proj, *order = early
    outer, proj_inner = gradient(spot, pieces, weights, out_proj, proj_in)
    tied = tie((outer, small, across, *belows))
    outer, small, across, belows = tied[0], tied[1], tied[2], tied[3:]
    band_rows, count = gram_in.shape[1], queries.shape[0]
    rows = band_rows + count // 2
    parts = [side[i * rows : (i + 1) * rows] for i in range(4) for side in (small, across)]
    diag = jnp.concatenate([part[:band_rows] for part in parts], axis=0)
    heads = jnp.concatenate([part[band_rows:] for part in parts], axis=0)
    proj_outer = outer[0]
    for s in range(1, 4):
        part = lax.dynamic_index_in_dim(outer, order[s - 1], 0, False)
        proj_outer = proj_outer + shift(part, "z", -s)
    over_y, over_core = shift(proj_outer, "y", 1), shift(proj_outer, "core", 1)
    proj_outer = (proj_outer + over_core) + (over_y + shift(proj_outer, "both", 1))
    diag, proj_outer = tie((diag, proj_outer))
    diag_y = shift(diag, "y", 1)
    features = sequence_features(proj_inner, proj_outer, lengths, loss_mask)
    cycles, band_rows, _, band_cols = gram_in.shape
    seqs = features.shape[0]
    features = features.reshape(seqs * cycles, -1)
    mine = [
        lax.dynamic_slice_in_dim(features, (2 * i + me["core"]) * band_cols, band_cols, 1)
        for i in range(2)
    ]
    mine = jnp.concatenate(mine, axis=1)
    pair = jnp.concatenate([mine, shift(mine, "x", 1)], axis=0)
    near = jnp.concatenate([pair] + [shift(pair, "z", s) for s in range(1, 4)], axis=0)
    diag, diag_y, near = tie((diag, diag_y, near))
    far = shift(near, "core", 1)
    diags = [diag, shift(diag, "core", 1), diag_y, shift(diag_y, "core", 1)]
    share = cycles / near.shape[0]
    part, query_next, scores, own = panel(
        where, diags, belows, near, far, heads, queries.reshape(-1, band_rows), seqs, share
    )
    col = lax.dynamic_slice_in_dim(near, me["y"] * band_cols, band_cols, 1)
    gram_next = gram_update(gram_in, own, col, part, share)
    return gram_next, query_next.reshape(queries.shape), scores


def solution(mesh):
    fits = mesh.shape["rows"] == 8 and mesh.shape["cols"] == 4
    return jax.shard_map(
        local if fits else general,
        mesh=mesh,
        in_specs=(
            P("rows", "cols"),
            P("rows", "cols"),
            P("rows", "cols"),
            P("rows", "cols"),
            P(),
            P("cols", None),
            P("rows"),
            P("rows", None),
            P(None, "rows", None, "cols"),
            P("cols", None, "rows"),
        ),
        out_specs=(P(None, "rows", None, "cols"), P("cols", None, "rows"), P("cols", "rows")),
        check_vma=False,
    )
```
